32 devices in a mesh: groups: 2 (over x), row: 16 (over z, y, core).
Axes of the slice: x: 2, y: 2, z: 4, core: 2. Of those that a mesh axis runs over, the one named last changes fastest.
Arguments:
- tiles: bfloat16 [1536, 256, 256], P(('groups', 'row')), parts along dimension 0, may hold values from -0.375 to 0.375
- tile_rows: int32 [1536], P(('groups', 'row')), parts along dimension 0, may hold values from 0 to 7
- tile_cols: int32 [1536], P(('groups', 'row')), parts along dimension 0, may hold values from 0 to 127, as said below
- counts: int32 [32], P(('groups', 'row')), parts along dimension 0, may hold values from 4 to 48, as said below
- positions: float32 [65536, 128], P(('groups', 'row')), parts along dimension 0, may hold values from -1 to 1
- momenta: float32 [65536, 128], P(('groups', 'row')), parts along dimension 0, may hold values from -0.5 to 0.5
Outputs:
- final_positions: float32 [65536, 128], P(('groups', 'row')), parts along dimension 0
- final_momenta: float32 [65536, 128], P(('groups', 'row')), parts along dimension 0
- energy: float32 [256], P('groups'), parts along dimension 0
The draws below stay inside these ranges and needn't reach their ends.
There are 2 independent parts, one for each index of `groups`. The reference program is written for one: setup_inputs(seed, part) draws one part's arguments, and reference() takes and returns one part's arrays. A program takes and returns all parts, laid end to end along the dimension named above; each array names one. Nothing has to cross between parts.
Inputs may be any that keep to these rules, and one draw needn't show every extreme that they name: `tile_cols`: among the first counts[d] slots of device d, at most 3 have column blocks held by one device (column block // 8); some device reaches 3. `counts`: some device has all 48 slots used.
All inputs are finite; a program needn't handle non-finite values.
Results may differ from the reference program's by a relative error of at most 0.0018.
Values may be sent and summed in bfloat16 or wider, within the bound.
No kernel may reach another device: no remote copies, remote signals or barrier semaphores. Data moves between devices by JAX's collectives and lax.ppermute only.
A program may use at most 64 MiB of HBM per device.

```python
import jax
import jax.numpy as jnp
from jax import lax

TILE = 256
REPL = 128
BLOCKS_DEV = 8
SLOTS = 48
STEPS = 4
ORDER = 32768
NBLK = 128
TILES = 768
N_ROW = 16


def draw_counts(key, part):
    key = jax.random.fold_in(key, 1)
    ranks = jax.random.permutation(key, N_ROW).astype(jnp.int32)
    least = max(1, SLOTS // 12)
    return (least + (SLOTS - least) * ranks * ranks // ((N_ROW - 1) * (N_ROW - 1))).astype(jnp.int32)


def draw_tile_cols(key, part):
    key = jax.random.fold_in(key, 2)
    first, second = jax.random.split(key)
    orders = jax.vmap(lambda k: jax.random.permutation(k, N_ROW))(jax.random.split(first, N_ROW))
    source = orders[:, jnp.arange(SLOTS) % N_ROW]
    offset = jax.random.randint(second, (N_ROW, SLOTS), 0, BLOCKS_DEV)
    return (source * BLOCKS_DEV + offset).reshape(-1).astype(jnp.int32)


def touch_ends(result, rng, low, top_value):
    longest = result.shape.index(max(result.shape))
    spots = []
    for shift in (0, 1):
        where = [jax.random.randint(jax.random.fold_in(rng, axis), (), 0, length) for axis, length in enumerate(result.shape)]
        where[longest] = (where[longest] + shift) % result.shape[longest]
        spots.append(tuple(where))
    return result.at[spots[0]].set(low).at[spots[1]].set(top_value)


def steps_of(own_key, extent, shards, low, high):
    factor_of = 1.0
    for axis_at, blocks in shards:
        heights = jax.random.uniform(jax.random.fold_in(jax.random.fold_in(own_key, 6), axis_at), (blocks,), jnp.float32, low / len(shards), high / len(shards))
        factor_of = factor_of * jnp.repeat(jnp.exp(heights), extent[axis_at] // blocks).reshape((-1,) + (1,) * (len(extent) - 1 - axis_at))
    return factor_of


def gaussian(stream_key, shape, spread, bound, pieces=(), kind=jnp.bfloat16):
    array = spread * jax.random.normal(stream_key, shape, jnp.float32)
    if pieces:
        array = array * steps_of(stream_key, shape, pieces, -0.22, 0.18)
    return jnp.clip(array, -bound, bound).astype(kind)


def setup_inputs(seed: int = 0, part: int = 0) -> dict:
    splits = jax.random.split(jax.random.key(seed), 7)
    own_keys = jax.random.split(jax.random.fold_in(splits[6], part), 7)
    tiles = gaussian(own_keys[0], (TILES, TILE, TILE), TILE ** -0.5, 0.375, ((0, 16),))
    tile_rows = touch_ends(jax.random.randint(own_keys[1], (TILES,), 0, BLOCKS_DEV), jax.random.fold_in(own_keys[1], 1), 0, BLOCKS_DEV - 1).astype(jnp.int32)
    tile_cols = draw_tile_cols(jax.random.fold_in(jax.random.fold_in(splits[6], part), 71), part)
    counts = draw_counts(jax.random.fold_in(jax.random.fold_in(splits[6], part), 71), part)
    positions = jnp.clip(jax.random.uniform(own_keys[4], (ORDER, REPL), jnp.float32, -1.0, 1.0) * steps_of(own_keys[4], (ORDER, REPL), ((0, 16),), -0.4, 0.0), -1.0, 1.0)
    momenta = jnp.clip(jax.random.uniform(own_keys[5], (ORDER, REPL), jnp.float32, -0.5, 0.5) * steps_of(own_keys[5], (ORDER, REPL), ((0, 16),), -0.4, 0.0), -0.5, 0.5)
    return dict(tiles=tiles, tile_rows=tile_rows, tile_cols=tile_cols, counts=counts, positions=positions, momenta=momenta)


def device_field(args, xb):
    tiles, rows, cols, count = args
    used = jnp.arange(SLOTS) < count
    xsel = xb[cols].astype(jnp.float32)
    prods = jnp.einsum('sij,sjr->sir', tiles.astype(jnp.float32), xsel)
    onehot = ((rows[None, :] == jnp.arange(BLOCKS_DEV)[:, None]) & used[None, :]).astype(jnp.float32)
    return jnp.einsum('bs,sir->bir', onehot, prods, precision=lax.Precision.HIGHEST)

def reference(tiles, tile_rows, tile_cols, counts, positions, momenta):
    grouped = (tiles.reshape(N_ROW, SLOTS, TILE, TILE), tile_rows.reshape(N_ROW, SLOTS), tile_cols.reshape(N_ROW, SLOTS), counts)
    used = (jnp.arange(SLOTS)[None, :] < counts[:, None]).reshape(-1)
    squares = lax.optimization_barrier(jnp.sum(tiles.astype(jnp.float32) ** 2, axis=(1, 2)))
    total = jnp.sum(jnp.where(used, squares, jnp.float32(0.0)))
    coeff = 0.7 * jnp.sqrt((ORDER - 1) / total)
    xpos = positions
    ymom = momenta
    energy = jnp.zeros((REPL,), jnp.float32)
    for step in range(STEPS):
        xb = xpos.astype(jnp.bfloat16).reshape(NBLK, TILE, REPL)
        field = lax.map(lambda g: device_field(g, xb), grouped).reshape(ORDER, REPL)
        if step == STEPS - 1:
            energy = -0.5 * lax.optimization_barrier(jnp.sum(xpos * field, axis=0))
        pump = 0.4 - 0.1 * step
        ymom = ymom + 0.5 * (-(xpos * xpos + pump) * xpos + coeff * field)
        xpos = xpos + 0.5 * ymom
    return (xpos, ymom, energy)
```

```python
import functools

import jax
import jax.numpy as jnp
from jax import lax
from jax.experimental import pallas as pl
from jax.experimental.pallas import tpu as pltpu
from jax.sharding import PartitionSpec as P

STEPS = 4


def step_kernel(last, rows, cols, count, coeff, pump, tiles, gathered, xpos, ymom, xout, yout, extra, tbuf, xbuf, field, tsem, xsem):
    tile = tbuf.shape[1]
    used = count[0]

    def tile_copy(s):
        return pltpu.make_async_copy(tiles.at[s], tbuf.at[s], tsem.at[s])

    def block_copy(s):
        return pltpu.make_async_copy(gathered.at[cols[s]], xbuf.at[s], xsem.at[s])

    @pl.loop(0, used)
    def _(s):
        tile_copy(s).start()
        block_copy(s).start()

    field[...] = jnp.zeros_like(field)

    @pl.loop(0, used)
    def _(s):
        tile_copy(s).wait()
        block_copy(s).wait()
        here = pl.ds(pl.multiple_of(rows[s] * tile, tile), tile)
        field[here, :] += jnp.dot(tbuf[s], xbuf[s], preferred_element_type=jnp.float32)

    x = xpos[...]
    h = field[...]
    if last:
        extra[...] = -0.5 * jnp.sum(x * h, axis=0, keepdims=True)
    y = ymom[...] + 0.5 * (-(x * x + pump[0]) * x + coeff[0] * h)
    x = x + 0.5 * y
    yout[...] = y
    xout[...] = x
    if not last:
        extra[...] = x.astype(jnp.bfloat16)


def run_step(last, rows, cols, count, coeff, pump, tiles, gathered, xpos, ymom):
    slots, tile, _ = tiles.shape
    order, repl = xpos.shape
    smem = pl.BlockSpec(memory_space=pltpu.SMEM)
    vmem = pl.BlockSpec(memory_space=pltpu.VMEM)
    hbm = pl.BlockSpec(memory_space=pl.ANY)
    if last:
        extra = jax.ShapeDtypeStruct((1, repl), jnp.float32)
    else:
        extra = jax.ShapeDtypeStruct((order, repl), jnp.bfloat16)
    return pl.pallas_call(
        functools.partial(step_kernel, last),
        out_shape=(
            jax.ShapeDtypeStruct(xpos.shape, jnp.float32),
            jax.ShapeDtypeStruct(ymom.shape, jnp.float32),
            extra,
        ),
        in_specs=[smem] * 5 + [hbm, hbm, vmem, vmem],
        out_specs=(vmem, vmem, vmem),
        scratch_shapes=[
            pltpu.VMEM((slots, tile, tile), jnp.bfloat16),
            pltpu.VMEM((slots, tile, repl), jnp.bfloat16),
            pltpu.VMEM((order, repl), jnp.float32),
            pltpu.SemaphoreType.DMA((slots,)),
            pltpu.SemaphoreType.DMA((slots,)),
        ],
        compiler_params=pltpu.CompilerParams(vmem_limit_bytes=40 * 2**20),
        cost_estimate=pl.CostEstimate(
            flops=2 * slots * tile * tile * repl, bytes_accessed=slots * tile * (tile + repl) * 2, transcendentals=0
        ),
    )(rows, cols, count, coeff, pump, tiles, gathered, xpos, ymom)


def row_sum(part):
    devices = lax.axis_size("row")
    spread = jnp.broadcast_to(part, (devices,) + part.shape[1:])
    return jnp.sum(lax.all_to_all(spread, "row", split_axis=0, concat_axis=0, tiled=True), axis=0)


def body(tiles, tile_rows, tile_cols, counts, positions, momenta):
    slots = tiles.shape[0]
    tile = tiles.shape[1]
    repl = positions.shape[1]
    blocks = positions.shape[0] // tile
    devices = lax.axis_size("row")
    order = blocks * tile * devices
    xpos = positions
    ymom = momenta
    extra = xpos.astype(jnp.bfloat16)
    coeff = None
    for step in range(STEPS):
        gathered = lax.all_gather(extra, "row", tiled=True).reshape(devices * blocks, tile, repl)
        if step == 0:
            squares = jnp.sum(jnp.square(tiles.astype(jnp.float32)), axis=(1, 2))
            local_sum = jnp.sum(jnp.where(jnp.arange(slots) < counts[0], squares, jnp.float32(0.0)))
            total = row_sum(jnp.broadcast_to(local_sum, (1, repl)))[:1]
            coeff = 0.7 * jnp.sqrt((order - 1) / total)
        pump = jnp.full((1,), 0.4 - 0.1 * step, jnp.float32)
        xpos, ymom, extra = run_step(
            step == STEPS - 1, tile_rows, tile_cols, counts, coeff, pump, tiles, gathered, xpos, ymom
        )
    energy = row_sum(extra)
    return (xpos, ymom, energy)


def solution(mesh):
    in_specs = (
        P(("groups", "row"), None, None),
        P(("groups", "row")),
        P(("groups", "row")),
        P(("groups", "row")),
        P(("groups", "row"), None),
        P(("groups", "row"), None),
    )
    out_specs = (P(("groups", "row"), None), P(("groups", "row"), None), P("groups"))
    return jax.shard_map(body, mesh=mesh, in_specs=in_specs, out_specs=out_specs, check_vma=False)
```

```python
import functools

import jax
import jax.numpy as jnp
from jax import lax
from jax.experimental import pallas as pl
from jax.experimental.pallas import tpu as pltpu
from jax.sharding import PartitionSpec as P

STEPS = 4


def step_kernel(last, nsrc, cap, rows, cols, count, table, coeff, pump, tiles, *refs):
    sources = refs[:nsrc]
    xpos, ymom, xout, yout, extra, tbuf, xbuf, field, tsem, xsem = refs[nsrc:]
    tile = tbuf.shape[1]
    used = count[0]

    def tile_copy(s):
        return pltpu.make_async_copy(tiles.at[s], tbuf.at[s], tsem.at[s])

    def block_copy(source, block, s):
        return pltpu.make_async_copy(source.at[block], xbuf.at[s], xsem.at[s])

    @pl.loop(0, used)
    def _(s):
        tile_copy(s).start()

    if nsrc == 1:
        @pl.loop(0, used)
        def _(s):
            block_copy(sources[0], cols[s], s).start()
    else:
        for i, source in enumerate(sources):
            for r in range(cap):
                s = table[i * cap + r]

                @pl.when(s >= 0)
                def _():
                    block_copy(source, lax.rem(cols[s], source.shape[0]), s).start()

    field[...] = jnp.zeros_like(field)

    @pl.loop(0, used)
    def _(s):
        tile_copy(s).wait()
        block_copy(sources[0], 0, s).wait()
        here = pl.ds(pl.multiple_of(rows[s] * tile, tile), tile)
        field[here, :] += jnp.dot(tbuf[s], xbuf[s], preferred_element_type=jnp.float32)

    x = xpos[...]
    h = field[...]
    if last:
        extra[...] = -0.5 * jnp.sum(x * h, axis=0, keepdims=True)
    y = ymom[...] + 0.5 * (-(x * x + pump[0]) * x + coeff[0] * h)
    x = x + 0.5 * y
    yout[...] = y
    xout[...] = x
    if not last:
        extra[...] = x.astype(jnp.bfloat16)


def run_step(last, cap, rows, cols, count, table, coeff, pump, tiles, sources, xpos, ymom):
    slots, tile, _ = tiles.shape
    order, repl = xpos.shape
    smem = pl.BlockSpec(memory_space=pltpu.SMEM)
    vmem = pl.BlockSpec(memory_space=pltpu.VMEM)
    hbm = pl.BlockSpec(memory_space=pl.ANY)
    if last:
        extra = jax.ShapeDtypeStruct((1, repl), jnp.float32)
    else:
        extra = jax.ShapeDtypeStruct((order, repl), jnp.bfloat16)
    return pl.pallas_call(
        functools.partial(step_kernel, last, len(sources), cap),
        out_shape=(
            jax.ShapeDtypeStruct(xpos.shape, jnp.float32),
            jax.ShapeDtypeStruct(ymom.shape, jnp.float32),
            extra,
        ),
        in_specs=[smem] * 6 + [hbm] * (1 + len(sources)) + [vmem, vmem],
        out_specs=(vmem, vmem, vmem),
        scratch_shapes=[
            pltpu.VMEM((slots, tile, tile), jnp.bfloat16),
            pltpu.VMEM((slots, tile, repl), jnp.bfloat16),
            pltpu.VMEM((order, repl), jnp.float32),
            pltpu.SemaphoreType.DMA((slots,)),
            pltpu.SemaphoreType.DMA((slots,)),
        ],
        compiler_params=pltpu.CompilerParams(vmem_limit_bytes=40 * 2**20),
        cost_estimate=pl.CostEstimate(
            flops=2 * slots * tile * tile * repl, bytes_accessed=slots * tile * (tile + repl) * 2, transcendentals=0
        ),
    )(rows, cols, count, table, coeff, pump, tiles, *sources, xpos, ymom)


def row_sum(part):
    devices = lax.axis_size("row")
    spread = jnp.broadcast_to(part, (devices,) + part.shape[1:])
    return jnp.sum(lax.all_to_all(spread, "row", split_axis=0, concat_axis=0, tiled=True), axis=0)


def spread_out(xb):
    me = lax.axis_index("row")
    z, yc = me // 4, me % 4

    def along_z(pairs, value):
        return lax.ppermute(value, "row", [(a * 4 + i, b * 4 + i) for a, b in pairs for i in range(4)])

    def to(flip, zs, value):
        return lax.ppermute(value, "row", [(a * 4 + i, a * 4 + (i ^ flip)) for a in zs for i in range(4)])

    everyone, inner, outer = (0, 1, 2, 3), (1, 2), (0, 3)
    is_inner = (z == 1) | (z == 2)
    near = along_z([(0, 1), (1, 0), (2, 3), (3, 2)], xb)
    skip = along_z([(0, 2), (2, 0), (1, 3), (3, 1)], xb)
    mid = along_z([(1, 2), (2, 1)], xb)
    far = along_z([(1, 0), (2, 3)], skip)
    yes = z >= 0
    column = [
        (xb, z, yes, everyone),
        (near, z ^ 1, yes, everyone),
        (skip, z ^ 2, yes, everyone),
        (mid, z ^ 3, is_inner, inner),
        (far, z ^ 3, ~is_inner, outer),
    ]
    found = []
    for value, zs, valid, who in column:
        across = to(2, who, value)
        for y, v in ((0, value), (2, across)):
            found.append((v, zs * 4 + (yc ^ y), valid))
            found.append((to(1, who, v), zs * 4 + (yc ^ y ^ 1), valid))
    return found


def body(tiles, tile_rows, tile_cols, counts, positions, momenta):
    slots = tiles.shape[0]
    tile = tiles.shape[1]
    repl = positions.shape[1]
    blocks = positions.shape[0] // tile
    devices = lax.axis_size("row")
    order = blocks * tile * devices
    cap = (slots + devices - 1) // devices
    slot_ids = jnp.arange(slots)
    used = slot_ids < counts[0]
    by_hand = devices == 16
    xpos = positions
    ymom = momenta
    extra = xpos.astype(jnp.bfloat16)
    coeff = None
    for step in range(STEPS):
        if by_hand:
            found = spread_out(extra)
            sources = [v.reshape(blocks, tile, repl) for v, _, _ in found]
        else:
            sources = [lax.all_gather(extra, "row", tiled=True).reshape(devices * blocks, tile, repl)]
        if step == 0:
            table = jnp.zeros((1,), jnp.int32)
            if by_hand:
                source = tile_cols // blocks
                same = (source[:, None] == source[None, :]) & used[None, :]
                rank = jnp.sum((same & (slot_ids[None, :] < slot_ids[:, None])).astype(jnp.int32), axis=1)
                owner = jnp.stack([jnp.where(valid, src, -1) for _, src, valid in found]).astype(jnp.int32)
                want = (
                    (source[None, None, :] == owner[:, None, None])
                    & (rank[None, None, :] == jnp.arange(cap)[None, :, None])
                    & used[None, None, :]
                )
                table = jnp.max(jnp.where(want, slot_ids[None, None, :], -1), axis=2).astype(jnp.int32).reshape(-1)
            squares = jnp.sum(jnp.square(tiles.astype(jnp.float32)), axis=(1, 2))
            local_sum = jnp.sum(jnp.where(used, squares, jnp.float32(0.0)))
            total = row_sum(jnp.broadcast_to(local_sum, (1, repl)))[:1]
            coeff = 0.7 * jnp.sqrt((order - 1) / total)
        pump = jnp.full((1,), 0.4 - 0.1 * step, jnp.float32)
        xpos, ymom, extra = run_step(
            step == STEPS - 1, cap, tile_rows, tile_cols, counts, table, coeff, pump, tiles, sources, xpos, ymom
        )
    energy = row_sum(extra)
    return (xpos, ymom, energy)


def solution(mesh):
    in_specs = (
        P(("groups", "row"), None, None),
        P(("groups", "row")),
        P(("groups", "row")),
        P(("groups", "row")),
        P(("groups", "row"), None),
        P(("groups", "row"), None),
    )
    out_specs = (P(("groups", "row"), None), P(("groups", "row"), None), P("groups"))
    return jax.shard_map(body, mesh=mesh, in_specs=in_specs, out_specs=out_specs, check_vma=False)
```

```python
import functools

import jax
import jax.numpy as jnp
from jax import lax
from jax.experimental import pallas as pl
from jax.experimental.pallas import tpu as pltpu
from jax.sharding import PartitionSpec as P

STEPS = 4


GROUP = 4


def step_kernel(last, nsrc, cap, rows, cols, count, table, coeff, pump, tiles, *refs):
    sources = refs[:nsrc]
    xpos, ymom, xout, yout, extra, xbuf, field, xsem = refs[nsrc:]
    slots, tile, _ = xbuf.shape
    used = count[0]

    def block_copy(source, block, s):
        return pltpu.make_async_copy(source.at[block], xbuf.at[s], xsem.at[s])

    if nsrc == 1:
        @pl.loop(0, used)
        def _(s):
            block_copy(sources[0], cols[s], s).start()
    else:
        for i, source in enumerate(sources):
            for r in range(cap):
                s = table[i * cap + r]

                @pl.when(s >= 0)
                def _():
                    block_copy(source, lax.rem(cols[s], source.shape[0]), s).start()

    field[...] = jnp.zeros_like(field)
    groups = (used + GROUP - 1) // GROUP

    @pl.loop(used, groups * GROUP)
    def _(s):
        xbuf[s] = jnp.zeros(xbuf.shape[1:], xbuf.dtype)

    @pl.loop(0, used)
    def _(s):
        block_copy(sources[0], 0, s).wait()

    @pl.loop(0, groups)
    def _(g):
        prods = [
            jnp.dot(tiles[g * GROUP + i], xbuf[g * GROUP + i], preferred_element_type=jnp.float32) for i in range(GROUP)
        ]
        for i in range(GROUP):
            here = pl.ds(pl.multiple_of(rows[g * GROUP + i] * tile, tile), tile)
            field[here, :] += prods[i]

    x = xpos[...]
    h = field[...]
    if last:
        extra[...] = -0.5 * jnp.sum(x * h, axis=0, keepdims=True)
    y = ymom[...] + 0.5 * (-(x * x + pump[0]) * x + coeff[0] * h)
    x = x + 0.5 * y
    yout[...] = y
    xout[...] = x
    if not last:
        extra[...] = x.astype(jnp.bfloat16)


def run_step(last, cap, rows, cols, count, table, coeff, pump, tiles, sources, xpos, ymom):
    slots, tile, _ = tiles.shape
    order, repl = xpos.shape
    smem = pl.BlockSpec(memory_space=pltpu.SMEM)
    vmem = pl.BlockSpec(memory_space=pltpu.VMEM)
    hbm = pl.BlockSpec(memory_space=pl.ANY)
    if last:
        extra = jax.ShapeDtypeStruct((1, repl), jnp.float32)
    else:
        extra = jax.ShapeDtypeStruct((order, repl), jnp.bfloat16)
    return pl.pallas_call(
        functools.partial(step_kernel, last, len(sources), cap),
        out_shape=(
            jax.ShapeDtypeStruct(xpos.shape, jnp.float32),
            jax.ShapeDtypeStruct(ymom.shape, jnp.float32),
            extra,
        ),
        in_specs=[smem] * 6 + [vmem] + [hbm] * len(sources) + [vmem, vmem],
        out_specs=(vmem, vmem, vmem),
        scratch_shapes=[
            pltpu.VMEM((slots, tile, repl), jnp.bfloat16),
            pltpu.VMEM((order, repl), jnp.float32),
            pltpu.SemaphoreType.DMA((slots,)),
        ],
        compiler_params=pltpu.CompilerParams(vmem_limit_bytes=24 * 2**20),
        cost_estimate=pl.CostEstimate(
            flops=2 * slots * tile * tile * repl, bytes_accessed=slots * tile * (tile + repl) * 2, transcendentals=0
        ),
    )(rows, cols, count, table, coeff, pump, tiles, *sources, xpos, ymom)


def row_sum(part):
    devices = lax.axis_size("row")
    spread = jnp.broadcast_to(part, (devices,) + part.shape[1:])
    return jnp.sum(lax.all_to_all(spread, "row", split_axis=0, concat_axis=0, tiled=True), axis=0)


def spread_out(xb):
    me = lax.axis_index("row")
    z, yc = me // 4, me % 4

    def along_z(pairs, value):
        return lax.ppermute(value, "row", [(a * 4 + i, b * 4 + i) for a, b in pairs for i in range(4)])

    def to(flip, value):
        return lax.ppermute(value, "row", [(a * 4 + i, a * 4 + (i ^ flip)) for a in range(4) for i in range(4)])

    near = along_z([(0, 1), (1, 0), (2, 3), (3, 2)], xb)
    skip = along_z([(0, 2), (2, 0), (1, 3), (3, 1)], xb)
    far = along_z([(0, 1), (1, 0), (2, 3), (3, 2)], skip)
    found = []
    for value, zs in ((xb, z), (near, z ^ 1), (skip, z ^ 2), (far, z ^ 3)):
        across = to(2, value)
        for y, v in ((0, value), (2, across)):
            found.append((v, zs * 4 + (yc ^ y)))
            found.append((to(1, v), zs * 4 + (yc ^ y ^ 1)))
    return found


def body(tiles, tile_rows, tile_cols, counts, positions, momenta):
    slots = tiles.shape[0]
    tile = tiles.shape[1]
    repl = positions.shape[1]
    blocks = positions.shape[0] // tile
    devices = lax.axis_size("row")
    order = blocks * tile * devices
    cap = (slots + devices - 1) // devices
    slot_ids = jnp.arange(slots)
    used = slot_ids < counts[0]
    by_hand = devices == 16
    xpos = positions
    ymom = momenta
    extra = xpos.astype(jnp.bfloat16)
    coeff = None
    for step in range(STEPS):
        if by_hand:
            found = spread_out(extra)
            sources = [v.reshape(blocks, tile, repl) for v, _ in found]
        else:
            sources = [lax.all_gather(extra, "row", tiled=True).reshape(devices * blocks, tile, repl)]
        if step == 0:
            table = jnp.zeros((1,), jnp.int32)
            if by_hand:
                source = tile_cols // blocks
                same = (source[:, None] == source[None, :]) & used[None, :]
                rank = jnp.sum((same & (slot_ids[None, :] < slot_ids[:, None])).astype(jnp.int32), axis=1)
                owner = jnp.stack([src for _, src in found]).astype(jnp.int32)
                want = (
                    (source[None, None, :] == owner[:, None, None])
                    & (rank[None, None, :] == jnp.arange(cap)[None, :, None])
                    & used[None, None, :]
                )
                table = jnp.max(jnp.where(want, slot_ids[None, None, :], -1), axis=2).astype(jnp.int32).reshape(-1)
            squares = jnp.sum(jnp.square(tiles.astype(jnp.float32)), axis=(1, 2))
            local_sum = jnp.sum(jnp.where(used, squares, jnp.float32(0.0)))
            total = row_sum(jnp.broadcast_to(local_sum, (1, repl)))[:1]
            coeff = 0.7 * jnp.sqrt((order - 1) / total)
        pump = jnp.full((1,), 0.4 - 0.1 * step, jnp.float32)
        xpos, ymom, extra = run_step(
            step == STEPS - 1, cap, tile_rows, tile_cols, counts, table, coeff, pump, tiles, sources, xpos, ymom
        )
    energy = row_sum(extra)
    return (xpos, ymom, energy)


def solution(mesh):
    in_specs = (
        P(("groups", "row"), None, None),
        P(("groups", "row")),
        P(("groups", "row")),
        P(("groups", "row")),
        P(("groups", "row"), None),
        P(("groups", "row"), None),
    )
    out_specs = (P(("groups", "row"), None), P(("groups", "row"), None), P("groups"))
    return jax.shard_map(body, mesh=mesh, in_specs=in_specs, out_specs=out_specs, check_vma=False)
```

```python
import functools

import jax
import jax.numpy as jnp
from jax import lax
from jax.experimental import pallas as pl
from jax.experimental.pallas import tpu as pltpu
from jax.sharding import PartitionSpec as P

STEPS = 4
GROUP = 6
LIMIT = 32 * 2**20

SMEM = pl.BlockSpec(memory_space=pltpu.SMEM)
VMEM = pl.BlockSpec(memory_space=pltpu.VMEM)
ANY = pl.BlockSpec(memory_space=pl.ANY)


def params():
    return pltpu.CompilerParams(vmem_limit_bytes=LIMIT)


def squares_kernel(count, tiles, out):
    tile = tiles.shape[1]

    def add(s, acc):
        t = tiles[s].astype(jnp.float32)
        return acc + jnp.sum((t * t).reshape(tile // 8, 8, tile), axis=0)

    acc = lax.fori_loop(0, count[0], add, jnp.zeros((8, tile), jnp.float32))
    acc = jnp.sum(acc, axis=0, keepdims=True)
    out[...] = sum(acc[:, i : i + 128] for i in range(0, tile, 128))


def squares(count, tiles):
    return pl.pallas_call(
        squares_kernel,
        out_shape=jax.ShapeDtypeStruct((1, 128), jnp.float32),
        in_specs=[SMEM, VMEM],
        out_specs=VMEM,
        compiler_params=params(),
        cost_estimate=pl.CostEstimate(flops=2 * tiles.size, bytes_accessed=2 * tiles.size, transcendentals=0),
    )(count, tiles)


def update(pump, coeff, h, x, y):
    y = y + 0.5 * (-(x * x + pump) * x + coeff * h)
    return x + 0.5 * y, y


class Layout:
    def __init__(self, cap):
        self.cap = cap
        self.inner = 0
        self.packs = 1
        self.entries = 1 + 4 * 3 * cap

    def pack(self, j, flip, r):
        return self.packs + (j * 3 + flip - 1) * self.cap + r

    def entry(self, j, flip, r):
        return self.entries + 3 * ((j * 4 + flip) * self.cap + r)


def pack_into(layout, table, j, shard, outs):
    for flip in (1, 2, 3):
        for r in range(layout.cap):
            outs[flip - 1][r] = shard[table[layout.pack(j, flip, r)]]


def pack_kernel(layout, j, nshards, table, *refs):
    shards, outs = refs[:nshards], refs[-3:]
    if len(shards) == 1:
        pack_into(layout, table, j, shards[0], outs)
        return

    @pl.when(table[layout.inner] == 1)
    def _():
        pack_into(layout, table, j, shards[0], outs)

    @pl.when(table[layout.inner] == 0)
    def _():
        pack_into(layout, table, j, shards[1], outs)


def pack(layout, j, table, shards, after):
    _, tile, repl = shards[0].shape
    out = jax.ShapeDtypeStruct((layout.cap, tile, repl), jnp.bfloat16)
    return pl.pallas_call(
        functools.partial(pack_kernel, layout, j, len(shards)),
        out_shape=(out,) * 3,
        in_specs=[SMEM] + [VMEM] * len(shards) + [ANY] * len(after),
        out_specs=(VMEM,) * 3,
        compiler_params=params(),
        cost_estimate=pl.CostEstimate(flops=0, bytes_accessed=12 * layout.cap * tile * repl, transcendentals=0),
    )(table, *shards, *after)


def take_blocks(layout, table, j, shards, packs, xbuf, first):
    cap = layout.cap

    def own(shard):
        for r in range(cap):
            xbuf[first + r] = shard[table[layout.entry(j, 0, r) + 2]]

    if len(shards) == 1:
        own(shards[0])
    else:
        pl.when(table[layout.inner] == 1)(lambda: own(shards[0]))
        pl.when(table[layout.inner] == 0)(lambda: own(shards[1]))
    for flip in (1, 2, 3):
        for r in range(cap):
            xbuf[first + flip * cap + r] = packs[flip - 1][r]


def early_kernel(layout, table, tiles, own0, own1, own2a, own2b, *refs):
    packs, (field, xbuf) = refs[:9], refs[9:]
    per = 4 * layout.cap
    for j, shards in enumerate(([own0], [own1], [own2a, own2b])):
        take_blocks(layout, table, j, shards, packs[3 * j : 3 * j + 3], xbuf, j * per)
    field[...] = jnp.zeros_like(field)

    @pl.loop(0, 3 * per // GROUP)
    def _(g):
        at = [g * GROUP + i for i in range(GROUP)]
        prods = [
            jnp.dot(tiles[table[layout.entries + 3 * e]], xbuf[e], preferred_element_type=jnp.float32) for e in at
        ]
        for e, prod in zip(at, prods):
            field[table[layout.entries + 3 * e + 1]] += prod


def early(layout, table, tiles, shards, packs):
    _, tile, _ = tiles.shape
    blocks, _, repl = shards[0].shape
    entries = 12 * layout.cap
    return pl.pallas_call(
        functools.partial(early_kernel, layout),
        out_shape=jax.ShapeDtypeStruct((blocks + 1, tile, repl), jnp.float32),
        in_specs=[SMEM] + [VMEM] * (1 + len(shards) + len(packs)),
        out_specs=VMEM,
        scratch_shapes=[pltpu.VMEM((entries, tile, repl), jnp.bfloat16)],
        compiler_params=params(),
        cost_estimate=pl.CostEstimate(
            flops=2 * entries * tile * tile * repl,
            bytes_accessed=entries * tile * (tile + repl) * 2,
            transcendentals=0,
        ),
    )(table, tiles, *shards, *packs)


def late_kernel(layout, last, table, scalars, tiles, own3a, own3b, pack1, pack2, pack3, field, xpos, ymom, *refs):
    if last:
        xout, yout, energy, xbuf, acc = refs
    else:
        xout, yout, xb, out1, out2, out3, xbuf, acc = refs
    blocks = xpos.shape[0]
    take_blocks(layout, table, 3, [own3a, own3b], [pack1, pack2, pack3], xbuf, 0)
    acc[...] = field[...]
    at = [layout.entry(3, flip, r) for flip in range(4) for r in range(layout.cap)]
    for first in range(0, len(at), GROUP):
        some = at[first : first + GROUP]
        prods = [
            jnp.dot(tiles[table[e]], xbuf[first + i], preferred_element_type=jnp.float32) for i, e in enumerate(some)
        ]
        for e, prod in zip(some, prods):
            acc[table[e + 1]] += prod
    total = jnp.zeros((1, xpos.shape[2]), jnp.float32)
    for b in range(blocks):
        x, h = xpos[b], acc[b]
        if last:
            total += jnp.sum(x * h, axis=0, keepdims=True)
        x, y = update(scalars[0], scalars[1], h, x, ymom[b])
        xout[b] = x
        yout[b] = y
        if not last:
            xb[b] = x.astype(jnp.bfloat16)
    if last:
        energy[...] = -0.5 * total
    else:
        pack_into(layout, table, 0, xb, (out1, out2, out3))


def late(layout, last, table, scalars, tiles, shards, packs, field, xpos, ymom):
    tile = tiles.shape[1]
    blocks, _, repl = xpos.shape
    entries = 4 * layout.cap
    state = jax.ShapeDtypeStruct(xpos.shape, jnp.float32)
    if last:
        extra = (jax.ShapeDtypeStruct((1, repl), jnp.float32),)
    else:
        out = jax.ShapeDtypeStruct((layout.cap, tile, repl), jnp.bfloat16)
        extra = (jax.ShapeDtypeStruct(xpos.shape, jnp.bfloat16), out, out, out)
    return pl.pallas_call(
        functools.partial(late_kernel, layout, last),
        out_shape=(state, state) + extra,
        in_specs=[SMEM, SMEM] + [VMEM] * (1 + len(shards) + len(packs) + 3),
        out_specs=(VMEM,) * (2 + len(extra)),
        scratch_shapes=[
            pltpu.VMEM((entries, tile, repl), jnp.bfloat16),
            pltpu.VMEM((blocks + 1, tile, repl), jnp.float32),
        ],
        compiler_params=params(),
        cost_estimate=pl.CostEstimate(
            flops=2 * entries * tile * tile * repl,
            bytes_accessed=entries * tile * (tile + repl) * 2 + 20 * xpos.size,
            transcendentals=0,
        ),
    )(table, scalars, tiles, *shards, *packs, field, xpos, ymom)


PAIRS = ((0, 1), (1, 0), (2, 3), (3, 2))
MIDDLE = ((1, 2), (2, 1))
OUTWARD = ((1, 0), (2, 3))


def along_z(pairs, value):
    return lax.ppermute(value, "row", [(a * 4 + i, b * 4 + i) for a, b in pairs for i in range(4)])


def across(flip, value):
    return lax.ppermute(value, "row", [(i, i ^ flip) for i in range(16)])


def send(packs):
    return [across(flip, packs[flip - 1]) for flip in (1, 2, 3)]


def row_sum_16(part):
    part = part + (across(1, part) + across(2, part) + across(3, part))
    return part + (across(4, part) + across(8, part) + across(12, part))


def make_table(layout, blocks, tile_rows, tile_cols, used):
    cap = layout.cap
    slots = tile_cols.shape[0]
    slot_ids = jnp.arange(slots)
    me = lax.axis_index("row")
    z, yc = me // 4, me % 4
    inner = (z == 1) | (z == 2)
    zs = jnp.stack([z, z ^ 1, jnp.where(inner, z ^ 3, z ^ 2), jnp.where(inner, z ^ 2, z ^ 3)])
    source = tile_cols // blocks
    local = tile_cols % blocks
    same = (source[:, None] == source[None, :]) & used[None, :]
    rank = jnp.sum((same & (slot_ids[None, :] < slot_ids[:, None])).astype(jnp.int32), axis=1)
    key = jnp.where(used, source * cap + rank, -1)
    match = key[None, :] == jnp.arange(16 * cap)[:, None]

    def pick(values, default):
        found = jnp.sum(jnp.where(match, values[None, :] - default, 0), axis=1) + default
        return found.reshape(16, cap).astype(jnp.int32)

    wants = pick(local, 0)
    asked = jnp.stack([across(flip, wants) for flip in (1, 2, 3)])
    mine = zs * 4 + yc
    packs = asked[:, mine].transpose(1, 0, 2)
    owner = zs[:, None] * 4 + (yc ^ jnp.arange(4))[None, :]
    entries = jnp.stack([pick(slot_ids, 0), pick(tile_rows, blocks), wants], axis=-1)[owner]
    return jnp.concatenate([inner.astype(jnp.int32)[None], packs.reshape(-1), entries.reshape(-1)])


def body_16(tiles, tile_rows, tile_cols, counts, positions, momenta):
    slots, tile, _ = tiles.shape
    repl = positions.shape[1]
    blocks = positions.shape[0] // tile
    cap = (slots + 15) // 16
    order = blocks * tile * 16
    layout = Layout(cap)
    used = jnp.arange(slots) < counts[0]
    xpos = positions.reshape(blocks, tile, repl)
    ymom = momenta.reshape(blocks, tile, repl)
    own0 = xpos.astype(jnp.bfloat16)
    table = make_table(layout, blocks, tile_rows, tile_cols, used)
    packs0 = pack(layout, 0, table, [own0], [])
    coeff = None
    for step in range(STEPS):
        last = step == STEPS - 1
        own1 = along_z(PAIRS, own0)
        own2a = along_z(MIDDLE, own0)
        got = [send(packs0)]
        (own1, own2a, got[0]) = lax.optimization_barrier((own1, own2a, got[0]))
        own3a = along_z(MIDDLE, own1)
        own2b = along_z(OUTWARD, own2a)
        got.append(send(pack(layout, 1, table, [own1], got[0])))
        (own3a, own2b, got[1]) = lax.optimization_barrier((own3a, own2b, got[1]))
        own3b = along_z(OUTWARD, own3a)
        got.append(send(pack(layout, 2, table, [own2a, own2b], got[1])))
        got.append(send(pack(layout, 3, table, [own3a, own3b], got[2])))
        field = early(layout, table, tiles, [own0, own1, own2a, own2b], got[0] + got[1] + got[2])
        if step == 0:
            total = jnp.sum(row_sum_16(squares(counts, tiles)))
            coeff = 0.7 * jnp.sqrt((order - 1) / total)
        scalars = jnp.stack([jnp.float32(0.4 - 0.1 * step), coeff])
        outs = late(layout, last, table, scalars, tiles, [own3a, own3b], got[3], field, xpos, ymom)
        xpos, ymom = outs[0], outs[1]
        if not last:
            own0, packs0 = outs[2], outs[3:]
    energy = row_sum_16(outs[2])
    return (xpos.reshape(positions.shape), ymom.reshape(momenta.shape), energy.reshape(repl))


def gathered_kernel(last, rows, cols, count, scalars, tiles, gathered, xpos, ymom, xout, yout, extra, xbuf, field, xsem):
    tile = xbuf.shape[1]
    used = count[0]

    def block_copy(s):
        return pltpu.make_async_copy(gathered.at[cols[s]], xbuf.at[s], xsem.at[s])

    @pl.loop(0, used)
    def _(s):
        block_copy(s).start()

    field[...] = jnp.zeros_like(field)

    @pl.loop(0, used)
    def _(s):
        block_copy(s).wait()
        here = pl.ds(pl.multiple_of(rows[s] * tile, tile), tile)
        field[here, :] += jnp.dot(tiles[s], xbuf[s], preferred_element_type=jnp.float32)

    x, h = xpos[...], field[...]
    if last:
        extra[...] = -0.5 * jnp.sum(x * h, axis=0, keepdims=True)
    x, y = update(scalars[0], scalars[1], h, x, ymom[...])
    xout[...] = x
    yout[...] = y
    if not last:
        extra[...] = x.astype(jnp.bfloat16)


def body_any(tiles, tile_rows, tile_cols, counts, positions, momenta):
    slots, tile, _ = tiles.shape
    order, repl = positions.shape
    devices = lax.axis_size("row")
    state = jax.ShapeDtypeStruct(positions.shape, jnp.float32)
    total = jnp.sum(lax.psum(squares(counts, tiles), "row"))
    coeff = 0.7 * jnp.sqrt((order * devices - 1) / total)
    xpos, ymom, extra = positions, momenta, positions.astype(jnp.bfloat16)
    for step in range(STEPS):
        last = step == STEPS - 1
        gathered = lax.all_gather(extra, "row", tiled=True).reshape(-1, tile, repl)
        scalars = jnp.stack([jnp.float32(0.4 - 0.1 * step), coeff])
        xpos, ymom, extra = pl.pallas_call(
            functools.partial(gathered_kernel, last),
            out_shape=(
                state,
                state,
                jax.ShapeDtypeStruct((1, repl), jnp.float32) if last else jax.ShapeDtypeStruct(state.shape, jnp.bfloat16),
            ),
            in_specs=[SMEM] * 4 + [VMEM, ANY, VMEM, VMEM],
            out_specs=(VMEM,) * 3,
            scratch_shapes=[
                pltpu.VMEM((slots, tile, repl), jnp.bfloat16),
                pltpu.VMEM(positions.shape, jnp.float32),
                pltpu.SemaphoreType.DMA((slots,)),
            ],
            compiler_params=params(),
        )(tile_rows, tile_cols, counts, scalars, tiles, gathered, xpos, ymom)
    return (xpos, ymom, lax.psum(extra, "row").reshape(repl))


def solution(mesh):
    in_specs = (
        P(("groups", "row"), None, None),
        P(("groups", "row")),
        P(("groups", "row")),
        P(("groups", "row")),
        P(("groups", "row"), None),
        P(("groups", "row"), None),
    )
    out_specs = (P(("groups", "row"), None), P(("groups", "row"), None), P("groups"))
    body = body_16 if mesh.shape["row"] == 16 else body_any
    return jax.shard_map(body, mesh=mesh, in_specs=in_specs, out_specs=out_specs, check_vma=False)
```

```python
import functools

import jax
import jax.numpy as jnp
from jax import lax
from jax.experimental import pallas as pl
from jax.experimental.pallas import tpu as pltpu
from jax.sharding import PartitionSpec as P

STEPS = 4
GROUP = 6
LIMIT = 16 * 2**20

SMEM = pl.BlockSpec(memory_space=pltpu.SMEM)
VMEM = pl.BlockSpec(memory_space=pltpu.VMEM)
ANY = pl.BlockSpec(memory_space=pl.ANY)


def params():
    return pltpu.CompilerParams(vmem_limit_bytes=LIMIT)


def squares_kernel(count, tiles, out):
    tile = tiles.shape[1]

    def add(s, acc):
        t = tiles[s].astype(jnp.float32)
        return acc + jnp.sum((t * t).reshape(tile // 8, 8, tile), axis=0)

    acc = lax.fori_loop(0, count[0], add, jnp.zeros((8, tile), jnp.float32))
    acc = jnp.sum(acc, axis=0, keepdims=True)
    out[...] = sum(acc[:, i : i + 128] for i in range(0, tile, 128))


def squares(count, tiles):
    return pl.pallas_call(
        squares_kernel,
        out_shape=jax.ShapeDtypeStruct((1, 128), jnp.float32),
        in_specs=[SMEM, VMEM],
        out_specs=VMEM,
        compiler_params=params(),
        cost_estimate=pl.CostEstimate(flops=2 * tiles.size, bytes_accessed=2 * tiles.size, transcendentals=0),
    )(count, tiles)


def update(pump, coeff, h, x, y):
    y = y + 0.5 * (-(x * x + pump) * x + coeff * h)
    return x + 0.5 * y, y


FIRST = ((0, 2), (3, 1), (1, 0), (2, 3))
SECOND = ((0, 1), (3, 2), (1, 3), (2, 0))
FROM_FIRST = (1, 3, 0, 2)
FROM_SECOND = (2, 0, 3, 1)


class Layout:
    def __init__(self, cap):
        self.cap = cap
        self.inner = 0
        self.packs = 1
        self.entries = 1 + 13 * cap

    def pack(self, j, flip):
        return self.packs + (j * 3 + flip - 1) * self.cap

    def pack_far(self, flip):
        return self.packs + (9 + flip) * self.cap

    def entry(self, i):
        return self.entries + 3 * i


EARLY = tuple((j, flip) for j in range(3) for flip in range(4))
LATE = tuple((3, flip) for flip in range(4))


def copy_blocks(table, at, cap, shard, out):
    for r in range(cap):
        out[r] = shard[table[at + r]]


def pack_shard_kernel(layout, table, shard, *refs):
    outs = refs[-3:]
    for flip in (1, 2, 3):
        copy_blocks(table, layout.pack(1, flip), layout.cap, shard, outs[flip - 1])


def pack_own_kernel(layout, table, shard, *refs):
    outs = refs[-3:]
    for flip in (1, 2, 3):
        copy_blocks(table, layout.pack(0, flip), layout.cap, shard, outs[flip - 1])


def pack_second_kernel(layout, table, first, second, *refs):
    here, far = refs[-7:-4], refs[-4:]
    for flip in (1, 2, 3):
        copy_blocks(table, layout.pack(2, flip), layout.cap, second, here[flip - 1])

    def send(shard):
        for flip in range(4):
            copy_blocks(table, layout.pack_far(flip), layout.cap, shard, far[flip])

    pl.when(table[layout.inner] == 1)(lambda: send(first))
    pl.when(table[layout.inner] == 0)(lambda: send(second))


def pack(kernel, layout, table, shards, sizes, after=()):
    _, tile, repl = shards[0].shape
    return pl.pallas_call(
        functools.partial(kernel, layout),
        out_shape=[jax.ShapeDtypeStruct((size, tile, repl), jnp.bfloat16) for size in sizes],
        in_specs=[SMEM] + [VMEM] * len(shards) + [ANY] * len(after),
        out_specs=[VMEM] * len(sizes),
        compiler_params=params(),
        cost_estimate=pl.CostEstimate(flops=0, bytes_accessed=0, transcendentals=0),
    )(table, *shards, *after)


def multiply(layout, table, tiles, xbuf, first, number, field):
    def some(start, place):
        prods = [
            jnp.dot(tiles[table[layout.entry(start + i)]], xbuf[place + i], preferred_element_type=jnp.float32)
            for i in range(GROUP)
        ]
        for i, prod in enumerate(prods):
            field[table[layout.entry(start + i) + 1]] += prod

    if number <= 3 * GROUP:
        for place in range(0, number, GROUP):
            some(first + place, place)
    else:

        @pl.loop(0, number // GROUP)
        def _(g):
            some(first + g * GROUP, g * GROUP)


def early_kernel(layout, table, tiles, *refs):
    sources, (field, xbuf) = refs[: len(EARLY)], refs[len(EARLY) :]
    cap = layout.cap
    for i, ((_, flip), source) in enumerate(zip(EARLY, sources)):
        for r in range(cap):
            e = i * cap + r
            xbuf[e] = source[table[layout.entry(e) + 2]] if flip == 0 else source[r]
    field[...] = jnp.zeros_like(field)
    multiply(layout, table, tiles, xbuf, 0, len(EARLY) * cap, field)


def cost(entries, tile, repl, more=0):
    return pl.CostEstimate(
        flops=2 * entries * tile * tile * repl,
        bytes_accessed=entries * tile * (tile + repl) * 2 + more,
        transcendentals=0,
    )


def early(layout, table, tiles, sources):
    tile = tiles.shape[1]
    blocks, _, repl = sources[0].shape
    entries = len(EARLY) * layout.cap
    return pl.pallas_call(
        functools.partial(early_kernel, layout),
        out_shape=jax.ShapeDtypeStruct((blocks + 1, tile, repl), jnp.float32),
        in_specs=[SMEM] + [VMEM] * (1 + len(sources)),
        out_specs=VMEM,
        scratch_shapes=[pltpu.VMEM((entries, tile, repl), jnp.bfloat16)],
        compiler_params=params(),
        cost_estimate=pl.CostEstimate(flops=0, bytes_accessed=0, transcendentals=0),
    )(table, tiles, *sources)


def late_kernel(layout, last, table, scalars, tiles, far0, far1, far2, far3, field, xpos, ymom, *refs):
    if last:
        xout, yout, energy, xbuf, acc = refs
    else:
        xout, yout, xb, out1, out2, out3, xbuf, acc = refs
    blocks = xpos.shape[0]
    cap = layout.cap
    for i, far in enumerate((far0, far1, far2, far3)):
        for r in range(cap):
            xbuf[i * cap + r] = far[r]
    acc[...] = field[...]
    multiply(layout, table, tiles, xbuf, len(EARLY) * cap, len(LATE) * cap, acc)
    total = jnp.zeros((1, xpos.shape[2]), jnp.float32)
    for b in range(blocks):
        x, h = xpos[b], acc[b]
        if last:
            total += jnp.sum(x * h, axis=0, keepdims=True)
        x, y = update(scalars[0], scalars[1], h, x, ymom[b])
        xout[b] = x
        yout[b] = y
        if not last:
            xb[b] = x.astype(jnp.bfloat16)
    if last:
        energy[...] = -0.5 * total
    else:
        for flip, out in ((1, out1), (2, out2), (3, out3)):
            copy_blocks(table, layout.pack(0, flip), cap, xb, out)


def late(layout, last, table, scalars, tiles, packs, field, xpos, ymom):
    tile = tiles.shape[1]
    blocks, _, repl = xpos.shape
    entries = len(LATE) * layout.cap
    state = jax.ShapeDtypeStruct(xpos.shape, jnp.float32)
    if last:
        extra = (jax.ShapeDtypeStruct((1, repl), jnp.float32),)
    else:
        out = jax.ShapeDtypeStruct((layout.cap, tile, repl), jnp.bfloat16)
        extra = (jax.ShapeDtypeStruct(xpos.shape, jnp.bfloat16), out, out, out)
    return pl.pallas_call(
        functools.partial(late_kernel, layout, last),
        out_shape=(state, state) + extra,
        in_specs=[SMEM, SMEM] + [VMEM] * (1 + len(packs) + 3),
        out_specs=(VMEM,) * (2 + len(extra)),
        scratch_shapes=[
            pltpu.VMEM((entries, tile, repl), jnp.bfloat16),
            pltpu.VMEM((blocks + 1, tile, repl), jnp.float32),
        ],
        compiler_params=params(),
        cost_estimate=cost(entries, tile, repl, 20 * xpos.size),
    )(table, scalars, tiles, *packs, field, xpos, ymom)


def along_z(pairs, value):
    return lax.ppermute(value, "row", [(a * 4 + i, b * 4 + i) for a, b in pairs for i in range(4)])


def across(flip, value):
    return lax.ppermute(value, "row", [(i, i ^ flip) for i in range(16)])


def row_sum(part):
    devices = lax.axis_size("row")
    spread = jnp.broadcast_to(part, (devices,) + part.shape[1:])
    return jnp.sum(lax.all_to_all(spread, "row", split_axis=0, concat_axis=0, tiled=True), axis=0, keepdims=True)


def make_table(layout, blocks, tile_rows, tile_cols, used):
    cap = layout.cap
    slots = tile_cols.shape[0]
    slot_ids = jnp.arange(slots)
    me = lax.axis_index("row")
    z, yc = me // 4, me % 4
    inner = (z == 1) | (z == 2)
    zs = jnp.stack([z, jnp.array(FROM_FIRST)[z], jnp.array(FROM_SECOND)[z], z ^ 3])
    source = tile_cols // blocks
    local = tile_cols % blocks
    same = (source[:, None] == source[None, :]) & used[None, :]
    rank = jnp.sum((same & (slot_ids[None, :] < slot_ids[:, None])).astype(jnp.int32), axis=1)
    key = jnp.where(used, source * cap + rank, -1)
    match = key[None, :] == jnp.arange(16 * cap)[:, None]

    def pick(values, default):
        found = jnp.sum(jnp.where(match, values[None, :] - default, 0), axis=1) + default
        return found.reshape(16, cap).astype(jnp.int32)

    wants = pick(local, 0)
    asked = jnp.stack([wants] + [across(flip, wants) for flip in (1, 2, 3)])
    asked_far = across(4, asked)
    packs = asked[1:, zs[:3] * 4 + yc].transpose(1, 0, 2)
    packs_far = asked_far[:, (z ^ 2) * 4 + yc]
    owner = jnp.stack([zs[j] * 4 + (yc ^ flip) for j, flip in EARLY + LATE])
    entries = jnp.stack([pick(slot_ids, 0), pick(tile_rows, blocks), wants], axis=-1)[owner]
    parts = (inner.astype(jnp.int32)[None], packs, packs_far, entries)
    return jnp.concatenate([part.reshape(-1) for part in parts])


def body_16(tiles, tile_rows, tile_cols, counts, positions, momenta):
    slots, tile, _ = tiles.shape
    repl = positions.shape[1]
    blocks = positions.shape[0] // tile
    cap = (slots + 15) // 16
    order = blocks * tile * 16
    layout = Layout(cap)
    used = jnp.arange(slots) < counts[0]
    xpos = positions.reshape(blocks, tile, repl)
    ymom = momenta.reshape(blocks, tile, repl)
    own0 = xpos.astype(jnp.bfloat16)
    table = make_table(layout, blocks, tile_rows, tile_cols, used)
    packs0 = None
    coeff = None
    for step in range(STEPS):
        last = step == STEPS - 1
        own1 = along_z(FIRST, own0)
        own2 = along_z(SECOND, own0)
        if step == 0:
            part = squares(counts, tiles)
            packs0 = pack(pack_own_kernel, layout, table, [own0], [cap] * 3, [part])
        got0 = [across(flip, packs0[flip - 1]) for flip in (1, 2, 3)]
        own1, got0 = lax.optimization_barrier((own1, got0))
        packs1 = pack(pack_shard_kernel, layout, table, [own1], [cap] * 3)
        got1 = [across(flip, packs1[flip - 1]) for flip in (1, 2, 3)]
        if step == 0:
            total = jnp.sum(row_sum(part))
            coeff = 0.7 * jnp.sqrt((order - 1) / total)
        own2, got1 = lax.optimization_barrier((own2, got1))
        packs2 = pack(pack_second_kernel, layout, table, [own1, own2], [cap] * 7)
        got2 = [across(flip, packs2[flip - 1]) for flip in (1, 2, 3)]
        far = [across(4 + flip, packs2[3 + flip]) for flip in range(4)]
        sources = [own0] + got0 + [own1] + got1 + [own2] + got2
        field = early(layout, table, tiles, sources)
        scalars = jnp.stack([jnp.float32(0.4 - 0.1 * step), coeff])
        outs = late(layout, last, table, scalars, tiles, far, field, xpos, ymom)
        xpos, ymom = outs[0], outs[1]
        if not last:
            own0, packs0 = outs[2], outs[3:]
    energy = row_sum(outs[2])
    return (xpos.reshape(positions.shape), ymom.reshape(momenta.shape), energy.reshape(repl))


def gathered_kernel(last, rows, cols, count, scalars, tiles, gathered, xpos, ymom, xout, yout, extra, xbuf, field, xsem):
    tile = xbuf.shape[1]
    used = count[0]

    def block_copy(s):
        return pltpu.make_async_copy(gathered.at[cols[s]], xbuf.at[s], xsem.at[s])

    @pl.loop(0, used)
    def _(s):
        block_copy(s).start()

    field[...] = jnp.zeros_like(field)

    @pl.loop(0, used)
    def _(s):
        block_copy(s).wait()
        here = pl.ds(pl.multiple_of(rows[s] * tile, tile), tile)
        field[here, :] += jnp.dot(tiles[s], xbuf[s], preferred_element_type=jnp.float32)

    x, h = xpos[...], field[...]
    if last:
        extra[...] = -0.5 * jnp.sum(x * h, axis=0, keepdims=True)
    x, y = update(scalars[0], scalars[1], h, x, ymom[...])
    xout[...] = x
    yout[...] = y
    if not last:
        extra[...] = x.astype(jnp.bfloat16)


def body_any(tiles, tile_rows, tile_cols, counts, positions, momenta):
    slots, tile, _ = tiles.shape
    order, repl = positions.shape
    devices = lax.axis_size("row")
    state = jax.ShapeDtypeStruct(positions.shape, jnp.float32)
    total = jnp.sum(lax.psum(squares(counts, tiles), "row"))
    coeff = 0.7 * jnp.sqrt((order * devices - 1) / total)
    xpos, ymom, extra = positions, momenta, positions.astype(jnp.bfloat16)
    for step in range(STEPS):
        last = step == STEPS - 1
        gathered = lax.all_gather(extra, "row", tiled=True).reshape(-1, tile, repl)
        scalars = jnp.stack([jnp.float32(0.4 - 0.1 * step), coeff])
        xpos, ymom, extra = pl.pallas_call(
            functools.partial(gathered_kernel, last),
            out_shape=(
                state,
                state,
                jax.ShapeDtypeStruct((1, repl), jnp.float32) if last else jax.ShapeDtypeStruct(state.shape, jnp.bfloat16),
            ),
            in_specs=[SMEM] * 4 + [VMEM, ANY, VMEM, VMEM],
            out_specs=(VMEM,) * 3,
            scratch_shapes=[
                pltpu.VMEM((slots, tile, repl), jnp.bfloat16),
                pltpu.VMEM(positions.shape, jnp.float32),
                pltpu.SemaphoreType.DMA((slots,)),
            ],
            compiler_params=params(),
        )(tile_rows, tile_cols, counts, scalars, tiles, gathered, xpos, ymom)
    return (xpos, ymom, lax.psum(extra, "row").reshape(repl))


def solution(mesh):
    in_specs = (
        P(("groups", "row"), None, None),
        P(("groups", "row")),
        P(("groups", "row")),
        P(("groups", "row")),
        P(("groups", "row"), None),
        P(("groups", "row"), None),
    )
    out_specs = (P(("groups", "row"), None), P(("groups", "row"), None), P("groups"))
    body = body_16 if mesh.shape["row"] == 16 else body_any
    return jax.shard_map(body, mesh=mesh, in_specs=in_specs, out_specs=out_specs, check_vma=False)
```

```python
import functools

import jax
import jax.numpy as jnp
from jax import lax
from jax.experimental import pallas as pl
from jax.experimental.pallas import tpu as pltpu
from jax.sharding import PartitionSpec as P

STEPS = 4
GROUP = 6
LIMIT = 16 * 2**20

SMEM = pl.BlockSpec(memory_space=pltpu.SMEM)
VMEM = pl.BlockSpec(memory_space=pltpu.VMEM)
ANY = pl.BlockSpec(memory_space=pl.ANY)


def params():
    return pltpu.CompilerParams(vmem_limit_bytes=LIMIT)


def squares_kernel(count, tiles, out):
    tile = tiles.shape[1]

    def add(s, acc):
        t = tiles[s].astype(jnp.float32)
        return acc + jnp.sum((t * t).reshape(tile // 8, 8, tile), axis=0)

    acc = lax.fori_loop(0, count[0], add, jnp.zeros((8, tile), jnp.float32))
    acc = jnp.sum(acc, axis=0, keepdims=True)
    out[...] = sum(acc[:, i : i + 128] for i in range(0, tile, 128))


def squares(count, tiles):
    return pl.pallas_call(
        squares_kernel,
        out_shape=jax.ShapeDtypeStruct((1, 128), jnp.float32),
        in_specs=[SMEM, VMEM],
        out_specs=VMEM,
        compiler_params=params(),
        cost_estimate=pl.CostEstimate(flops=2 * tiles.size, bytes_accessed=2 * tiles.size, transcendentals=0),
    )(count, tiles)


def update(pump, coeff, h, x, y):
    y = y + 0.5 * (-(x * x + pump) * x + coeff * h)
    return x + 0.5 * y, y


FIRST = ((0, 2), (3, 1), (1, 0), (2, 3))
SECOND = ((0, 1), (3, 2), (1, 3), (2, 0))


class Layout:
    def __init__(self, cap):
        self.cap = cap
        self.packs = 0
        self.entries = 9 * cap
        self.size = 9 * cap + 3 * 16 * cap

    def pack(self, j, flip):
        return self.packs + (j * 3 + flip - 1) * self.cap

    def entry(self, i):
        return self.entries + 3 * i


def whereabouts():
    me = lax.axis_index("row")
    z, yc = lax.div(me, 4), lax.rem(me, 4)
    inner = (z == 1) | (z == 2)
    near, skip = z ^ 1, z ^ 2
    return z, yc, inner, (z, jnp.where(inner, skip, near), jnp.where(inner, near, skip), z ^ 3)


EARLY = tuple((j, flip) for j in range(3) for flip in range(4))
LATE = tuple((3, flip) for flip in range(4))


def plan_kernel(layout, blocks, rows, cols, count, wants, mine, seen):
    cap = layout.cap
    keys = 16 * cap

    @pl.loop(0, 16)
    def _(d):
        seen[d] = 0

    @pl.loop(0, keys)
    def _(k):
        wants[k] = 0
        mine[k] = 0
        mine[keys + k] = blocks

    @pl.loop(0, count[0])
    def _(s):
        source = lax.div(cols[s], blocks)
        rank = seen[source]
        seen[source] = rank + 1
        key = source * cap + jnp.minimum(rank, cap - 1)
        wants[key] = lax.rem(cols[s], blocks)
        mine[key] = s
        mine[keys + key] = rows[s]


def plan(layout, blocks, rows, cols, count):
    keys = 16 * layout.cap
    return pl.pallas_call(
        functools.partial(plan_kernel, layout, blocks),
        out_shape=(jax.ShapeDtypeStruct((keys,), jnp.int32), jax.ShapeDtypeStruct((2 * keys,), jnp.int32)),
        in_specs=[SMEM] * 3,
        out_specs=(SMEM, SMEM),
        scratch_shapes=[pltpu.SMEM((16,), jnp.int32)],
        cost_estimate=pl.CostEstimate(flops=0, bytes_accessed=0, transcendentals=0),
    )(rows, cols, count)


def table_kernel(layout, wants, mine, near1, near2, near3, table):
    cap = layout.cap
    keys = 16 * cap
    _, yc, _, zs = whereabouts()
    for j in range(3):
        for flip, asked in ((1, near1), (2, near2), (3, near3)):
            for r in range(cap):
                table[layout.pack(j, flip) + r] = asked[(zs[j] * 4 + yc) * cap + r]
    for i, (j, flip) in enumerate(EARLY + LATE):
        for r in range(cap):
            key = (zs[j] * 4 + (yc ^ flip)) * cap + r
            at = layout.entry(i * cap + r)
            table[at] = mine[key]
            table[at + 1] = mine[keys + key]
            table[at + 2] = wants[key]


def make_table(layout, wants, mine, near):
    return pl.pallas_call(
        functools.partial(table_kernel, layout),
        out_shape=jax.ShapeDtypeStruct((layout.size,), jnp.int32),
        in_specs=[SMEM] * 5,
        out_specs=SMEM,
        cost_estimate=pl.CostEstimate(flops=0, bytes_accessed=0, transcendentals=0),
    )(wants, mine, *near)


def copy_blocks(table, at, cap, shard, out):
    for r in range(cap):
        out[r] = shard[table[at + r]]


def pack_shard_kernel(layout, j, table, shard, *refs):
    outs = refs[-3:]
    for flip in (1, 2, 3):
        copy_blocks(table, layout.pack(j, flip), layout.cap, shard, outs[flip - 1])


def pack_second_kernel(layout, table, asked, first, second, *refs):
    here, far = refs[-7:-4], refs[-4:]
    cap = layout.cap
    z, yc, inner, _ = whereabouts()
    for flip in (1, 2, 3):
        copy_blocks(table, layout.pack(2, flip), cap, second, here[flip - 1])

    def send(shard):
        for flip in range(4):
            copy_blocks(asked, (flip * 16 + (z ^ 2) * 4 + yc) * cap, cap, shard, far[flip])

    pl.when(inner)(lambda: send(first))
    pl.when(jnp.logical_not(inner))(lambda: send(second))


def pack(kernel, cap, number, tables, shards, after=()):
    _, tile, repl = shards[0].shape
    return pl.pallas_call(
        kernel,
        out_shape=[jax.ShapeDtypeStruct((cap, tile, repl), jnp.bfloat16)] * number,
        in_specs=[SMEM] * len(tables) + [VMEM] * len(shards) + [ANY] * len(after),
        out_specs=[VMEM] * number,
        compiler_params=params(),
        cost_estimate=pl.CostEstimate(flops=0, bytes_accessed=0, transcendentals=0),
    )(*tables, *shards, *after)


def multiply(layout, table, tiles, xbuf, first, number, field):
    def some(start, place):
        prods = [
            jnp.dot(tiles[table[layout.entry(start + i)]], xbuf[place + i], preferred_element_type=jnp.float32)
            for i in range(GROUP)
        ]
        for i, prod in enumerate(prods):
            field[table[layout.entry(start + i) + 1]] += prod

    if number <= 3 * GROUP:
        for place in range(0, number, GROUP):
            some(first + place, place)
    else:

        @pl.loop(0, number // GROUP)
        def _(g):
            some(first + g * GROUP, g * GROUP)


def early_kernel(layout, table, tiles, *refs):
    sources, (field, xbuf) = refs[: len(EARLY)], refs[len(EARLY) :]
    cap = layout.cap
    for i, ((_, flip), source) in enumerate(zip(EARLY, sources)):
        for r in range(cap):
            e = i * cap + r
            xbuf[e] = source[table[layout.entry(e) + 2]] if flip == 0 else source[r]
    field[...] = jnp.zeros_like(field)
    multiply(layout, table, tiles, xbuf, 0, len(EARLY) * cap, field)


def cost(entries, tile, repl, more=0):
    return pl.CostEstimate(
        flops=2 * entries * tile * tile * repl,
        bytes_accessed=entries * tile * (tile + repl) * 2 + more,
        transcendentals=0,
    )


def early(layout, table, tiles, sources):
    tile = tiles.shape[1]
    blocks, _, repl = sources[0].shape
    entries = len(EARLY) * layout.cap
    return pl.pallas_call(
        functools.partial(early_kernel, layout),
        out_shape=jax.ShapeDtypeStruct((blocks + 1, tile, repl), jnp.float32),
        in_specs=[SMEM] + [VMEM] * (1 + len(sources)),
        out_specs=VMEM,
        scratch_shapes=[pltpu.VMEM((entries, tile, repl), jnp.bfloat16)],
        compiler_params=params(),
        cost_estimate=pl.CostEstimate(flops=0, bytes_accessed=0, transcendentals=0),
    )(table, tiles, *sources)


def late_kernel(layout, last, table, scalars, tiles, far0, far1, far2, far3, field, xpos, ymom, *refs):
    if last:
        xout, yout, energy, xbuf, acc = refs
    else:
        xout, yout, xb, out1, out2, out3, xbuf, acc = refs
    blocks = xpos.shape[0]
    cap = layout.cap
    for i, far in enumerate((far0, far1, far2, far3)):
        for r in range(cap):
            xbuf[i * cap + r] = far[r]
    acc[...] = field[...]
    multiply(layout, table, tiles, xbuf, len(EARLY) * cap, len(LATE) * cap, acc)
    total = jnp.zeros((1, xpos.shape[2]), jnp.float32)
    for b in range(blocks):
        x, h = xpos[b], acc[b]
        if last:
            total += jnp.sum(x * h, axis=0, keepdims=True)
        x, y = update(scalars[0], scalars[1], h, x, ymom[b])
        xout[b] = x
        yout[b] = y
        if not last:
            xb[b] = x.astype(jnp.bfloat16)
    if last:
        energy[...] = -0.5 * total
    else:
        for flip, out in ((1, out1), (2, out2), (3, out3)):
            copy_blocks(table, layout.pack(0, flip), cap, xb, out)


def late(layout, last, table, scalars, tiles, packs, field, xpos, ymom):
    tile = tiles.shape[1]
    blocks, _, repl = xpos.shape
    entries = len(LATE) * layout.cap
    state = jax.ShapeDtypeStruct(xpos.shape, jnp.float32)
    if last:
        extra = (jax.ShapeDtypeStruct((1, repl), jnp.float32),)
    else:
        out = jax.ShapeDtypeStruct((layout.cap, tile, repl), jnp.bfloat16)
        extra = (jax.ShapeDtypeStruct(xpos.shape, jnp.bfloat16), out, out, out)
    return pl.pallas_call(
        functools.partial(late_kernel, layout, last),
        out_shape=(state, state) + extra,
        in_specs=[SMEM, SMEM] + [VMEM] * (1 + len(packs) + 3),
        out_specs=(VMEM,) * (2 + len(extra)),
        scratch_shapes=[
            pltpu.VMEM((entries, tile, repl), jnp.bfloat16),
            pltpu.VMEM((blocks + 1, tile, repl), jnp.float32),
        ],
        compiler_params=params(),
        cost_estimate=cost(entries, tile, repl, 20 * xpos.size),
    )(table, scalars, tiles, *packs, field, xpos, ymom)


def along_z(pairs, value):
    return lax.ppermute(value, "row", [(a * 4 + i, b * 4 + i) for a, b in pairs for i in range(4)])


def across(flip, value):
    return lax.ppermute(value, "row", [(i, i ^ flip) for i in range(16)])


def row_sum(part):
    devices = lax.axis_size("row")
    spread = jnp.broadcast_to(part, (devices,) + part.shape[1:])
    return jnp.sum(lax.all_to_all(spread, "row", split_axis=0, concat_axis=0, tiled=True), axis=0, keepdims=True)


def body_16(tiles, tile_rows, tile_cols, counts, positions, momenta):
    slots, tile, _ = tiles.shape
    repl = positions.shape[1]
    blocks = positions.shape[0] // tile
    cap = (slots + 15) // 16
    order = blocks * tile * 16
    layout = Layout(cap)
    pack_own = functools.partial(pack_shard_kernel, layout, 0)
    pack_first = functools.partial(pack_shard_kernel, layout, 1)
    pack_second = functools.partial(pack_second_kernel, layout)
    xpos = positions.reshape(blocks, tile, repl)
    ymom = momenta.reshape(blocks, tile, repl)
    own0 = xpos.astype(jnp.bfloat16)
    wants, mine = plan(layout, blocks, tile_rows, tile_cols, counts)
    near = [across(flip, wants) for flip in (1, 2, 3)]
    table = make_table(layout, wants, mine, near)
    packs0 = pack(pack_own, cap, 3, [table], [own0])
    asked = coeff = None
    for step in range(STEPS):
        last = step == STEPS - 1
        own1 = along_z(FIRST, own0)
        own2 = along_z(SECOND, own0)
        got0 = [across(flip, packs0[flip - 1]) for flip in (1, 2, 3)]
        after = []
        if step == 0:
            part = squares(counts, tiles)
            after = [part]
            near, got0 = lax.optimization_barrier((near, got0))
            asked = across(4, jnp.concatenate([wants] + near))
        own1, got0 = lax.optimization_barrier((own1, got0))
        packs1 = pack(pack_first, cap, 3, [table], [own1], after)
        got1 = [across(flip, packs1[flip - 1]) for flip in (1, 2, 3)]
        if step == 0:
            total = jnp.sum(lax.all_gather(part, "row"))
            coeff = 0.7 * jnp.sqrt((order - 1) / total)
        own2, got1 = lax.optimization_barrier((own2, got1))
        packs2 = pack(pack_second, cap, 7, [table, asked], [own1, own2])
        got2 = [across(flip, packs2[flip - 1]) for flip in (1, 2, 3)]
        far = [across(4 + flip, packs2[3 + flip]) for flip in range(4)]
        sources = [own0] + got0 + [own1] + got1 + [own2] + got2
        field = early(layout, table, tiles, sources)
        scalars = jnp.stack([jnp.float32(0.4 - 0.1 * step), coeff])
        outs = late(layout, last, table, scalars, tiles, far, field, xpos, ymom)
        xpos, ymom = outs[0], outs[1]
        if not last:
            own0, packs0 = outs[2], outs[3:]
    energy = row_sum(outs[2])
    return (xpos.reshape(positions.shape), ymom.reshape(momenta.shape), energy.reshape(repl))


def gathered_kernel(last, rows, cols, count, scalars, tiles, gathered, xpos, ymom, xout, yout, extra, xbuf, field, xsem):
    tile = xbuf.shape[1]
    used = count[0]

    def block_copy(s):
        return pltpu.make_async_copy(gathered.at[cols[s]], xbuf.at[s], xsem.at[s])

    @pl.loop(0, used)
    def _(s):
        block_copy(s).start()

    field[...] = jnp.zeros_like(field)

    @pl.loop(0, used)
    def _(s):
        block_copy(s).wait()
        here = pl.ds(pl.multiple_of(rows[s] * tile, tile), tile)
        field[here, :] += jnp.dot(tiles[s], xbuf[s], preferred_element_type=jnp.float32)

    x, h = xpos[...], field[...]
    if last:
        extra[...] = -0.5 * jnp.sum(x * h, axis=0, keepdims=True)
    x, y = update(scalars[0], scalars[1], h, x, ymom[...])
    xout[...] = x
    yout[...] = y
    if not last:
        extra[...] = x.astype(jnp.bfloat16)


def body_any(tiles, tile_rows, tile_cols, counts, positions, momenta):
    slots, tile, _ = tiles.shape
    order, repl = positions.shape
    devices = lax.axis_size("row")
    state = jax.ShapeDtypeStruct(positions.shape, jnp.float32)
    total = jnp.sum(lax.psum(squares(counts, tiles), "row"))
    coeff = 0.7 * jnp.sqrt((order * devices - 1) / total)
    xpos, ymom, extra = positions, momenta, positions.astype(jnp.bfloat16)
    for step in range(STEPS):
        last = step == STEPS - 1
        gathered = lax.all_gather(extra, "row", tiled=True).reshape(-1, tile, repl)
        scalars = jnp.stack([jnp.float32(0.4 - 0.1 * step), coeff])
        xpos, ymom, extra = pl.pallas_call(
            functools.partial(gathered_kernel, last),
            out_shape=(
                state,
                state,
                jax.ShapeDtypeStruct((1, repl), jnp.float32) if last else jax.ShapeDtypeStruct(state.shape, jnp.bfloat16),
            ),
            in_specs=[SMEM] * 4 + [VMEM, ANY, VMEM, VMEM],
            out_specs=(VMEM,) * 3,
            scratch_shapes=[
                pltpu.VMEM((slots, tile, repl), jnp.bfloat16),
                pltpu.VMEM(positions.shape, jnp.float32),
                pltpu.SemaphoreType.DMA((slots,)),
            ],
            compiler_params=params(),
        )(tile_rows, tile_cols, counts, scalars, tiles, gathered, xpos, ymom)
    return (xpos, ymom, lax.psum(extra, "row").reshape(repl))


def solution(mesh):
    in_specs = (
        P(("groups", "row"), None, None),
        P(("groups", "row")),
        P(("groups", "row")),
        P(("groups", "row")),
        P(("groups", "row"), None),
        P(("groups", "row"), None),
    )
    out_specs = (P(("groups", "row"), None), P(("groups", "row"), None), P("groups"))
    body = body_16 if mesh.shape["row"] == 16 else body_any
    return jax.shard_map(body, mesh=mesh, in_specs=in_specs, out_specs=out_specs, check_vma=False)
```

```python
import functools

import jax
import jax.numpy as jnp
from jax import lax
from jax.experimental import pallas as pl
from jax.experimental.pallas import tpu as pltpu
from jax.sharding import PartitionSpec as P

STEPS = 4
GROUP = 6
LANES = 128
SUM_AT = LANES - 1
LIMIT = 16 * 2**20

SMEM = pl.BlockSpec(memory_space=pltpu.SMEM)
VMEM = pl.BlockSpec(memory_space=pltpu.VMEM)
ANY = pl.BlockSpec(memory_space=pl.ANY)


def params(limit=LIMIT):
    return pltpu.CompilerParams(vmem_limit_bytes=limit)


def squares_kernel(count, tiles, out):
    tile = tiles.shape[1]

    def add(s, acc):
        t = tiles[s].astype(jnp.float32)
        return acc + jnp.sum((t * t).reshape(tile // 8, 8, tile), axis=0)

    acc = lax.fori_loop(0, count[0], add, jnp.zeros((8, tile), jnp.float32))
    acc = jnp.sum(acc, axis=0, keepdims=True)
    out[...] = sum(acc[:, i : i + 128] for i in range(0, tile, 128))


def squares(count, tiles):
    return pl.pallas_call(
        squares_kernel,
        out_shape=jax.ShapeDtypeStruct((1, 128), jnp.float32),
        in_specs=[SMEM, VMEM],
        out_specs=VMEM,
        compiler_params=params(),
        cost_estimate=pl.CostEstimate(flops=2 * tiles.size, bytes_accessed=2 * tiles.size, transcendentals=0),
    )(count, tiles)


def update(pump, coeff, h, x, y):
    y = y + 0.5 * (-(x * x + pump) * x + coeff * h)
    return x + 0.5 * y, y


FIRST = ((0, 2), (3, 1), (1, 0), (2, 3))
SECOND = ((0, 1), (3, 2), (1, 3), (2, 0))


class Layout:
    def __init__(self, cap):
        self.cap = cap
        self.packs = 0
        self.entries = 9 * cap
        self.size = 9 * cap + 3 * 16 * cap

    def pack(self, j, flip):
        return self.packs + (j * 3 + flip - 1) * self.cap

    def entry(self, i):
        return self.entries + 3 * i


def whereabouts():
    me = lax.axis_index("row")
    z, yc = lax.div(me, 4), lax.rem(me, 4)
    inner = (z == 1) | (z == 2)
    near, skip = z ^ 1, z ^ 2
    return z, yc, inner, (z, jnp.where(inner, skip, near), jnp.where(inner, near, skip), z ^ 3)


EARLY = tuple((j, flip) for j in range(3) for flip in range(4))
LATE = tuple((3, flip) for flip in range(4))


def plan_kernel(layout, blocks, rows, cols, count, tiles, mine, note, seen, buffer, sems):
    cap = layout.cap
    keys = 16 * cap
    slots, tile, _ = buffer.shape
    chunks = [pl.ds(first, GROUP) for first in range(0, slots, GROUP)]
    copies = [pltpu.make_async_copy(tiles.at[c], buffer.at[c], sems.at[i]) for i, c in enumerate(chunks)]
    for copy in copies:
        copy.start()

    @pl.loop(0, 16)
    def _(d):
        seen[d] = 0

    @pl.loop(0, keys)
    def _(k):
        mine[k] = 0
        mine[keys + k] = blocks
        mine[2 * keys + k] = 0

    @pl.loop(0, count[0])
    def _(s):
        source = lax.div(cols[s], blocks)
        rank = seen[source]
        seen[source] = rank + 1
        key = source * cap + jnp.minimum(rank, cap - 1)
        mine[key] = s
        mine[keys + key] = rows[s]
        mine[2 * keys + key] = lax.rem(cols[s], blocks)

    lane = lax.broadcasted_iota(jnp.int32, note.shape, 1)
    wants = jnp.zeros(note.shape, jnp.int32)
    for k in range(keys):
        wants = jnp.where(lane == k, mine[2 * keys + k], wants)

    def add(s, acc):
        t = buffer[s].astype(jnp.float32)
        return acc + jnp.sum((t * t).reshape(tile // 8, 8, tile), axis=0)

    acc = jnp.zeros((8, tile), jnp.float32)
    for i, copy in enumerate(copies):
        copy.wait()
        acc = lax.fori_loop(i * GROUP, jnp.clip(count[0], i * GROUP, (i + 1) * GROUP), add, acc)
    note[...] = jnp.where(lane == SUM_AT, jnp.sum(acc), wants.astype(jnp.float32))


def plan(layout, blocks, rows, cols, count, tiles):
    return pl.pallas_call(
        functools.partial(plan_kernel, layout, blocks),
        out_shape=(
            jax.ShapeDtypeStruct((3 * 16 * layout.cap,), jnp.int32),
            jax.ShapeDtypeStruct((1, LANES), jnp.float32),
        ),
        in_specs=[SMEM] * 3 + [ANY],
        out_specs=(SMEM, VMEM),
        scratch_shapes=[
            pltpu.SMEM((16,), jnp.int32),
            pltpu.VMEM(tiles.shape, tiles.dtype),
            pltpu.SemaphoreType.DMA((tiles.shape[0] // GROUP,)),
        ],
        compiler_params=params(59 * 2**20),
        cost_estimate=pl.CostEstimate(flops=0, bytes_accessed=0, transcendentals=0),
    )(rows, cols, count, tiles)


def table_kernel(layout, mine, asked, table):
    cap = layout.cap
    keys = 16 * cap
    _, yc, _, zs = whereabouts()
    for j in range(3):
        for flip in (1, 2, 3):
            for r in range(cap):
                table[layout.pack(j, flip) + r] = asked[flip * LANES + (zs[j] * 4 + yc) * cap + r]
    for i, (j, flip) in enumerate(EARLY + LATE):
        for r in range(cap):
            key = (zs[j] * 4 + (yc ^ flip)) * cap + r
            at = layout.entry(i * cap + r)
            table[at] = mine[key]
            table[at + 1] = mine[keys + key]
            table[at + 2] = mine[2 * keys + key]


def make_table(layout, mine, asked):
    return pl.pallas_call(
        functools.partial(table_kernel, layout),
        out_shape=jax.ShapeDtypeStruct((layout.size,), jnp.int32),
        in_specs=[SMEM] * 2,
        out_specs=SMEM,
        cost_estimate=pl.CostEstimate(flops=0, bytes_accessed=0, transcendentals=0),
    )(mine, asked)


def copy_blocks(table, at, cap, shard, out):
    for r in range(cap):
        out[r] = shard[table[at + r]]


def pack_shard_kernel(layout, j, table, shard, *refs):
    outs = refs[-3:]
    for flip in (1, 2, 3):
        copy_blocks(table, layout.pack(j, flip), layout.cap, shard, outs[flip - 1])


def pack_second_kernel(layout, table, asked, first, second, *refs):
    here, far = refs[-7:-4], refs[-4:]
    cap = layout.cap
    z, yc, inner, _ = whereabouts()
    for flip in (1, 2, 3):
        copy_blocks(table, layout.pack(2, flip), cap, second, here[flip - 1])

    def send(shard):
        for flip in range(4):
            copy_blocks(asked, flip * LANES + ((z ^ 2) * 4 + yc) * cap, cap, shard, far[flip])

    pl.when(inner)(lambda: send(first))
    pl.when(jnp.logical_not(inner))(lambda: send(second))


def pack(kernel, cap, number, tables, shards):
    _, tile, repl = shards[0].shape
    return pl.pallas_call(
        kernel,
        out_shape=[jax.ShapeDtypeStruct((cap, tile, repl), jnp.bfloat16)] * number,
        in_specs=[SMEM] * len(tables) + [VMEM] * len(shards),
        out_specs=[VMEM] * number,
        compiler_params=params(),
        cost_estimate=pl.CostEstimate(flops=0, bytes_accessed=0, transcendentals=0),
    )(*tables, *shards)


def multiply(layout, table, tiles, xbuf, first, number, field):
    def some(start, place):
        prods = [
            jnp.dot(tiles[table[layout.entry(start + i)]], xbuf[place + i], preferred_element_type=jnp.float32)
            for i in range(GROUP)
        ]
        for i, prod in enumerate(prods):
            field[table[layout.entry(start + i) + 1]] += prod

    if number <= 3 * GROUP:
        for place in range(0, number, GROUP):
            some(first + place, place)
    else:

        @pl.loop(0, number // GROUP)
        def _(g):
            some(first + g * GROUP, g * GROUP)


def early_kernel(layout, table, tiles, *refs):
    sources, (field, xbuf) = refs[: len(EARLY)], refs[len(EARLY) :]
    cap = layout.cap
    for i, ((_, flip), source) in enumerate(zip(EARLY, sources)):
        for r in range(cap):
            e = i * cap + r
            xbuf[e] = source[table[layout.entry(e) + 2]] if flip == 0 else source[r]
    field[...] = jnp.zeros_like(field)
    multiply(layout, table, tiles, xbuf, 0, len(EARLY) * cap, field)


def cost(entries, tile, repl, more=0):
    return pl.CostEstimate(
        flops=2 * entries * tile * tile * repl,
        bytes_accessed=entries * tile * (tile + repl) * 2 + more,
        transcendentals=0,
    )


def early(layout, table, tiles, sources):
    tile = tiles.shape[1]
    blocks, _, repl = sources[0].shape
    entries = len(EARLY) * layout.cap
    return pl.pallas_call(
        functools.partial(early_kernel, layout),
        out_shape=jax.ShapeDtypeStruct((blocks + 1, tile, repl), jnp.float32),
        in_specs=[SMEM] + [VMEM] * (1 + len(sources)),
        out_specs=VMEM,
        scratch_shapes=[pltpu.VMEM((entries, tile, repl), jnp.bfloat16)],
        compiler_params=params(),
        cost_estimate=pl.CostEstimate(flops=0, bytes_accessed=0, transcendentals=0),
    )(table, tiles, *sources)


def late_kernel(layout, last, table, scalars, tiles, far0, far1, far2, far3, field, xpos, ymom, *refs):
    if last:
        xout, yout, energy, xbuf, acc = refs
    else:
        xout, yout, xb, out1, out2, out3, xbuf, acc = refs
    blocks = xpos.shape[0]
    cap = layout.cap
    for i, far in enumerate((far0, far1, far2, far3)):
        for r in range(cap):
            xbuf[i * cap + r] = far[r]
    acc[...] = field[...]
    multiply(layout, table, tiles, xbuf, len(EARLY) * cap, len(LATE) * cap, acc)
    total = jnp.zeros((1, xpos.shape[2]), jnp.float32)
    for b in range(blocks):
        x, h = xpos[b], acc[b]
        if last:
            total += jnp.sum(x * h, axis=0, keepdims=True)
        x, y = update(scalars[0], scalars[1], h, x, ymom[b])
        xout[b] = x
        yout[b] = y
        if not last:
            xb[b] = x.astype(jnp.bfloat16)
    if last:
        energy[...] = -0.5 * total
    else:
        for flip, out in ((1, out1), (2, out2), (3, out3)):
            copy_blocks(table, layout.pack(0, flip), cap, xb, out)


def late(layout, last, table, scalars, tiles, packs, field, xpos, ymom):
    tile = tiles.shape[1]
    blocks, _, repl = xpos.shape
    entries = len(LATE) * layout.cap
    state = jax.ShapeDtypeStruct(xpos.shape, jnp.float32)
    if last:
        extra = (jax.ShapeDtypeStruct((1, repl), jnp.float32),)
    else:
        out = jax.ShapeDtypeStruct((layout.cap, tile, repl), jnp.bfloat16)
        extra = (jax.ShapeDtypeStruct(xpos.shape, jnp.bfloat16), out, out, out)
    return pl.pallas_call(
        functools.partial(late_kernel, layout, last),
        out_shape=(state, state) + extra,
        in_specs=[SMEM, SMEM] + [VMEM] * (1 + len(packs) + 3),
        out_specs=(VMEM,) * (2 + len(extra)),
        scratch_shapes=[
            pltpu.VMEM((entries, tile, repl), jnp.bfloat16),
            pltpu.VMEM((blocks + 1, tile, repl), jnp.float32),
        ],
        compiler_params=params(),
        cost_estimate=cost(entries, tile, repl, 20 * xpos.size),
    )(table, scalars, tiles, *packs, field, xpos, ymom)


def along_z(pairs, value):
    return lax.ppermute(value, "row", [(a * 4 + i, b * 4 + i) for a, b in pairs for i in range(4)])


def across(flip, value):
    return lax.ppermute(value, "row", [(i, i ^ flip) for i in range(16)])


def row_sum(part):
    devices = lax.axis_size("row")
    spread = jnp.broadcast_to(part, (devices,) + part.shape[1:])
    return jnp.sum(lax.all_to_all(spread, "row", split_axis=0, concat_axis=0, tiled=True), axis=0, keepdims=True)


def body_16(tiles, tile_rows, tile_cols, counts, positions, momenta):
    slots, tile, _ = tiles.shape
    repl = positions.shape[1]
    blocks = positions.shape[0] // tile
    cap = (slots + 15) // 16
    order = blocks * tile * 16
    layout = Layout(cap)
    pack_own = functools.partial(pack_shard_kernel, layout, 0)
    pack_first = functools.partial(pack_shard_kernel, layout, 1)
    pack_second = functools.partial(pack_second_kernel, layout)
    xpos = positions.reshape(blocks, tile, repl)
    ymom = momenta.reshape(blocks, tile, repl)
    own0 = xpos.astype(jnp.bfloat16)
    mine, note = plan(layout, blocks, tile_rows, tile_cols, counts, tiles)
    notes = jnp.concatenate([note] + [across(flip, note) for flip in (1, 2, 3)])
    table = make_table(layout, mine, notes.astype(jnp.int32).reshape(-1))
    packs0 = pack(pack_own, cap, 3, [table], [own0])
    asked = coeff = None
    for step in range(STEPS):
        last = step == STEPS - 1
        own1 = along_z(FIRST, own0)
        own2 = along_z(SECOND, own0)
        got0 = [across(flip, packs0[flip - 1]) for flip in (1, 2, 3)]
        if step == 0:
            notes, got0 = lax.optimization_barrier((notes, got0))
            far_notes = across(4, notes)
            asked = far_notes.astype(jnp.int32).reshape(-1)
        own1, got0 = lax.optimization_barrier((own1, got0))
        packs1 = pack(pack_first, cap, 3, [table], [own1])
        got1 = [across(flip, packs1[flip - 1]) for flip in (1, 2, 3)]
        if step == 0:
            half = jnp.broadcast_to(jnp.sum(notes[:, SUM_AT]) + jnp.sum(far_notes[:, SUM_AT]), (1, LANES))
            total = jnp.sum((half + across(8, half))[0, 0])
            coeff = 0.7 * jnp.sqrt((order - 1) / total)
        own2, got1 = lax.optimization_barrier((own2, got1))
        packs2 = pack(pack_second, cap, 7, [table, asked], [own1, own2])
        got2 = [across(flip, packs2[flip - 1]) for flip in (1, 2, 3)]
        far = [across(4 + flip, packs2[3 + flip]) for flip in range(4)]
        sources = [own0] + got0 + [own1] + got1 + [own2] + got2
        field = early(layout, table, tiles, sources)
        scalars = jnp.stack([jnp.float32(0.4 - 0.1 * step), coeff])
        outs = late(layout, last, table, scalars, tiles, far, field, xpos, ymom)
        xpos, ymom = outs[0], outs[1]
        if not last:
            own0, packs0 = outs[2], outs[3:]
    energy = row_sum(outs[2])
    return (xpos.reshape(positions.shape), ymom.reshape(momenta.shape), energy.reshape(repl))


def gathered_kernel(last, rows, cols, count, scalars, tiles, gathered, xpos, ymom, xout, yout, extra, xbuf, field, xsem):
    tile = xbuf.shape[1]
    used = count[0]

    def block_copy(s):
        return pltpu.make_async_copy(gathered.at[cols[s]], xbuf.at[s], xsem.at[s])

    @pl.loop(0, used)
    def _(s):
        block_copy(s).start()

    field[...] = jnp.zeros_like(field)

    @pl.loop(0, used)
    def _(s):
        block_copy(s).wait()
        here = pl.ds(pl.multiple_of(rows[s] * tile, tile), tile)
        field[here, :] += jnp.dot(tiles[s], xbuf[s], preferred_element_type=jnp.float32)

    x, h = xpos[...], field[...]
    if last:
        extra[...] = -0.5 * jnp.sum(x * h, axis=0, keepdims=True)
    x, y = update(scalars[0], scalars[1], h, x, ymom[...])
    xout[...] = x
    yout[...] = y
    if not last:
        extra[...] = x.astype(jnp.bfloat16)


def body_any(tiles, tile_rows, tile_cols, counts, positions, momenta):
    slots, tile, _ = tiles.shape
    order, repl = positions.shape
    devices = lax.axis_size("row")
    state = jax.ShapeDtypeStruct(positions.shape, jnp.float32)
    total = jnp.sum(lax.psum(squares(counts, tiles), "row"))
    coeff = 0.7 * jnp.sqrt((order * devices - 1) / total)
    xpos, ymom, extra = positions, momenta, positions.astype(jnp.bfloat16)
    for step in range(STEPS):
        last = step == STEPS - 1
        gathered = lax.all_gather(extra, "row", tiled=True).reshape(-1, tile, repl)
        scalars = jnp.stack([jnp.float32(0.4 - 0.1 * step), coeff])
        xpos, ymom, extra = pl.pallas_call(
            functools.partial(gathered_kernel, last),
            out_shape=(
                state,
                state,
                jax.ShapeDtypeStruct((1, repl), jnp.float32) if last else jax.ShapeDtypeStruct(state.shape, jnp.bfloat16),
            ),
            in_specs=[SMEM] * 4 + [VMEM, ANY, VMEM, VMEM],
            out_specs=(VMEM,) * 3,
            scratch_shapes=[
                pltpu.VMEM((slots, tile, repl), jnp.bfloat16),
                pltpu.VMEM(positions.shape, jnp.float32),
                pltpu.SemaphoreType.DMA((slots,)),
            ],
            compiler_params=params(),
        )(tile_rows, tile_cols, counts, scalars, tiles, gathered, xpos, ymom)
    return (xpos, ymom, lax.psum(extra, "row").reshape(repl))


def solution(mesh):
    in_specs = (
        P(("groups", "row"), None, None),
        P(("groups", "row")),
        P(("groups", "row")),
        P(("groups", "row")),
        P(("groups", "row"), None),
        P(("groups", "row"), None),
    )
    out_specs = (P(("groups", "row"), None), P(("groups", "row"), None), P("groups"))

    def body(tiles, *args):
        slots = tiles.shape[0]
        by_hand = mesh.shape["row"] == 16 and slots % GROUP == 0 and slots <= 96
        return (body_16 if by_hand else body_any)(tiles, *args)

    return jax.shard_map(body, mesh=mesh, in_specs=in_specs, out_specs=out_specs, check_vma=False)
```

```python
import functools

import jax
import jax.numpy as jnp
from jax import lax
from jax.experimental import pallas as pl
from jax.experimental.pallas import tpu as pltpu
from jax.sharding import PartitionSpec as P

STEPS = 4
GROUP = 6
LANES = 128
SUM_AT = LANES - 1
LIMIT = 16 * 2**20

SMEM = pl.BlockSpec(memory_space=pltpu.SMEM)
VMEM = pl.BlockSpec(memory_space=pltpu.VMEM)
ANY = pl.BlockSpec(memory_space=pl.ANY)


def params(limit=LIMIT):
    return pltpu.CompilerParams(vmem_limit_bytes=limit)


def squares_kernel(count, tiles, out):
    tile = tiles.shape[1]

    def add(s, acc):
        t = tiles[s].astype(jnp.float32)
        return acc + jnp.sum((t * t).reshape(tile // 8, 8, tile), axis=0)

    acc = lax.fori_loop(0, count[0], add, jnp.zeros((8, tile), jnp.float32))
    acc = jnp.sum(acc, axis=0, keepdims=True)
    out[...] = sum(acc[:, i : i + 128] for i in range(0, tile, 128))


def squares(count, tiles):
    return pl.pallas_call(
        squares_kernel,
        out_shape=jax.ShapeDtypeStruct((1, 128), jnp.float32),
        in_specs=[SMEM, VMEM],
        out_specs=VMEM,
        compiler_params=params(),
        cost_estimate=pl.CostEstimate(flops=2 * tiles.size, bytes_accessed=2 * tiles.size, transcendentals=0),
    )(count, tiles)


def update(pump, coeff, h, x, y):
    y = y + 0.5 * (-(x * x + pump) * x + coeff * h)
    return x + 0.5 * y, y


FIRST = ((0, 2), (3, 1), (1, 0), (2, 3))
SECOND = ((0, 1), (3, 2), (1, 3), (2, 0))
OUTWARD = ((1, 0), (2, 3))
MIDDLE = ((1, 2), (2, 1))


class Layout:
    def __init__(self, cap):
        self.cap = cap
        self.packs = 0
        self.entries = 9 * cap
        self.size = 9 * cap + 3 * 16 * cap

    def pack(self, j, flip):
        return self.packs + (j * 3 + flip - 1) * self.cap

    def entry(self, i):
        return self.entries + 3 * i


def whereabouts():
    me = lax.axis_index("row")
    z, yc = lax.div(me, 4), lax.rem(me, 4)
    inner = (z == 1) | (z == 2)
    near, skip = z ^ 1, z ^ 2
    return z, yc, inner, (z, jnp.where(inner, skip, near), jnp.where(inner, near, skip), z ^ 3)


EARLY = tuple((j, flip) for j in (0, 1, 2) for flip in (0, 2))
MEDIUM = tuple((j, flip) for j in (0, 1, 2) for flip in (1, 3))
LATE = tuple((3, flip) for flip in (0, 2, 1, 3))


def plan_kernel(layout, blocks, rows, cols, count, tiles, mine, note, seen, buffer, sems):
    cap = layout.cap
    keys = 16 * cap
    slots, tile, _ = buffer.shape
    chunks = [pl.ds(first, GROUP) for first in range(0, slots, GROUP)]
    copies = [pltpu.make_async_copy(tiles.at[c], buffer.at[c], sems.at[i]) for i, c in enumerate(chunks)]
    for copy in copies:
        copy.start()

    @pl.loop(0, 16)
    def _(d):
        seen[d] = 0

    @pl.loop(0, keys)
    def _(k):
        mine[k] = 0
        mine[keys + k] = blocks
        mine[2 * keys + k] = 0

    @pl.loop(0, count[0])
    def _(s):
        source = lax.div(cols[s], blocks)
        rank = seen[source]
        seen[source] = rank + 1
        key = source * cap + jnp.minimum(rank, cap - 1)
        mine[key] = s
        mine[keys + key] = rows[s]
        mine[2 * keys + key] = lax.rem(cols[s], blocks)

    lane = lax.broadcasted_iota(jnp.int32, note.shape, 1)
    wants = jnp.zeros(note.shape, jnp.int32)
    for k in range(keys):
        wants = jnp.where(lane == k, mine[2 * keys + k], wants)

    def add(s, acc):
        t = buffer[s].astype(jnp.float32)
        return acc + jnp.sum((t * t).reshape(tile // 8, 8, tile), axis=0)

    acc = jnp.zeros((8, tile), jnp.float32)
    for i, copy in enumerate(copies):
        copy.wait()
        acc = lax.fori_loop(i * GROUP, jnp.clip(count[0], i * GROUP, (i + 1) * GROUP), add, acc)
    note[...] = jnp.where(lane == SUM_AT, jnp.sum(acc), wants.astype(jnp.float32))


def plan(layout, blocks, rows, cols, count, tiles):
    return pl.pallas_call(
        functools.partial(plan_kernel, layout, blocks),
        out_shape=(
            jax.ShapeDtypeStruct((3 * 16 * layout.cap,), jnp.int32),
            jax.ShapeDtypeStruct((1, LANES), jnp.float32),
        ),
        in_specs=[SMEM] * 3 + [ANY],
        out_specs=(SMEM, VMEM),
        scratch_shapes=[
            pltpu.SMEM((16,), jnp.int32),
            pltpu.VMEM(tiles.shape, tiles.dtype),
            pltpu.SemaphoreType.DMA((tiles.shape[0] // GROUP,)),
        ],
        compiler_params=params(59 * 2**20),
        cost_estimate=pl.CostEstimate(flops=0, bytes_accessed=0, transcendentals=0),
    )(rows, cols, count, tiles)


def table_kernel(layout, mine, asked, table):
    cap = layout.cap
    keys = 16 * cap
    _, yc, _, zs = whereabouts()
    for j in range(3):
        for flip in (1, 2, 3):
            for r in range(cap):
                table[layout.pack(j, flip) + r] = asked[flip * LANES + (zs[j] * 4 + yc) * cap + r]
    for i, (j, flip) in enumerate(EARLY + MEDIUM + LATE):
        for r in range(cap):
            key = (zs[j] * 4 + (yc ^ flip)) * cap + r
            at = layout.entry(i * cap + r)
            table[at] = mine[key]
            table[at + 1] = mine[keys + key]
            table[at + 2] = mine[2 * keys + key]


def make_table(layout, mine, asked):
    return pl.pallas_call(
        functools.partial(table_kernel, layout),
        out_shape=jax.ShapeDtypeStruct((layout.size,), jnp.int32),
        in_specs=[SMEM] * 2,
        out_specs=SMEM,
        cost_estimate=pl.CostEstimate(flops=0, bytes_accessed=0, transcendentals=0),
    )(mine, asked)


def copy_asked(table, at, cap, shard, out, first=0):
    for r in range(cap):
        out[first + r] = shard[table[at + r]]


def copy_half(cap, source, half, out, first=0):
    for r in range(cap):
        out[first + r] = source[half * cap + r]


def fill_across_y(layout, j, table, shard, out):
    copy_asked(table, layout.pack(j, 2), layout.cap, shard, out)
    copy_asked(table, layout.pack(j, 3), layout.cap, shard, out, layout.cap)


def fill_far(layout, asked, z, shard, same_y, other_y):
    cap = layout.cap
    _, yc, _, _ = whereabouts()
    for flip, out in enumerate((same_y, same_y, other_y, other_y)):
        copy_asked(asked, flip * LANES + (z * 4 + yc) * cap, cap, shard, out, flip % 2 * cap)


def across_y_kernel(layout, j, table, shard, out):
    fill_across_y(layout, j, table, shard, out)


def outward_kernel(layout, asked, first, same_y, other_y):
    fill_far(layout, asked, whereabouts()[0] ^ 2, first, same_y, other_y)


def middle_kernel(layout, asked, own, same_y, other_y):
    fill_far(layout, asked, whereabouts()[0], own, same_y, other_y)


def core_kernel(layout, table, *refs):
    cap = layout.cap
    out = refs[6]
    for j in range(3):
        copy_asked(table, layout.pack(j, 1), cap, refs[j], out, 2 * j * cap)
        copy_half(cap, refs[3 + j], 1, out, (2 * j + 1) * cap)


def by_place(pairs, use):
    inner = whereabouts()[2]
    pl.when(inner)(lambda: use(*pairs[:2]))
    pl.when(jnp.logical_not(inner))(lambda: use(*pairs[2:]))


def core_late_kernel(layout, mid_same, mid_other, out_same, out_other, out):
    cap = layout.cap

    def use(same_y, other_y):
        copy_half(cap, same_y, 1, out)
        copy_half(cap, other_y, 1, out, cap)

    by_place((mid_same, mid_other, out_same, out_other), use)


def pack(kernel, sizes, tables, arrays):
    _, tile, repl = arrays[0].shape
    return pl.pallas_call(
        kernel,
        out_shape=[jax.ShapeDtypeStruct((size, tile, repl), jnp.bfloat16) for size in sizes],
        in_specs=[SMEM] * len(tables) + [VMEM] * len(arrays),
        out_specs=[VMEM] * len(sizes),
        compiler_params=params(),
        cost_estimate=pl.CostEstimate(flops=0, bytes_accessed=0, transcendentals=0),
    )(*tables, *arrays)


def multiply(layout, table, tiles, xbuf, first, number, field):
    def some(start, place):
        prods = [
            jnp.dot(tiles[table[layout.entry(start + i)]], xbuf[place + i], preferred_element_type=jnp.float32)
            for i in range(GROUP)
        ]
        for i, prod in enumerate(prods):
            field[table[layout.entry(start + i) + 1]] += prod

    if number <= 3 * GROUP:
        for place in range(0, number, GROUP):
            some(first + place, place)
    else:

        @pl.loop(0, number // GROUP)
        def _(g):
            some(first + g * GROUP, g * GROUP)


def take_own(layout, table, first, shard, xbuf, place):
    for r in range(layout.cap):
        xbuf[place + r] = shard[table[layout.entry(first + r) + 2]]


def early_kernel(layout, table, tiles, *refs):
    cap = layout.cap
    field, xbuf = refs[6:]
    for j in range(3):
        take_own(layout, table, 2 * j * cap, refs[j], xbuf, 2 * j * cap)
        copy_half(cap, refs[3 + j], 0, xbuf, (2 * j + 1) * cap)
    field[...] = jnp.zeros_like(field)
    multiply(layout, table, tiles, xbuf, 0, 6 * cap, field)


def medium_kernel(layout, table, tiles, core, before, field):
    field[...] = before[...]
    multiply(layout, table, tiles, core, 6 * layout.cap, 6 * layout.cap, field)


def products(kernel, layout, scratch, table, tiles, arrays, blocks):
    tile, repl = arrays[0].shape[1:]
    return pl.pallas_call(
        functools.partial(kernel, layout),
        out_shape=jax.ShapeDtypeStruct((blocks + 1, tile, repl), jnp.float32),
        in_specs=[SMEM] + [VMEM] * (1 + len(arrays)),
        out_specs=VMEM,
        scratch_shapes=[pltpu.VMEM((size, tile, repl), jnp.bfloat16) for size in scratch],
        compiler_params=params(),
        cost_estimate=pl.CostEstimate(flops=0, bytes_accessed=0, transcendentals=0),
    )(table, tiles, *arrays)


def late_kernel(layout, last, table, asked, scalars, tiles, *refs):
    far, (core, field, xpos, ymom), outs, (xbuf, acc) = refs[:4], refs[4:8], refs[8:-2], refs[-2:]
    xout, yout = outs[:2]
    blocks = xpos.shape[0]
    cap = layout.cap

    def use(same_y, other_y):
        copy_half(cap, same_y, 0, xbuf)
        copy_half(cap, other_y, 0, xbuf, cap)

    by_place(far, use)
    copy_half(cap, core, 0, xbuf, 2 * cap)
    copy_half(cap, core, 1, xbuf, 3 * cap)
    acc[...] = field[...]
    multiply(layout, table, tiles, xbuf, 12 * cap, 4 * cap, acc)
    total = jnp.zeros((1, xpos.shape[2]), jnp.float32)
    for b in range(blocks):
        x, h = xpos[b], acc[b]
        if last:
            total += jnp.sum(x * h, axis=0, keepdims=True)
        x, y = update(scalars[0], scalars[1], h, x, ymom[b])
        xout[b] = x
        yout[b] = y
        if not last:
            outs[2][b] = x.astype(jnp.bfloat16)
    if last:
        outs[2][...] = -0.5 * total
    else:
        xb, y0, same_y, other_y = outs[2:]
        fill_across_y(layout, 0, table, xb, y0)
        fill_far(layout, asked, whereabouts()[0], xb, same_y, other_y)


def late(layout, last, table, asked, scalars, tiles, far, core, field, xpos, ymom):
    tile = tiles.shape[1]
    blocks, _, repl = xpos.shape
    entries = 4 * layout.cap
    state = jax.ShapeDtypeStruct(xpos.shape, jnp.float32)
    if last:
        extra = (jax.ShapeDtypeStruct((1, repl), jnp.float32),)
    else:
        out = jax.ShapeDtypeStruct((2 * layout.cap, tile, repl), jnp.bfloat16)
        extra = (jax.ShapeDtypeStruct(xpos.shape, jnp.bfloat16), out, out, out)
    return pl.pallas_call(
        functools.partial(late_kernel, layout, last),
        out_shape=(state, state) + extra,
        in_specs=[SMEM] * 3 + [VMEM] * (1 + len(far) + 4),
        out_specs=(VMEM,) * (2 + len(extra)),
        scratch_shapes=[
            pltpu.VMEM((entries, tile, repl), jnp.bfloat16),
            pltpu.VMEM((blocks + 1, tile, repl), jnp.float32),
        ],
        compiler_params=params(),
        cost_estimate=pl.CostEstimate(
            flops=2 * entries * tile * tile * repl,
            bytes_accessed=entries * tile * (tile + repl) * 2 + 20 * xpos.size,
            transcendentals=0,
        ),
    )(table, asked, scalars, tiles, *far, core, field, xpos, ymom)


def along_z(pairs, value, flip=0):
    return lax.ppermute(value, "row", [(a * 4 + i, b * 4 + (i ^ flip)) for a, b in pairs for i in range(4)])


def across(flip, value):
    return lax.ppermute(value, "row", [(i, i ^ flip) for i in range(16)])


def row_sum(part):
    devices = lax.axis_size("row")
    spread = jnp.broadcast_to(part, (devices,) + part.shape[1:])
    return jnp.sum(lax.all_to_all(spread, "row", split_axis=0, concat_axis=0, tiled=True), axis=0, keepdims=True)


def body_16(tiles, tile_rows, tile_cols, counts, positions, momenta):
    slots, tile, _ = tiles.shape
    repl = positions.shape[1]
    blocks = positions.shape[0] // tile
    cap = (slots + 15) // 16
    order = blocks * tile * 16
    layout = Layout(cap)

    def across_y(j, shard):
        return pack(functools.partial(across_y_kernel, layout, j), [2 * cap], [table], [shard])[0]

    def far_packs(kernel, asked, shard):
        return pack(functools.partial(kernel, layout), [2 * cap] * 2, [asked], [shard])

    def to_core(kernel, size, tables, arrays):
        return across(1, pack(functools.partial(kernel, layout), [size * cap], tables, arrays)[0])

    xpos = positions.reshape(blocks, tile, repl)
    ymom = momenta.reshape(blocks, tile, repl)
    own0 = xpos.astype(jnp.bfloat16)
    mine, note = plan(layout, blocks, tile_rows, tile_cols, counts, tiles)
    notes = jnp.concatenate([note] + [across(flip, note) for flip in (1, 2, 3)])
    table = make_table(layout, mine, notes.astype(jnp.int32).reshape(-1))
    y0 = across_y(0, own0)
    for step in range(STEPS):
        last = step == STEPS - 1
        own1 = along_z(FIRST, own0)
        own2 = along_z(SECOND, own0)
        y0 = across(2, y0)
        if step == 0:
            notes, y0 = lax.optimization_barrier((notes, y0))
            plane = jnp.broadcast_to(jnp.sum(notes[:, SUM_AT]), (1, LANES))
            notes_out, notes_mid, plane_skip = across(4, notes), across(12, notes), across(8, plane)
            notes_out, notes_mid, plane_skip = lax.optimization_barrier((notes_out, notes_mid, plane_skip))
            asked_out = notes_out.astype(jnp.int32).reshape(-1)
            asked_mid = notes_mid.astype(jnp.int32).reshape(-1)
            mid = far_packs(middle_kernel, asked_mid, own0)
        mid = [along_z(MIDDLE, mid[0]), along_z(MIDDLE, mid[1], 2)]
        own1, y0 = lax.optimization_barrier((own1, y0))
        y1 = across(2, across_y(1, own1))
        out_same, out_other = far_packs(outward_kernel, asked_out, own1)
        out_same = along_z(OUTWARD, out_same)
        own2, out_other, y1 = lax.optimization_barrier((own2, out_other, y1))
        out_other = along_z(OUTWARD, out_other, 2)
        y2 = across(2, across_y(2, own2))
        out_other, y2, out_same, mid = lax.optimization_barrier((out_other, y2, out_same, mid))
        here = [own0, own1, own2, y0, y1, y2]
        core = to_core(core_kernel, 6, [table], here)
        far = mid + [out_same, out_other]
        core_late = to_core(core_late_kernel, 2, [], far)
        field = products(early_kernel, layout, [6 * cap], table, tiles, here, blocks)
        field = products(medium_kernel, layout, [], table, tiles, [core, field], blocks)
        if step == 0:
            total = plane[0, 0] + plane_skip[0, 0] + jnp.sum(notes_out[:, SUM_AT]) + jnp.sum(notes_mid[:, SUM_AT])
            coeff = 0.7 * jnp.sqrt((order - 1) / total)
        scalars = jnp.stack([jnp.float32(0.4 - 0.1 * step), coeff])
        outs = late(layout, last, table, asked_mid, scalars, tiles, far, core_late, field, xpos, ymom)
        xpos, ymom = outs[0], outs[1]
        if not last:
            own0, y0, mid = outs[2], outs[3], outs[4:]
    energy = row_sum(outs[2])
    return (xpos.reshape(positions.shape), ymom.reshape(momenta.shape), energy.reshape(repl))


def gathered_kernel(last, rows, cols, count, scalars, tiles, gathered, xpos, ymom, xout, yout, extra, xbuf, field, xsem):
    tile = xbuf.shape[1]
    used = count[0]

    def block_copy(s):
        return pltpu.make_async_copy(gathered.at[cols[s]], xbuf.at[s], xsem.at[s])

    @pl.loop(0, used)
    def _(s):
        block_copy(s).start()

    field[...] = jnp.zeros_like(field)

    @pl.loop(0, used)
    def _(s):
        block_copy(s).wait()
        here = pl.ds(pl.multiple_of(rows[s] * tile, tile), tile)
        field[here, :] += jnp.dot(tiles[s], xbuf[s], preferred_element_type=jnp.float32)

    x, h = xpos[...], field[...]
    if last:
        extra[...] = -0.5 * jnp.sum(x * h, axis=0, keepdims=True)
    x, y = update(scalars[0], scalars[1], h, x, ymom[...])
    xout[...] = x
    yout[...] = y
    if not last:
        extra[...] = x.astype(jnp.bfloat16)


def body_any(tiles, tile_rows, tile_cols, counts, positions, momenta):
    slots, tile, _ = tiles.shape
    order, repl = positions.shape
    devices = lax.axis_size("row")
    state = jax.ShapeDtypeStruct(positions.shape, jnp.float32)
    total = jnp.sum(lax.psum(squares(counts, tiles), "row"))
    coeff = 0.7 * jnp.sqrt((order * devices - 1) / total)
    xpos, ymom, extra = positions, momenta, positions.astype(jnp.bfloat16)
    for step in range(STEPS):
        last = step == STEPS - 1
        gathered = lax.all_gather(extra, "row", tiled=True).reshape(-1, tile, repl)
        scalars = jnp.stack([jnp.float32(0.4 - 0.1 * step), coeff])
        xpos, ymom, extra = pl.pallas_call(
            functools.partial(gathered_kernel, last),
            out_shape=(
                state,
                state,
                jax.ShapeDtypeStruct((1, repl), jnp.float32) if last else jax.ShapeDtypeStruct(state.shape, jnp.bfloat16),
            ),
            in_specs=[SMEM] * 4 + [VMEM, ANY, VMEM, VMEM],
            out_specs=(VMEM,) * 3,
            scratch_shapes=[
                pltpu.VMEM((slots, tile, repl), jnp.bfloat16),
                pltpu.VMEM(positions.shape, jnp.float32),
                pltpu.SemaphoreType.DMA((slots,)),
            ],
            compiler_params=params(),
        )(tile_rows, tile_cols, counts, scalars, tiles, gathered, xpos, ymom)
    return (xpos, ymom, lax.psum(extra, "row").reshape(repl))


def solution(mesh):
    in_specs = (
        P(("groups", "row"), None, None),
        P(("groups", "row")),
        P(("groups", "row")),
        P(("groups", "row")),
        P(("groups", "row"), None),
        P(("groups", "row"), None),
    )
    out_specs = (P(("groups", "row"), None), P(("groups", "row"), None), P("groups"))

    def body(tiles, *args):
        slots = tiles.shape[0]
        by_hand = mesh.shape["row"] == 16 and slots % GROUP == 0 and slots <= 96
        return (body_16 if by_hand else body_any)(tiles, *args)

    return jax.shard_map(body, mesh=mesh, in_specs=in_specs, out_specs=out_specs, check_vma=False)
```

```python
import functools

import jax
import jax.numpy as jnp
from jax import lax
from jax.experimental import pallas as pl
from jax.experimental.pallas import tpu as pltpu
from jax.sharding import PartitionSpec as P

STEPS = 4
GROUP = 6
LANES = 128
SUM_AT = LANES - 1
LIMIT = 16 * 2**20

SMEM = pl.BlockSpec(memory_space=pltpu.SMEM)
VMEM = pl.BlockSpec(memory_space=pltpu.VMEM)
ANY = pl.BlockSpec(memory_space=pl.ANY)


def params(limit=LIMIT):
    return pltpu.CompilerParams(vmem_limit_bytes=limit)


def squares_kernel(count, tiles, out):
    tile = tiles.shape[1]

    def add(s, acc):
        t = tiles[s].astype(jnp.float32)
        return acc + jnp.sum((t * t).reshape(tile // 8, 8, tile), axis=0)

    acc = lax.fori_loop(0, count[0], add, jnp.zeros((8, tile), jnp.float32))
    acc = jnp.sum(acc, axis=0, keepdims=True)
    out[...] = sum(acc[:, i : i + 128] for i in range(0, tile, 128))


def squares(count, tiles):
    return pl.pallas_call(
        squares_kernel,
        out_shape=jax.ShapeDtypeStruct((1, 128), jnp.float32),
        in_specs=[SMEM, VMEM],
        out_specs=VMEM,
        compiler_params=params(),
        cost_estimate=pl.CostEstimate(flops=2 * tiles.size, bytes_accessed=2 * tiles.size, transcendentals=0),
    )(count, tiles)


def update(pump, coeff, h, x, y):
    y = y + 0.5 * (-(x * x + pump) * x + coeff * h)
    return x + 0.5 * y, y


FIRST = ((0, 2), (3, 1), (1, 0), (2, 3))
SECOND = ((0, 1), (3, 2), (1, 3), (2, 0))
OUTWARD = ((1, 0), (2, 3))
MIDDLE = ((1, 2), (2, 1))


class Layout:
    def __init__(self, cap):
        self.cap = cap
        self.packs = 0
        self.entries = 12 * cap
        self.size = 12 * cap + 3 * 16 * cap

    def pack(self, j, flip):
        return self.packs + (j * 3 + flip - 1) * self.cap

    def entry(self, i):
        return self.entries + 3 * i


def whereabouts():
    me = lax.axis_index("row")
    z, yc = lax.div(me, 4), lax.rem(me, 4)
    inner = (z == 1) | (z == 2)
    near, skip = z ^ 1, z ^ 2
    return z, yc, inner, (z, jnp.where(inner, skip, near), jnp.where(inner, near, skip), z ^ 3)


EARLY = tuple((j, flip) for j in range(3) for flip in range(4))
LATE = tuple((3, flip) for flip in range(4))


def plan_kernel(layout, blocks, rows, cols, count, tiles, mine, note, seen, buffer, sems):
    cap = layout.cap
    keys = 16 * cap
    slots, tile, _ = buffer.shape
    chunks = [pl.ds(first, GROUP) for first in range(0, slots, GROUP)]
    copies = [pltpu.make_async_copy(tiles.at[c], buffer.at[c], sems.at[i]) for i, c in enumerate(chunks)]
    for copy in copies:
        copy.start()

    @pl.loop(0, 16)
    def _(d):
        seen[d] = 0

    @pl.loop(0, keys)
    def _(k):
        mine[k] = 0
        mine[keys + k] = blocks
        mine[2 * keys + k] = 0

    @pl.loop(0, count[0])
    def _(s):
        source = lax.div(cols[s], blocks)
        rank = seen[source]
        seen[source] = rank + 1
        key = source * cap + jnp.minimum(rank, cap - 1)
        mine[key] = s
        mine[keys + key] = rows[s]
        mine[2 * keys + key] = lax.rem(cols[s], blocks)

    lane = lax.broadcasted_iota(jnp.int32, note.shape, 1)
    wants = jnp.zeros(note.shape, jnp.int32)
    for k in range(keys):
        wants = jnp.where(lane == k, mine[2 * keys + k], wants)

    def add(s, acc):
        t = buffer[s].astype(jnp.float32)
        return acc + jnp.sum((t * t).reshape(tile // 8, 8, tile), axis=0)

    acc = jnp.zeros((8, tile), jnp.float32)
    for i, copy in enumerate(copies):
        copy.wait()
        acc = lax.fori_loop(i * GROUP, jnp.clip(count[0], i * GROUP, (i + 1) * GROUP), add, acc)
    note[...] = jnp.where(lane == SUM_AT, jnp.sum(acc), wants.astype(jnp.float32))


def plan(layout, blocks, rows, cols, count, tiles):
    return pl.pallas_call(
        functools.partial(plan_kernel, layout, blocks),
        out_shape=(
            jax.ShapeDtypeStruct((3 * 16 * layout.cap,), jnp.int32),
            jax.ShapeDtypeStruct((1, LANES), jnp.float32),
        ),
        in_specs=[SMEM] * 3 + [ANY],
        out_specs=(SMEM, VMEM),
        scratch_shapes=[
            pltpu.SMEM((16,), jnp.int32),
            pltpu.VMEM(tiles.shape, tiles.dtype),
            pltpu.SemaphoreType.DMA((tiles.shape[0] // GROUP,)),
        ],
        compiler_params=params(59 * 2**20),
        cost_estimate=pl.CostEstimate(flops=0, bytes_accessed=0, transcendentals=0),
    )(rows, cols, count, tiles)


def table_kernel(layout, mine, asked, table):
    cap = layout.cap
    keys = 16 * cap
    _, yc, _, zs = whereabouts()
    for j in range(4):
        for flip in (1, 2, 3):
            for r in range(cap):
                table[layout.pack(j, flip) + r] = asked[flip * LANES + (zs[j] * 4 + yc) * cap + r]
    for i, (j, flip) in enumerate(EARLY + LATE):
        for r in range(cap):
            key = (zs[j] * 4 + (yc ^ flip)) * cap + r
            at = layout.entry(i * cap + r)
            table[at] = mine[key]
            table[at + 1] = mine[keys + key]
            table[at + 2] = mine[2 * keys + key]


def make_table(layout, mine, asked):
    return pl.pallas_call(
        functools.partial(table_kernel, layout),
        out_shape=jax.ShapeDtypeStruct((layout.size,), jnp.int32),
        in_specs=[SMEM] * 2,
        out_specs=SMEM,
        cost_estimate=pl.CostEstimate(flops=0, bytes_accessed=0, transcendentals=0),
    )(mine, asked)


def copy_asked(layout, table, j, flip, shard, out, first=0):
    at = layout.pack(j, flip)
    for r in range(layout.cap):
        out[first + r] = shard[table[at + r]]


def copy_part(cap, source, part, out, first):
    for r in range(cap):
        out[first + r] = source[part * cap + r]


def by_place(mid, out, use):
    inner = whereabouts()[2]
    pl.when(inner)(lambda: use(mid))
    pl.when(jnp.logical_not(inner))(lambda: use(out))


def other_y_kernel(layout, js, table, *refs):
    shards, outs = refs[:-2], refs[-2:]
    for i, (j, shard) in enumerate(zip(js, shards)):
        for flip in (2, 3):
            copy_asked(layout, table, j, flip, shard, outs[flip - 2], i * layout.cap)


def second_kernel(layout, table, own, first, second, out2, out3, core):
    other_y_kernel(layout, (2,), table, second, out2, out3)
    for j, shard in enumerate((own, first, second)):
        copy_asked(layout, table, j, 1, shard, core, j * layout.cap)


def third_kernel(layout, table, mid, out, out2, out3, core):
    def use(shard):
        other_y_kernel(layout, (3,), table, shard, out2, out3)
        copy_asked(layout, table, 3, 1, shard, core)

    by_place(mid, out, use)


def pack(kernel, sizes, table, arrays):
    _, tile, repl = arrays[0].shape
    return pl.pallas_call(
        kernel,
        out_shape=[jax.ShapeDtypeStruct((size, tile, repl), jnp.bfloat16) for size in sizes],
        in_specs=[SMEM] + [VMEM] * len(arrays),
        out_specs=[VMEM] * len(sizes),
        compiler_params=params(),
        cost_estimate=pl.CostEstimate(flops=0, bytes_accessed=0, transcendentals=0),
    )(table, *arrays)


def multiply(layout, table, tiles, xbuf, first, number, field):
    def some(start, place):
        prods = [
            jnp.dot(tiles[table[layout.entry(start + i)]], xbuf[place + i], preferred_element_type=jnp.float32)
            for i in range(GROUP)
        ]
        for i, prod in enumerate(prods):
            field[table[layout.entry(start + i) + 1]] += prod

    if number <= 3 * GROUP:
        for place in range(0, number, GROUP):
            some(first + place, place)
    else:

        @pl.loop(0, number // GROUP)
        def _(g):
            some(first + g * GROUP, g * GROUP)


def take_own(layout, table, entry, shard, xbuf, place):
    for r in range(layout.cap):
        xbuf[place + r] = shard[table[layout.entry(entry + r) + 2]]


def early_kernel(layout, parts, table, tiles, *refs):
    cap = layout.cap
    field, xbuf = refs[-2:]
    core = refs[3]
    for j in range(3):
        base = 4 * cap * j
        take_own(layout, table, base, refs[j], xbuf, base)
        copy_part(cap, core, j, xbuf, base + cap)
        ref, part = parts[j]
        copy_part(cap, refs[ref], part, xbuf, base + 2 * cap)
        copy_part(cap, refs[ref + 1], part, xbuf, base + 3 * cap)
    field[...] = jnp.zeros_like(field)
    multiply(layout, table, tiles, xbuf, 0, 12 * cap, field)


def early(layout, parts, table, tiles, arrays):
    tile = tiles.shape[1]
    blocks, _, repl = arrays[0].shape
    return pl.pallas_call(
        functools.partial(early_kernel, layout, parts),
        out_shape=jax.ShapeDtypeStruct((blocks + 1, tile, repl), jnp.float32),
        in_specs=[SMEM] + [VMEM] * (1 + len(arrays)),
        out_specs=VMEM,
        scratch_shapes=[pltpu.VMEM((12 * layout.cap, tile, repl), jnp.bfloat16)],
        compiler_params=params(),
        cost_estimate=pl.CostEstimate(flops=0, bytes_accessed=0, transcendentals=0),
    )(table, tiles, *arrays)


def late_kernel(layout, last, table, scalars, tiles, mid, out, core, got2, got3, field, xpos, ymom, *refs):
    outs, (xbuf, acc) = refs[:-2], refs[-2:]
    xout, yout = outs[:2]
    blocks = xpos.shape[0]
    cap = layout.cap
    by_place(mid, out, lambda shard: take_own(layout, table, 12 * cap, shard, xbuf, 0))
    for i, got in enumerate((core, got2, got3)):
        copy_part(cap, got, 0, xbuf, (1 + i) * cap)
    acc[...] = field[...]
    multiply(layout, table, tiles, xbuf, 12 * cap, 4 * cap, acc)
    total = jnp.zeros((1, xpos.shape[2]), jnp.float32)
    for b in range(blocks):
        x, h = xpos[b], acc[b]
        if last:
            total += jnp.sum(x * h, axis=0, keepdims=True)
        x, y = update(scalars[0], scalars[1], h, x, ymom[b])
        xout[b] = x
        yout[b] = y
        if not last:
            outs[2][b] = x.astype(jnp.bfloat16)
    if last:
        outs[2][...] = -0.5 * total
    else:
        other_y_kernel(layout, (0,), table, *outs[2:])


def late(layout, last, table, scalars, tiles, sources, field, xpos, ymom):
    tile = tiles.shape[1]
    blocks, _, repl = xpos.shape
    entries = 4 * layout.cap
    state = jax.ShapeDtypeStruct(xpos.shape, jnp.float32)
    if last:
        extra = (jax.ShapeDtypeStruct((1, repl), jnp.float32),)
    else:
        out = jax.ShapeDtypeStruct((layout.cap, tile, repl), jnp.bfloat16)
        extra = (jax.ShapeDtypeStruct(xpos.shape, jnp.bfloat16), out, out)
    return pl.pallas_call(
        functools.partial(late_kernel, layout, last),
        out_shape=(state, state) + extra,
        in_specs=[SMEM, SMEM] + [VMEM] * (1 + len(sources) + 3),
        out_specs=(VMEM,) * (2 + len(extra)),
        scratch_shapes=[
            pltpu.VMEM((entries, tile, repl), jnp.bfloat16),
            pltpu.VMEM((blocks + 1, tile, repl), jnp.float32),
        ],
        compiler_params=params(),
        cost_estimate=pl.CostEstimate(
            flops=2 * entries * tile * tile * repl,
            bytes_accessed=entries * tile * (tile + repl) * 2 + 20 * xpos.size,
            transcendentals=0,
        ),
    )(table, scalars, tiles, *sources, field, xpos, ymom)


def along_z(pairs, value):
    return lax.ppermute(value, "row", [(a * 4 + i, b * 4 + i) for a, b in pairs for i in range(4)])


def across(flip, value):
    return lax.ppermute(value, "row", [(i, i ^ flip) for i in range(16)])


def row_sum(part):
    devices = lax.axis_size("row")
    spread = jnp.broadcast_to(part, (devices,) + part.shape[1:])
    return jnp.sum(lax.all_to_all(spread, "row", split_axis=0, concat_axis=0, tiled=True), axis=0, keepdims=True)


def body_16(tiles, tile_rows, tile_cols, counts, positions, momenta):
    slots, tile, _ = tiles.shape
    repl = positions.shape[1]
    blocks = positions.shape[0] // tile
    cap = (slots + 15) // 16
    order = blocks * tile * 16
    layout = Layout(cap)

    def other_y(js, shards):
        kernel = functools.partial(other_y_kernel, layout, js)
        return pack(kernel, [len(js) * cap] * 2, table, shards)

    def to_other_y(packs):
        return [across(2, packs[0]), across(3, packs[1])]

    xpos = positions.reshape(blocks, tile, repl)
    ymom = momenta.reshape(blocks, tile, repl)
    own0 = xpos.astype(jnp.bfloat16)
    mine, note = plan(layout, blocks, tile_rows, tile_cols, counts, tiles)
    notes = jnp.concatenate([note] + [across(flip, note) for flip in (1, 2, 3)])
    table = make_table(layout, mine, notes.astype(jnp.int32).reshape(-1))
    packs0 = None
    for step in range(STEPS):
        last = step == STEPS - 1
        own1 = along_z(FIRST, own0)
        own2 = along_z(SECOND, own0)
        mid = along_z(MIDDLE, own0)
        if step == 0:
            out = along_z(OUTWARD, own1)
            got1 = to_other_y(other_y((0, 1), [own0, own1]))
            own2, got1 = lax.optimization_barrier((own2, got1))
            parts = ((4, 0), (4, 1), (6, 0))
            got = got1
        else:
            got0 = to_other_y(packs0)
            own1, got0 = lax.optimization_barrier((own1, got0))
            out = along_z(OUTWARD, own1)
            got1 = to_other_y(other_y((1,), [own1]))
            own2, got1 = lax.optimization_barrier((own2, got1))
            parts = ((4, 0), (6, 0), (8, 0))
            got = got0 + got1
        packs2 = pack(functools.partial(second_kernel, layout), [cap, cap, 3 * cap], table, [own0, own1, own2])
        got = got + to_other_y(packs2)
        core = across(1, packs2[2])
        if step == 0:
            notes, core = lax.optimization_barrier((notes, core))
            plane = jnp.broadcast_to(jnp.sum(notes[:, SUM_AT]), (1, LANES))
            half = plane + across(4, plane)
        packs3 = pack(functools.partial(third_kernel, layout), [cap] * 3, table, [mid, out])
        far = [mid, out, across(1, packs3[2])] + to_other_y(packs3)
        field = early(layout, parts, table, tiles, [own0, own1, own2, core] + got)
        if step == 0:
            total = (half + across(8, half))[0, 0]
            coeff = 0.7 * jnp.sqrt((order - 1) / total)
        scalars = jnp.stack([jnp.float32(0.4 - 0.1 * step), coeff])
        outs = late(layout, last, table, scalars, tiles, far, field, xpos, ymom)
        xpos, ymom = outs[0], outs[1]
        if not last:
            own0, packs0 = outs[2], outs[3:]
    energy = row_sum(outs[2])
    return (xpos.reshape(positions.shape), ymom.reshape(momenta.shape), energy.reshape(repl))


def gathered_kernel(last, rows, cols, count, scalars, tiles, gathered, xpos, ymom, xout, yout, extra, xbuf, field, xsem):
    tile = xbuf.shape[1]
    used = count[0]

    def block_copy(s):
        return pltpu.make_async_copy(gathered.at[cols[s]], xbuf.at[s], xsem.at[s])

    @pl.loop(0, used)
    def _(s):
        block_copy(s).start()

    field[...] = jnp.zeros_like(field)

    @pl.loop(0, used)
    def _(s):
        block_copy(s).wait()
        here = pl.ds(pl.multiple_of(rows[s] * tile, tile), tile)
        field[here, :] += jnp.dot(tiles[s], xbuf[s], preferred_element_type=jnp.float32)

    x, h = xpos[...], field[...]
    if last:
        extra[...] = -0.5 * jnp.sum(x * h, axis=0, keepdims=True)
    x, y = update(scalars[0], scalars[1], h, x, ymom[...])
    xout[...] = x
    yout[...] = y
    if not last:
        extra[...] = x.astype(jnp.bfloat16)


def body_any(tiles, tile_rows, tile_cols, counts, positions, momenta):
    slots, tile, _ = tiles.shape
    order, repl = positions.shape
    devices = lax.axis_size("row")
    state = jax.ShapeDtypeStruct(positions.shape, jnp.float32)
    total = jnp.sum(lax.psum(squares(counts, tiles), "row"))
    coeff = 0.7 * jnp.sqrt((order * devices - 1) / total)
    xpos, ymom, extra = positions, momenta, positions.astype(jnp.bfloat16)
    for step in range(STEPS):
        last = step == STEPS - 1
        gathered = lax.all_gather(extra, "row", tiled=True).reshape(-1, tile, repl)
        scalars = jnp.stack([jnp.float32(0.4 - 0.1 * step), coeff])
        xpos, ymom, extra = pl.pallas_call(
            functools.partial(gathered_kernel, last),
            out_shape=(
                state,
                state,
                jax.ShapeDtypeStruct((1, repl), jnp.float32) if last else jax.ShapeDtypeStruct(state.shape, jnp.bfloat16),
            ),
            in_specs=[SMEM] * 4 + [VMEM, ANY, VMEM, VMEM],
            out_specs=(VMEM,) * 3,
            scratch_shapes=[
                pltpu.VMEM((slots, tile, repl), jnp.bfloat16),
                pltpu.VMEM(positions.shape, jnp.float32),
                pltpu.SemaphoreType.DMA((slots,)),
            ],
            compiler_params=params(),
        )(tile_rows, tile_cols, counts, scalars, tiles, gathered, xpos, ymom)
    return (xpos, ymom, lax.psum(extra, "row").reshape(repl))


def solution(mesh):
    in_specs = (
        P(("groups", "row"), None, None),
        P(("groups", "row")),
        P(("groups", "row")),
        P(("groups", "row")),
        P(("groups", "row"), None),
        P(("groups", "row"), None),
    )
    out_specs = (P(("groups", "row"), None), P(("groups", "row"), None), P("groups"))

    def body(tiles, *args):
        slots = tiles.shape[0]
        by_hand = mesh.shape["row"] == 16 and slots % GROUP == 0 and slots <= 96
        return (body_16 if by_hand else body_any)(tiles, *args)

    return jax.shard_map(body, mesh=mesh, in_specs=in_specs, out_specs=out_specs, check_vma=False)
```

```python
import functools

import jax
import jax.numpy as jnp
from jax import lax
from jax.experimental import pallas as pl
from jax.experimental.pallas import tpu as pltpu
from jax.sharding import PartitionSpec as P

STEPS = 4
GROUP = 6
LANES = 128
SUM_AT = LANES - 1
LIMIT = 16 * 2**20

SMEM = pl.BlockSpec(memory_space=pltpu.SMEM)
VMEM = pl.BlockSpec(memory_space=pltpu.VMEM)
ANY = pl.BlockSpec(memory_space=pl.ANY)


def params(limit=LIMIT):
    return pltpu.CompilerParams(vmem_limit_bytes=limit)


def squares_kernel(count, tiles, out):
    tile = tiles.shape[1]

    def add(s, acc):
        t = tiles[s].astype(jnp.float32)
        return acc + jnp.sum((t * t).reshape(tile // 8, 8, tile), axis=0)

    acc = lax.fori_loop(0, count[0], add, jnp.zeros((8, tile), jnp.float32))
    acc = jnp.sum(acc, axis=0, keepdims=True)
    out[...] = sum(acc[:, i : i + 128] for i in range(0, tile, 128))


def squares(count, tiles):
    return pl.pallas_call(
        squares_kernel,
        out_shape=jax.ShapeDtypeStruct((1, 128), jnp.float32),
        in_specs=[SMEM, VMEM],
        out_specs=VMEM,
        compiler_params=params(),
        cost_estimate=pl.CostEstimate(flops=2 * tiles.size, bytes_accessed=2 * tiles.size, transcendentals=0),
    )(count, tiles)


def update(pump, coeff, h, x, y):
    y = y + 0.5 * (-(x * x + pump) * x + coeff * h)
    return x + 0.5 * y, y


FIRST = ((0, 2), (3, 1), (1, 0), (2, 3))
SECOND = ((0, 1), (3, 2), (1, 3), (2, 0))
OUTWARD = ((1, 0), (2, 3))
MIDDLE = ((1, 2), (2, 1))


class Layout:
    def __init__(self, cap):
        self.cap = cap
        self.packs = 0
        self.entries = 12 * cap
        self.size = 12 * cap + 3 * 16 * cap

    def pack(self, j, flip):
        return self.packs + (j * 3 + flip - 1) * self.cap

    def entry(self, i):
        return self.entries + 3 * i


def whereabouts():
    me = lax.axis_index("row")
    z, yc = lax.div(me, 4), lax.rem(me, 4)
    inner = (z == 1) | (z == 2)
    near, skip = z ^ 1, z ^ 2
    return z, yc, inner, (z, jnp.where(inner, skip, near), jnp.where(inner, near, skip), z ^ 3)


EARLY = tuple((j, flip) for j in range(3) for flip in range(4))
LATE = tuple((3, flip) for flip in range(4))


def plan_kernel(layout, blocks, rows, cols, count, tiles, mine, note, seen, buffer, sems):
    cap = layout.cap
    keys = 16 * cap
    slots, tile, _ = buffer.shape
    chunks = [pl.ds(first, GROUP) for first in range(0, slots, GROUP)]
    copies = [pltpu.make_async_copy(tiles.at[c], buffer.at[c], sems.at[i]) for i, c in enumerate(chunks)]
    for copy in copies:
        copy.start()

    @pl.loop(0, 16)
    def _(d):
        seen[d] = 0

    @pl.loop(0, keys)
    def _(k):
        mine[k] = 0
        mine[keys + k] = blocks
        mine[2 * keys + k] = 0

    @pl.loop(0, count[0])
    def _(s):
        source = lax.div(cols[s], blocks)
        rank = seen[source]
        seen[source] = rank + 1
        key = source * cap + jnp.minimum(rank, cap - 1)
        mine[key] = s
        mine[keys + key] = rows[s]
        mine[2 * keys + key] = lax.rem(cols[s], blocks)

    lane = lax.broadcasted_iota(jnp.int32, note.shape, 1)
    wants = jnp.zeros(note.shape, jnp.int32)
    for k in range(keys):
        wants = jnp.where(lane == k, mine[2 * keys + k], wants)

    def add(s, acc):
        t = buffer[s].astype(jnp.float32)
        return acc + jnp.sum((t * t).reshape(tile // 8, 8, tile), axis=0)

    acc = jnp.zeros((8, tile), jnp.float32)
    for i, copy in enumerate(copies):
        copy.wait()
        acc = lax.fori_loop(i * GROUP, jnp.clip(count[0], i * GROUP, (i + 1) * GROUP), add, acc)
    note[...] = jnp.where(lane == SUM_AT, jnp.sum(acc), wants.astype(jnp.float32))


def plan(layout, blocks, rows, cols, count, tiles):
    return pl.pallas_call(
        functools.partial(plan_kernel, layout, blocks),
        out_shape=(
            jax.ShapeDtypeStruct((3 * 16 * layout.cap,), jnp.int32),
            jax.ShapeDtypeStruct((1, LANES), jnp.float32),
        ),
        in_specs=[SMEM] * 3 + [ANY],
        out_specs=(SMEM, VMEM),
        scratch_shapes=[
            pltpu.SMEM((16,), jnp.int32),
            pltpu.VMEM(tiles.shape, tiles.dtype),
            pltpu.SemaphoreType.DMA((tiles.shape[0] // GROUP,)),
        ],
        compiler_params=params(59 * 2**20),
        cost_estimate=pl.CostEstimate(flops=0, bytes_accessed=0, transcendentals=0),
    )(rows, cols, count, tiles)


def fill_table(layout, mine, notes, table):
    cap = layout.cap
    keys = 16 * cap
    _, yc, _, zs = whereabouts()
    for j in range(4):
        for flip, asked in enumerate(notes, 1):
            for r in range(cap):
                table[layout.pack(j, flip) + r] = asked[0, (zs[j] * 4 + yc) * cap + r].astype(jnp.int32)
    for i, (j, flip) in enumerate(EARLY + LATE):
        for r in range(cap):
            key = (zs[j] * 4 + (yc ^ flip)) * cap + r
            at = layout.entry(i * cap + r)
            table[at] = mine[key]
            table[at + 1] = mine[keys + key]
            table[at + 2] = mine[2 * keys + key]


def start_kernel(layout, mine, note1, note2, note3, own, first, table, out2, out3):
    fill_table(layout, mine, (note1, note2, note3), table)
    other_y_kernel(layout, (0, 1), table, own, first, out2, out3)


def start(layout, mine, notes, own, first):
    _, tile, repl = own.shape
    packs = jax.ShapeDtypeStruct((2 * layout.cap, tile, repl), jnp.bfloat16)
    return pl.pallas_call(
        functools.partial(start_kernel, layout),
        out_shape=(jax.ShapeDtypeStruct((layout.size,), jnp.int32), packs, packs),
        in_specs=[SMEM] * 4 + [VMEM] * 2,
        out_specs=(SMEM, VMEM, VMEM),
        compiler_params=params(),
        cost_estimate=pl.CostEstimate(flops=0, bytes_accessed=0, transcendentals=0),
    )(mine, *notes, own, first)


def copy_asked(layout, table, j, flip, shard, out, first=0):
    at = layout.pack(j, flip)
    for r in range(layout.cap):
        out[first + r] = shard[table[at + r]]


def copy_part(cap, source, part, out, first):
    for r in range(cap):
        out[first + r] = source[part * cap + r]


def by_place(mid, out, use):
    inner = whereabouts()[2]
    pl.when(inner)(lambda: use(mid))
    pl.when(jnp.logical_not(inner))(lambda: use(out))


def other_y_kernel(layout, js, table, *refs):
    shards, outs = refs[:-2], refs[-2:]
    for i, (j, shard) in enumerate(zip(js, shards)):
        for flip in (2, 3):
            copy_asked(layout, table, j, flip, shard, outs[flip - 2], i * layout.cap)


def second_kernel(layout, table, own, first, second, out2, out3, core):
    other_y_kernel(layout, (2,), table, second, out2, out3)
    for j, shard in enumerate((own, first, second)):
        copy_asked(layout, table, j, 1, shard, core, j * layout.cap)


def third_kernel(layout, table, mid, out, out2, out3, core):
    def use(shard):
        other_y_kernel(layout, (3,), table, shard, out2, out3)
        copy_asked(layout, table, 3, 1, shard, core)

    by_place(mid, out, use)


def pack(kernel, sizes, table, arrays):
    _, tile, repl = arrays[0].shape
    return pl.pallas_call(
        kernel,
        out_shape=[jax.ShapeDtypeStruct((size, tile, repl), jnp.bfloat16) for size in sizes],
        in_specs=[SMEM] + [VMEM] * len(arrays),
        out_specs=[VMEM] * len(sizes),
        compiler_params=params(),
        cost_estimate=pl.CostEstimate(flops=0, bytes_accessed=0, transcendentals=0),
    )(table, *arrays)


def multiply(layout, table, tiles, blocks, first, field):
    prods = [
        jnp.dot(tiles[table[layout.entry(first + i)]], block, preferred_element_type=jnp.float32)
        for i, block in enumerate(blocks)
    ]
    for i, prod in enumerate(prods):
        field[table[layout.entry(first + i) + 1]] += prod


def take_own(layout, table, entry, shard, xbuf, place):
    for r in range(layout.cap):
        xbuf[place + r] = shard[table[layout.entry(entry + r) + 2]]


def early_kernel(layout, parts, table, tiles, *refs):
    cap = layout.cap
    field, xbuf = refs[-2:]
    core = refs[3]
    for j in range(3):
        base = 4 * cap * j
        take_own(layout, table, base, refs[j], xbuf, base)
        copy_part(cap, core, j, xbuf, base + cap)
        ref, part = parts[j]
        copy_part(cap, refs[ref], part, xbuf, base + 2 * cap)
        copy_part(cap, refs[ref + 1], part, xbuf, base + 3 * cap)
    field[...] = jnp.zeros_like(field)

    @pl.loop(0, 12 * cap // GROUP)
    def _(g):
        multiply(layout, table, tiles, [xbuf[g * GROUP + i] for i in range(GROUP)], g * GROUP, field)


def early(layout, parts, table, tiles, arrays):
    tile = tiles.shape[1]
    blocks, _, repl = arrays[0].shape
    return pl.pallas_call(
        functools.partial(early_kernel, layout, parts),
        out_shape=jax.ShapeDtypeStruct((blocks + 1, tile, repl), jnp.float32),
        in_specs=[SMEM] + [VMEM] * (1 + len(arrays)),
        out_specs=VMEM,
        scratch_shapes=[pltpu.VMEM((12 * layout.cap, tile, repl), jnp.bfloat16)],
        compiler_params=params(),
        cost_estimate=pl.CostEstimate(flops=0, bytes_accessed=0, transcendentals=0),
    )(table, tiles, *arrays)


def late_kernel(layout, last, table, scalars, tiles, mid, out, core, got2, got3, field, xpos, ymom, *refs):
    outs, (xbuf, acc) = refs[:-2], refs[-2:]
    xout, yout = outs[:2]
    blocks = xpos.shape[0]
    cap = layout.cap
    by_place(mid, out, lambda shard: take_own(layout, table, 12 * cap, shard, xbuf, 0))
    acc[...] = field[...]
    blocks_in = [ref[r] for ref in (xbuf, core, got2, got3) for r in range(cap)]
    for first in range(0, 4 * cap, GROUP):
        multiply(layout, table, tiles, blocks_in[first : first + GROUP], 12 * cap + first, acc)
    total = jnp.zeros((1, xpos.shape[2]), jnp.float32)
    for b in range(blocks):
        x, h = xpos[b], acc[b]
        if last:
            total += jnp.sum(x * h, axis=0, keepdims=True)
        x, y = update(scalars[0], scalars[1], h, x, ymom[b])
        xout[b] = x
        yout[b] = y
        if not last:
            outs[2][b] = x.astype(jnp.bfloat16)
    if last:
        outs[2][...] = -0.5 * total
    else:
        other_y_kernel(layout, (0,), table, *outs[2:])


def late(layout, last, table, scalars, tiles, sources, field, xpos, ymom):
    tile = tiles.shape[1]
    blocks, _, repl = xpos.shape
    entries = 4 * layout.cap
    state = jax.ShapeDtypeStruct(xpos.shape, jnp.float32)
    if last:
        extra = (jax.ShapeDtypeStruct((1, repl), jnp.float32),)
    else:
        out = jax.ShapeDtypeStruct((layout.cap, tile, repl), jnp.bfloat16)
        extra = (jax.ShapeDtypeStruct(xpos.shape, jnp.bfloat16), out, out)
    return pl.pallas_call(
        functools.partial(late_kernel, layout, last),
        out_shape=(state, state) + extra,
        in_specs=[SMEM, SMEM] + [VMEM] * (1 + len(sources) + 3),
        out_specs=(VMEM,) * (2 + len(extra)),
        scratch_shapes=[
            pltpu.VMEM((layout.cap, tile, repl), jnp.bfloat16),
            pltpu.VMEM((blocks + 1, tile, repl), jnp.float32),
        ],
        compiler_params=params(),
        cost_estimate=pl.CostEstimate(
            flops=2 * entries * tile * tile * repl,
            bytes_accessed=entries * tile * (tile + repl) * 2 + 20 * xpos.size,
            transcendentals=0,
        ),
    )(table, scalars, tiles, *sources, field, xpos, ymom)


def along_z(pairs, value):
    return lax.ppermute(value, "row", [(a * 4 + i, b * 4 + i) for a, b in pairs for i in range(4)])


def across(flip, value):
    return lax.ppermute(value, "row", [(i, i ^ flip) for i in range(16)])


def row_sum(part):
    devices = lax.axis_size("row")
    spread = jnp.broadcast_to(part, (devices,) + part.shape[1:])
    return jnp.sum(lax.all_to_all(spread, "row", split_axis=0, concat_axis=0, tiled=True), axis=0, keepdims=True)


def body_16(tiles, tile_rows, tile_cols, counts, positions, momenta):
    slots, tile, _ = tiles.shape
    repl = positions.shape[1]
    blocks = positions.shape[0] // tile
    cap = (slots + 15) // 16
    order = blocks * tile * 16
    layout = Layout(cap)

    def other_y(js, shards):
        kernel = functools.partial(other_y_kernel, layout, js)
        return pack(kernel, [len(js) * cap] * 2, table, shards)

    def to_other_y(packs):
        return [across(2, packs[0]), across(3, packs[1])]

    xpos = positions.reshape(blocks, tile, repl)
    ymom = momenta.reshape(blocks, tile, repl)
    own0 = xpos.astype(jnp.bfloat16)
    mine, note = plan(layout, blocks, tile_rows, tile_cols, counts, tiles)
    notes = [across(flip, note) for flip in (1, 2, 3)]
    packs0 = None
    for step in range(STEPS):
        last = step == STEPS - 1
        own1 = along_z(FIRST, own0)
        own2 = along_z(SECOND, own0)
        mid = along_z(MIDDLE, own0)
        if step == 0:
            own1, notes = lax.optimization_barrier((own1, notes))
            out = along_z(OUTWARD, own1)
            table, *packs01 = start(layout, mine, notes, own0, own1)
            got1 = to_other_y(packs01)
            own2, got1, mid, out = lax.optimization_barrier((own2, got1, mid, out))
            parts = ((4, 0), (4, 1), (6, 0))
            got = got1
        else:
            got0 = to_other_y(packs0)
            own1, got0 = lax.optimization_barrier((own1, got0))
            out = along_z(OUTWARD, own1)
            got1 = to_other_y(other_y((1,), [own1]))
            own2, got1 = lax.optimization_barrier((own2, got1))
            parts = ((4, 0), (6, 0), (8, 0))
            got = got0 + got1
        packs2 = pack(functools.partial(second_kernel, layout), [cap, cap, 3 * cap], table, [own0, own1, own2])
        got = got + to_other_y(packs2)
        core = across(1, packs2[2])
        if step == 0:
            notes, core = lax.optimization_barrier((notes, core))
            plane = note + notes[0] + notes[1] + notes[2]
            half = plane + across(4, plane)
        packs3 = pack(functools.partial(third_kernel, layout), [cap] * 3, table, [mid, out])
        far = [mid, out, across(1, packs3[2])] + to_other_y(packs3)
        field = early(layout, parts, table, tiles, [own0, own1, own2, core] + got)
        if step == 0:
            total = (half + across(8, half))[0, SUM_AT]
            coeff = 0.7 * jnp.sqrt((order - 1) / total)
        scalars = jnp.stack([jnp.float32(0.4 - 0.1 * step), coeff])
        outs = late(layout, last, table, scalars, tiles, far, field, xpos, ymom)
        xpos, ymom = outs[0], outs[1]
        if not last:
            own0, packs0 = outs[2], outs[3:]
    energy = row_sum(outs[2])
    return (xpos.reshape(positions.shape), ymom.reshape(momenta.shape), energy.reshape(repl))


def gathered_kernel(last, rows, cols, count, scalars, tiles, gathered, xpos, ymom, xout, yout, extra, xbuf, field, xsem):
    tile = xbuf.shape[1]
    used = count[0]

    def block_copy(s):
        return pltpu.make_async_copy(gathered.at[cols[s]], xbuf.at[s], xsem.at[s])

    @pl.loop(0, used)
    def _(s):
        block_copy(s).start()

    field[...] = jnp.zeros_like(field)

    @pl.loop(0, used)
    def _(s):
        block_copy(s).wait()
        here = pl.ds(pl.multiple_of(rows[s] * tile, tile), tile)
        field[here, :] += jnp.dot(tiles[s], xbuf[s], preferred_element_type=jnp.float32)

    x, h = xpos[...], field[...]
    if last:
        extra[...] = -0.5 * jnp.sum(x * h, axis=0, keepdims=True)
    x, y = update(scalars[0], scalars[1], h, x, ymom[...])
    xout[...] = x
    yout[...] = y
    if not last:
        extra[...] = x.astype(jnp.bfloat16)


def body_any(tiles, tile_rows, tile_cols, counts, positions, momenta):
    slots, tile, _ = tiles.shape
    order, repl = positions.shape
    devices = lax.axis_size("row")
    state = jax.ShapeDtypeStruct(positions.shape, jnp.float32)
    total = jnp.sum(lax.psum(squares(counts, tiles), "row"))
    coeff = 0.7 * jnp.sqrt((order * devices - 1) / total)
    xpos, ymom, extra = positions, momenta, positions.astype(jnp.bfloat16)
    for step in range(STEPS):
        last = step == STEPS - 1
        gathered = lax.all_gather(extra, "row", tiled=True).reshape(-1, tile, repl)
        scalars = jnp.stack([jnp.float32(0.4 - 0.1 * step), coeff])
        xpos, ymom, extra = pl.pallas_call(
            functools.partial(gathered_kernel, last),
            out_shape=(
                state,
                state,
                jax.ShapeDtypeStruct((1, repl), jnp.float32) if last else jax.ShapeDtypeStruct(state.shape, jnp.bfloat16),
            ),
            in_specs=[SMEM] * 4 + [VMEM, ANY, VMEM, VMEM],
            out_specs=(VMEM,) * 3,
            scratch_shapes=[
                pltpu.VMEM((slots, tile, repl), jnp.bfloat16),
                pltpu.VMEM(positions.shape, jnp.float32),
                pltpu.SemaphoreType.DMA((slots,)),
            ],
            compiler_params=params(),
        )(tile_rows, tile_cols, counts, scalars, tiles, gathered, xpos, ymom)
    return (xpos, ymom, lax.psum(extra, "row").reshape(repl))


def solution(mesh):
    in_specs = (
        P(("groups", "row"), None, None),
        P(("groups", "row")),
        P(("groups", "row")),
        P(("groups", "row")),
        P(("groups", "row"), None),
        P(("groups", "row"), None),
    )
    out_specs = (P(("groups", "row"), None), P(("groups", "row"), None), P("groups"))

    def body(tiles, *args):
        slots = tiles.shape[0]
        by_hand = mesh.shape["row"] == 16 and slots % GROUP == 0 and slots <= 96
        return (body_16 if by_hand else body_any)(tiles, *args)

    return jax.shard_map(body, mesh=mesh, in_specs=in_specs, out_specs=out_specs, check_vma=False)
```

```python
import functools

import jax
import jax.numpy as jnp
from jax import lax
from jax.experimental import pallas as pl
from jax.experimental.pallas import tpu as pltpu
from jax.sharding import PartitionSpec as P

STEPS = 4
GROUP = 6
LANES = 128
SUM_AT = LANES - 1
LIMIT = 16 * 2**20

SMEM = pl.BlockSpec(memory_space=pltpu.SMEM)
VMEM = pl.BlockSpec(memory_space=pltpu.VMEM)
ANY = pl.BlockSpec(memory_space=pl.ANY)


def params(limit=LIMIT):
    return pltpu.CompilerParams(vmem_limit_bytes=limit)


def squares_kernel(count, tiles, out):
    tile = tiles.shape[1]

    def add(s, acc):
        t = tiles[s].astype(jnp.float32)
        return acc + jnp.sum((t * t).reshape(tile // 8, 8, tile), axis=0)

    acc = lax.fori_loop(0, count[0], add, jnp.zeros((8, tile), jnp.float32))
    acc = jnp.sum(acc, axis=0, keepdims=True)
    out[...] = sum(acc[:, i : i + 128] for i in range(0, tile, 128))


def squares(count, tiles):
    return pl.pallas_call(
        squares_kernel,
        out_shape=jax.ShapeDtypeStruct((1, 128), jnp.float32),
        in_specs=[SMEM, VMEM],
        out_specs=VMEM,
        compiler_params=params(),
        cost_estimate=pl.CostEstimate(flops=2 * tiles.size, bytes_accessed=2 * tiles.size, transcendentals=0),
    )(count, tiles)


def update(pump, coeff, h, x, y):
    y = y + 0.5 * (-(x * x + pump) * x + coeff * h)
    return x + 0.5 * y, y


FIRST = ((0, 2), (3, 1), (1, 0), (2, 3))
SECOND = ((0, 1), (3, 2), (1, 3), (2, 0))
OUTWARD = ((1, 0), (2, 3))
MIDDLE = ((1, 2), (2, 1))


class Layout:
    def __init__(self, cap):
        self.cap = cap
        self.packs = 0
        self.entries = 12 * cap
        self.size = 12 * cap + 3 * 16 * cap

    def pack(self, j, flip):
        return self.packs + (j * 3 + flip - 1) * self.cap

    def entry(self, i):
        return self.entries + 3 * i


def whereabouts():
    me = lax.axis_index("row")
    z, yc = lax.div(me, 4), lax.rem(me, 4)
    inner = (z == 1) | (z == 2)
    near, skip = z ^ 1, z ^ 2
    return z, yc, inner, (z, jnp.where(inner, skip, near), jnp.where(inner, near, skip), z ^ 3)


EARLY = tuple((j, flip) for j in range(3) for flip in range(4)) + ((3, 0), (3, 1))
LATE = ((3, 2), (3, 3))


def plan_kernel(layout, blocks, rows, cols, count, tiles, mine, note, seen, buffer, sems):
    cap = layout.cap
    keys = 16 * cap
    slots, tile, _ = buffer.shape
    chunks = [pl.ds(first, GROUP) for first in range(0, slots, GROUP)]
    copies = [pltpu.make_async_copy(tiles.at[c], buffer.at[c], sems.at[i]) for i, c in enumerate(chunks)]
    for copy in copies:
        copy.start()

    @pl.loop(0, 16)
    def _(d):
        seen[d] = 0

    @pl.loop(0, keys)
    def _(k):
        mine[k] = 0
        mine[keys + k] = blocks
        mine[2 * keys + k] = 0

    @pl.loop(0, count[0])
    def _(s):
        source = lax.div(cols[s], blocks)
        rank = seen[source]
        seen[source] = rank + 1
        key = source * cap + jnp.minimum(rank, cap - 1)
        mine[key] = s
        mine[keys + key] = rows[s]
        mine[2 * keys + key] = lax.rem(cols[s], blocks)

    lane = lax.broadcasted_iota(jnp.int32, note.shape, 1)
    wants = jnp.zeros(note.shape, jnp.int32)
    for k in range(keys):
        wants = jnp.where(lane == k, mine[2 * keys + k], wants)

    def add(s, acc):
        t = buffer[s].astype(jnp.float32)
        return acc + jnp.sum((t * t).reshape(tile // 8, 8, tile), axis=0)

    acc = jnp.zeros((8, tile), jnp.float32)
    for i, copy in enumerate(copies):
        copy.wait()
        acc = lax.fori_loop(i * GROUP, jnp.clip(count[0], i * GROUP, (i + 1) * GROUP), add, acc)
    note[...] = jnp.where(lane == SUM_AT, jnp.sum(acc), wants.astype(jnp.float32))


def plan(layout, blocks, rows, cols, count, tiles):
    return pl.pallas_call(
        functools.partial(plan_kernel, layout, blocks),
        out_shape=(
            jax.ShapeDtypeStruct((3 * 16 * layout.cap,), jnp.int32),
            jax.ShapeDtypeStruct((1, LANES), jnp.float32),
        ),
        in_specs=[SMEM] * 3 + [ANY],
        out_specs=(SMEM, VMEM),
        scratch_shapes=[
            pltpu.SMEM((16,), jnp.int32),
            pltpu.VMEM(tiles.shape, tiles.dtype),
            pltpu.SemaphoreType.DMA((tiles.shape[0] // GROUP,)),
        ],
        compiler_params=params(59 * 2**20),
        cost_estimate=pl.CostEstimate(flops=0, bytes_accessed=0, transcendentals=0),
    )(rows, cols, count, tiles)


def fill_table(layout, mine, notes, table):
    cap = layout.cap
    keys = 16 * cap
    _, yc, _, zs = whereabouts()
    for j in range(4):
        for flip, asked in enumerate(notes, 1):
            for r in range(cap):
                table[layout.pack(j, flip) + r] = asked[0, (zs[j] * 4 + yc) * cap + r].astype(jnp.int32)
    for i, (j, flip) in enumerate(EARLY + LATE):
        for r in range(cap):
            key = (zs[j] * 4 + (yc ^ flip)) * cap + r
            at = layout.entry(i * cap + r)
            table[at] = mine[key]
            table[at + 1] = mine[keys + key]
            table[at + 2] = mine[2 * keys + key]


def start_kernel(layout, mine, note1, note2, note3, own, first, table, out2, out3):
    fill_table(layout, mine, (note1, note2, note3), table)
    other_y_kernel(layout, (0, 1), table, own, first, out2, out3)


def start(layout, mine, notes, own, first):
    _, tile, repl = own.shape
    packs = jax.ShapeDtypeStruct((2 * layout.cap, tile, repl), jnp.bfloat16)
    return pl.pallas_call(
        functools.partial(start_kernel, layout),
        out_shape=(jax.ShapeDtypeStruct((layout.size,), jnp.int32), packs, packs),
        in_specs=[SMEM] * 4 + [VMEM] * 2,
        out_specs=(SMEM, VMEM, VMEM),
        compiler_params=params(),
        cost_estimate=pl.CostEstimate(flops=0, bytes_accessed=0, transcendentals=0),
    )(mine, *notes, own, first)


def copy_asked(layout, table, j, flip, shard, out, first=0):
    at = layout.pack(j, flip)
    for r in range(layout.cap):
        out[first + r] = shard[table[at + r]]


def copy_part(cap, source, part, out, first):
    for r in range(cap):
        out[first + r] = source[part * cap + r]


def by_place(mid, out, use):
    inner = whereabouts()[2]
    pl.when(inner)(lambda: use(mid))
    pl.when(jnp.logical_not(inner))(lambda: use(out))


def other_y_kernel(layout, js, table, *refs):
    shards, outs = refs[:-2], refs[-2:]
    for i, (j, shard) in enumerate(zip(js, shards)):
        for flip in (2, 3):
            copy_asked(layout, table, j, flip, shard, outs[flip - 2], i * layout.cap)


def second_kernel(layout, table, own, first, second, out2, out3, core):
    other_y_kernel(layout, (2,), table, second, out2, out3)
    for j, shard in enumerate((own, first, second)):
        copy_asked(layout, table, j, 1, shard, core, j * layout.cap)


def third_kernel(layout, table, mid, out, out2, out3, core):
    def use(shard):
        other_y_kernel(layout, (3,), table, shard, out2, out3)
        copy_asked(layout, table, 3, 1, shard, core)

    by_place(mid, out, use)


def pack(kernel, sizes, table, arrays):
    _, tile, repl = arrays[0].shape
    return pl.pallas_call(
        kernel,
        out_shape=[jax.ShapeDtypeStruct((size, tile, repl), jnp.bfloat16) for size in sizes],
        in_specs=[SMEM] + [VMEM] * len(arrays),
        out_specs=[VMEM] * len(sizes),
        compiler_params=params(),
        cost_estimate=pl.CostEstimate(flops=0, bytes_accessed=0, transcendentals=0),
    )(table, *arrays)


def multiply(layout, table, tiles, blocks, first, field):
    prods = [
        jnp.dot(tiles[table[layout.entry(first + i)]], block, preferred_element_type=jnp.float32)
        for i, block in enumerate(blocks)
    ]
    for i, prod in enumerate(prods):
        field[table[layout.entry(first + i) + 1]] += prod


def take_own(layout, table, entry, shard, xbuf, place):
    for r in range(layout.cap):
        xbuf[place + r] = shard[table[layout.entry(entry + r) + 2]]


def early_kernel(layout, parts, table, tiles, own, first, second, mid, out, core, core3, *refs):
    cap = layout.cap
    field, xbuf = refs[-2:]
    for j, shard in enumerate((own, first, second)):
        base = 4 * cap * j
        take_own(layout, table, base, shard, xbuf, base)
        copy_part(cap, core, j, xbuf, base + cap)
        ref, part = parts[j]
        copy_part(cap, refs[ref], part, xbuf, base + 2 * cap)
        copy_part(cap, refs[ref + 1], part, xbuf, base + 3 * cap)
    by_place(mid, out, lambda shard: take_own(layout, table, 12 * cap, shard, xbuf, 12 * cap))
    copy_part(cap, core3, 0, xbuf, 13 * cap)
    field[...] = jnp.zeros_like(field)

    @pl.loop(0, len(EARLY) * cap // GROUP)
    def _(g):
        multiply(layout, table, tiles, [xbuf[g * GROUP + i] for i in range(GROUP)], g * GROUP, field)


def early(layout, parts, table, tiles, arrays):
    tile = tiles.shape[1]
    blocks, _, repl = arrays[0].shape
    return pl.pallas_call(
        functools.partial(early_kernel, layout, parts),
        out_shape=jax.ShapeDtypeStruct((blocks + 1, tile, repl), jnp.float32),
        in_specs=[SMEM] + [VMEM] * (1 + len(arrays)),
        out_specs=VMEM,
        scratch_shapes=[pltpu.VMEM((len(EARLY) * layout.cap, tile, repl), jnp.bfloat16)],
        compiler_params=params(),
        cost_estimate=pl.CostEstimate(flops=0, bytes_accessed=0, transcendentals=0),
    )(table, tiles, *arrays)


def late_kernel(layout, last, table, scalars, tiles, got2, got3, field, xpos, ymom, *refs):
    cap = layout.cap
    blocks, _, repl = xpos.shape
    outs, acc = (refs[:3], refs[3]) if last else (refs[:5], refs[5])
    xout, yout = outs[:2]
    acc[...] = field[...]
    multiply(layout, table, tiles, [ref[r] for ref in (got2, got3) for r in range(cap)], len(EARLY) * cap, acc)
    if last:
        xnew, ynew, sems = refs[4:]
    else:
        xnew, ynew = xout, yout
    total = jnp.zeros((1, repl), jnp.float32)
    copies = []
    for b in range(blocks):
        x, h = xpos[b], acc[b]
        if last:
            total += jnp.sum(x * h, axis=0, keepdims=True)
        x, y = update(scalars[0], scalars[1], h, x, ymom[b])
        xnew[b] = x
        ynew[b] = y
        if last:
            copies.append(pltpu.make_async_copy(xnew.at[b], xout.at[b], sems.at[0, b]))
            copies.append(pltpu.make_async_copy(ynew.at[b], yout.at[b], sems.at[1, b]))
            copies[-2].start()
            copies[-1].start()
        else:
            outs[2][b] = x.astype(jnp.bfloat16)
    if last:
        outs[2][...] = -0.5 * total
        for copy in copies:
            copy.wait()
    else:
        other_y_kernel(layout, (0,), table, *outs[2:])


def late(layout, last, table, scalars, tiles, sources, field, xpos, ymom):
    tile = tiles.shape[1]
    blocks, _, repl = xpos.shape
    entries = len(LATE) * layout.cap
    state = jax.ShapeDtypeStruct(xpos.shape, jnp.float32)
    scratch = [pltpu.VMEM((blocks + 1, tile, repl), jnp.float32)]
    if last:
        extra = (jax.ShapeDtypeStruct((1, repl), jnp.float32),)
        scratch += [pltpu.VMEM(xpos.shape, jnp.float32)] * 2 + [pltpu.SemaphoreType.DMA((2, blocks))]
    else:
        out = jax.ShapeDtypeStruct((layout.cap, tile, repl), jnp.bfloat16)
        extra = (jax.ShapeDtypeStruct(xpos.shape, jnp.bfloat16), out, out)
    return pl.pallas_call(
        functools.partial(late_kernel, layout, last),
        out_shape=(state, state) + extra,
        in_specs=[SMEM, SMEM] + [VMEM] * (1 + len(sources) + 3),
        out_specs=((ANY, ANY) if last else (VMEM, VMEM)) + (VMEM,) * len(extra),
        scratch_shapes=scratch,
        compiler_params=params(),
        cost_estimate=pl.CostEstimate(
            flops=2 * entries * tile * tile * repl,
            bytes_accessed=entries * tile * (tile + repl) * 2 + 20 * xpos.size,
            transcendentals=0,
        ),
    )(table, scalars, tiles, *sources, field, xpos, ymom)


def along_z(pairs, value):
    return lax.ppermute(value, "row", [(a * 4 + i, b * 4 + i) for a, b in pairs for i in range(4)])


def across(flip, value):
    return lax.ppermute(value, "row", [(i, i ^ flip) for i in range(16)])


def row_sum(part):
    devices = lax.axis_size("row")
    spread = jnp.broadcast_to(part, (devices,) + part.shape[1:])
    return jnp.sum(lax.all_to_all(spread, "row", split_axis=0, concat_axis=0, tiled=True), axis=0, keepdims=True)


def body_16(tiles, tile_rows, tile_cols, counts, positions, momenta):
    slots, tile, _ = tiles.shape
    repl = positions.shape[1]
    blocks = positions.shape[0] // tile
    cap = (slots + 15) // 16
    order = blocks * tile * 16
    layout = Layout(cap)

    def other_y(js, shards):
        kernel = functools.partial(other_y_kernel, layout, js)
        return pack(kernel, [len(js) * cap] * 2, table, shards)

    def to_other_y(packs):
        return [across(2, packs[0]), across(3, packs[1])]

    xpos = positions.reshape(blocks, tile, repl)
    ymom = momenta.reshape(blocks, tile, repl)
    own0 = xpos.astype(jnp.bfloat16)
    mine, note = plan(layout, blocks, tile_rows, tile_cols, counts, tiles)
    notes = [across(flip, note) for flip in (1, 2, 3)]
    packs0 = None
    for step in range(STEPS):
        last = step == STEPS - 1
        own1 = along_z(FIRST, own0)
        own2 = along_z(SECOND, own0)
        mid = along_z(MIDDLE, own0)
        if step == 0:
            own1, notes = lax.optimization_barrier((own1, notes))
            out = along_z(OUTWARD, own1)
            table, *packs01 = start(layout, mine, notes, own0, own1)
            got1 = to_other_y(packs01)
            plane = note + notes[0] + notes[1] + notes[2]
            half = across(4, plane)
            own2, got1, half = lax.optimization_barrier((own2, got1, half))
            half = plane + half
            parts = ((0, 0), (0, 1), (2, 0))
            got = got1
        else:
            got0 = to_other_y(packs0)
            own1, got0 = lax.optimization_barrier((own1, got0))
            out = along_z(OUTWARD, own1)
            got1 = to_other_y(other_y((1,), [own1]))
            own2, got1 = lax.optimization_barrier((own2, got1))
            parts = ((0, 0), (2, 0), (4, 0))
            got = got0 + got1
        packs2 = pack(functools.partial(second_kernel, layout), [cap, cap, 3 * cap], table, [own0, own1, own2])
        got2 = to_other_y(packs2)
        core = across(1, packs2[2])
        packs3 = pack(functools.partial(third_kernel, layout), [cap] * 3, table, [mid, out])
        core3 = across(1, packs3[2])
        got3 = to_other_y(packs3)
        field = early(layout, parts, table, tiles, [own0, own1, own2, mid, out, core, core3] + got + got2)
        if step == 0:
            total = (half + across(8, half))[0, SUM_AT]
            coeff = 0.7 * jnp.sqrt((order - 1) / total)
        scalars = jnp.stack([jnp.float32(0.4 - 0.1 * step), coeff])
        outs = late(layout, last, table, scalars, tiles, got3, field, xpos, ymom)
        xpos, ymom = outs[0], outs[1]
        if not last:
            own0, packs0 = outs[2], outs[3:]
    energy = row_sum(outs[2])
    return (xpos.reshape(positions.shape), ymom.reshape(momenta.shape), energy.reshape(repl))


def gathered_kernel(last, rows, cols, count, scalars, tiles, gathered, xpos, ymom, xout, yout, extra, xbuf, field, xsem):
    tile = xbuf.shape[1]
    used = count[0]

    def block_copy(s):
        return pltpu.make_async_copy(gathered.at[cols[s]], xbuf.at[s], xsem.at[s])

    @pl.loop(0, used)
    def _(s):
        block_copy(s).start()

    field[...] = jnp.zeros_like(field)

    @pl.loop(0, used)
    def _(s):
        block_copy(s).wait()
        here = pl.ds(pl.multiple_of(rows[s] * tile, tile), tile)
        field[here, :] += jnp.dot(tiles[s], xbuf[s], preferred_element_type=jnp.float32)

    x, h = xpos[...], field[...]
    if last:
        extra[...] = -0.5 * jnp.sum(x * h, axis=0, keepdims=True)
    x, y = update(scalars[0], scalars[1], h, x, ymom[...])
    xout[...] = x
    yout[...] = y
    if not last:
        extra[...] = x.astype(jnp.bfloat16)


def body_any(tiles, tile_rows, tile_cols, counts, positions, momenta):
    slots, tile, _ = tiles.shape
    order, repl = positions.shape
    devices = lax.axis_size("row")
    state = jax.ShapeDtypeStruct(positions.shape, jnp.float32)
    total = jnp.sum(lax.psum(squares(counts, tiles), "row"))
    coeff = 0.7 * jnp.sqrt((order * devices - 1) / total)
    xpos, ymom, extra = positions, momenta, positions.astype(jnp.bfloat16)
    for step in range(STEPS):
        last = step == STEPS - 1
        gathered = lax.all_gather(extra, "row", tiled=True).reshape(-1, tile, repl)
        scalars = jnp.stack([jnp.float32(0.4 - 0.1 * step), coeff])
        xpos, ymom, extra = pl.pallas_call(
            functools.partial(gathered_kernel, last),
            out_shape=(
                state,
                state,
                jax.ShapeDtypeStruct((1, repl), jnp.float32) if last else jax.ShapeDtypeStruct(state.shape, jnp.bfloat16),
            ),
            in_specs=[SMEM] * 4 + [VMEM, ANY, VMEM, VMEM],
            out_specs=(VMEM,) * 3,
            scratch_shapes=[
                pltpu.VMEM((slots, tile, repl), jnp.bfloat16),
                pltpu.VMEM(positions.shape, jnp.float32),
                pltpu.SemaphoreType.DMA((slots,)),
            ],
            compiler_params=params(),
        )(tile_rows, tile_cols, counts, scalars, tiles, gathered, xpos, ymom)
    return (xpos, ymom, lax.psum(extra, "row").reshape(repl))


def solution(mesh):
    in_specs = (
        P(("groups", "row"), None, None),
        P(("groups", "row")),
        P(("groups", "row")),
        P(("groups", "row")),
        P(("groups", "row"), None),
        P(("groups", "row"), None),
    )
    out_specs = (P(("groups", "row"), None), P(("groups", "row"), None), P("groups"))

    def body(tiles, *args):
        slots = tiles.shape[0]
        by_hand = mesh.shape["row"] == 16 and slots % GROUP == 0 and slots <= 96
        return (body_16 if by_hand else body_any)(tiles, *args)

    return jax.shard_map(body, mesh=mesh, in_specs=in_specs, out_specs=out_specs, check_vma=False)
```

```python
import functools

import jax
import jax.numpy as jnp
from jax import lax
from jax.experimental import pallas as pl
from jax.experimental.pallas import tpu as pltpu
from jax.sharding import PartitionSpec as P

STEPS = 4
GROUP = 6
LANES = 128
SUM_AT = LANES - 1
LIMIT = 16 * 2**20

SMEM = pl.BlockSpec(memory_space=pltpu.SMEM)
VMEM = pl.BlockSpec(memory_space=pltpu.VMEM)
ANY = pl.BlockSpec(memory_space=pl.ANY)


def params(limit=LIMIT):
    return pltpu.CompilerParams(vmem_limit_bytes=limit)


def squares_kernel(count, tiles, out):
    tile = tiles.shape[1]

    def add(s, acc):
        t = tiles[s].astype(jnp.float32)
        return acc + jnp.sum((t * t).reshape(tile // 8, 8, tile), axis=0)

    acc = lax.fori_loop(0, count[0], add, jnp.zeros((8, tile), jnp.float32))
    acc = jnp.sum(acc, axis=0, keepdims=True)
    out[...] = sum(acc[:, i : i + 128] for i in range(0, tile, 128))


def squares(count, tiles):
    return pl.pallas_call(
        squares_kernel,
        out_shape=jax.ShapeDtypeStruct((1, 128), jnp.float32),
        in_specs=[SMEM, VMEM],
        out_specs=VMEM,
        compiler_params=params(),
        cost_estimate=pl.CostEstimate(flops=2 * tiles.size, bytes_accessed=2 * tiles.size, transcendentals=0),
    )(count, tiles)


def update(pump, coeff, h, x, y):
    y = y + 0.5 * (-(x * x + pump) * x + coeff * h)
    return x + 0.5 * y, y


FIRST = ((0, 2), (3, 1), (1, 0), (2, 3))
SECOND = ((0, 1), (3, 2), (1, 3), (2, 0))
OUTWARD = ((1, 0), (2, 3))
MIDDLE = ((1, 2), (2, 1))


class Layout:
    def __init__(self, cap):
        self.cap = cap
        self.packs = 0
        self.entries = 12 * cap
        self.size = 12 * cap + 3 * 16 * cap

    def pack(self, j, flip):
        return self.packs + (j * 3 + flip - 1) * self.cap

    def entry(self, i):
        return self.entries + 3 * i


def whereabouts():
    me = lax.axis_index("row")
    z, yc = lax.div(me, 4), lax.rem(me, 4)
    inner = (z == 1) | (z == 2)
    near, skip = z ^ 1, z ^ 2
    return z, yc, inner, (z, jnp.where(inner, skip, near), jnp.where(inner, near, skip), z ^ 3)


EARLY = tuple((j, flip) for j in range(3) for flip in range(4)) + ((3, 0), (3, 1))
LATE = ((3, 2), (3, 3))


def plan_kernel(layout, blocks, rows, cols, count, tiles, mine, note, seen, buffer, sems):
    cap = layout.cap
    keys = 16 * cap
    slots, tile, _ = buffer.shape
    chunks = [pl.ds(first, GROUP) for first in range(0, slots, GROUP)]
    copies = [pltpu.make_async_copy(tiles.at[c], buffer.at[c], sems.at[i]) for i, c in enumerate(chunks)]
    for copy in copies:
        copy.start()

    @pl.loop(0, 16)
    def _(d):
        seen[d] = 0

    @pl.loop(0, keys)
    def _(k):
        mine[k] = 0
        mine[keys + k] = blocks
        mine[2 * keys + k] = 0

    @pl.loop(0, count[0])
    def _(s):
        source = lax.div(cols[s], blocks)
        rank = seen[source]
        seen[source] = rank + 1
        key = source * cap + jnp.minimum(rank, cap - 1)
        mine[key] = s
        mine[keys + key] = rows[s]
        mine[2 * keys + key] = lax.rem(cols[s], blocks)

    lane = lax.broadcasted_iota(jnp.int32, note.shape, 1)
    wants = jnp.zeros(note.shape, jnp.int32)
    for k in range(keys):
        wants = jnp.where(lane == k, mine[2 * keys + k], wants)

    def add(s, acc):
        t = buffer[s].astype(jnp.float32)
        return acc + jnp.sum((t * t).reshape(tile // 8, 8, tile), axis=0)

    acc = jnp.zeros((8, tile), jnp.float32)
    for i, copy in enumerate(copies):
        copy.wait()
        acc = lax.fori_loop(i * GROUP, jnp.clip(count[0], i * GROUP, (i + 1) * GROUP), add, acc)
    note[...] = jnp.where(lane == SUM_AT, jnp.sum(acc), wants.astype(jnp.float32))


def plan(layout, blocks, rows, cols, count, tiles):
    return pl.pallas_call(
        functools.partial(plan_kernel, layout, blocks),
        out_shape=(
            jax.ShapeDtypeStruct((3 * 16 * layout.cap,), jnp.int32),
            jax.ShapeDtypeStruct((1, LANES), jnp.float32),
        ),
        in_specs=[SMEM] * 3 + [ANY],
        out_specs=(SMEM, VMEM),
        scratch_shapes=[
            pltpu.SMEM((16,), jnp.int32),
            pltpu.VMEM(tiles.shape, tiles.dtype),
            pltpu.SemaphoreType.DMA((tiles.shape[0] // GROUP,)),
        ],
        compiler_params=params(59 * 2**20),
        cost_estimate=pl.CostEstimate(flops=0, bytes_accessed=0, transcendentals=0),
    )(rows, cols, count, tiles)


def fill_table(layout, mine, notes, table):
    cap = layout.cap
    keys = 16 * cap
    _, yc, _, zs = whereabouts()
    for j in range(4):
        for flip, asked in enumerate(notes, 1):
            for r in range(cap):
                table[layout.pack(j, flip) + r] = asked[0, (zs[j] * 4 + yc) * cap + r].astype(jnp.int32)
    for i, (j, flip) in enumerate(EARLY + LATE):
        for r in range(cap):
            key = (zs[j] * 4 + (yc ^ flip)) * cap + r
            at = layout.entry(i * cap + r)
            table[at] = mine[key]
            table[at + 1] = mine[keys + key]
            table[at + 2] = mine[2 * keys + key]


def start_kernel(layout, mine, note1, note2, note3, own, first, table, out2, out3):
    fill_table(layout, mine, (note1, note2, note3), table)
    other_y_kernel(layout, (0, 1), table, own, first, out2, out3)


def start(layout, mine, notes, own, first):
    _, tile, repl = own.shape
    packs = jax.ShapeDtypeStruct((2 * layout.cap, tile, repl), jnp.bfloat16)
    return pl.pallas_call(
        functools.partial(start_kernel, layout),
        out_shape=(jax.ShapeDtypeStruct((layout.size,), jnp.int32), packs, packs),
        in_specs=[SMEM] * 4 + [VMEM] * 2,
        out_specs=(SMEM, VMEM, VMEM),
        compiler_params=params(),
        cost_estimate=pl.CostEstimate(flops=0, bytes_accessed=0, transcendentals=0),
    )(mine, *notes, own, first)


def copy_asked(layout, table, j, flip, shard, out, first=0):
    at = layout.pack(j, flip)
    for r in range(layout.cap):
        out[first + r] = shard[table[at + r]]


def copy_part(cap, source, part, out, first):
    for r in range(cap):
        out[first + r] = source[part * cap + r]


def by_place(mid, out, use):
    inner = whereabouts()[2]
    pl.when(inner)(lambda: use(mid))
    pl.when(jnp.logical_not(inner))(lambda: use(out))


def other_y_kernel(layout, js, table, *refs):
    shards, outs = refs[:-2], refs[-2:]
    for i, (j, shard) in enumerate(zip(js, shards)):
        for flip in (2, 3):
            copy_asked(layout, table, j, flip, shard, outs[flip - 2], i * layout.cap)


def second_kernel(layout, table, own, first, second, out2, out3, core):
    other_y_kernel(layout, (2,), table, second, out2, out3)
    for j, shard in enumerate((own, first, second)):
        copy_asked(layout, table, j, 1, shard, core, j * layout.cap)


def third_kernel(layout, table, mid, out, out2, out3, core):
    def use(shard):
        other_y_kernel(layout, (3,), table, shard, out2, out3)
        copy_asked(layout, table, 3, 1, shard, core)

    by_place(mid, out, use)


def pack(kernel, sizes, table, arrays):
    _, tile, repl = arrays[0].shape
    return pl.pallas_call(
        kernel,
        out_shape=[jax.ShapeDtypeStruct((size, tile, repl), jnp.bfloat16) for size in sizes],
        in_specs=[SMEM] + [VMEM] * len(arrays),
        out_specs=[VMEM] * len(sizes),
        compiler_params=params(),
        cost_estimate=pl.CostEstimate(flops=0, bytes_accessed=0, transcendentals=0),
    )(table, *arrays)


def multiply(layout, table, tiles, blocks, first, field):
    prods = [
        jnp.dot(tiles[table[layout.entry(first + i)]], block, preferred_element_type=jnp.float32)
        for i, block in enumerate(blocks)
    ]
    for i, prod in enumerate(prods):
        field[table[layout.entry(first + i) + 1]] += prod


def take_own(layout, table, entry, shard, xbuf, place):
    for r in range(layout.cap):
        xbuf[place + r] = shard[table[layout.entry(entry + r) + 2]]


def early_kernel(layout, parts, table, tiles, own, first, second, mid, out, core, core3, *refs):
    cap = layout.cap
    field, xbuf = refs[-2:]
    for j, shard in enumerate((own, first, second)):
        base = 4 * cap * j
        take_own(layout, table, base, shard, xbuf, base)
        copy_part(cap, core, j, xbuf, base + cap)
        ref, part = parts[j]
        copy_part(cap, refs[ref], part, xbuf, base + 2 * cap)
        copy_part(cap, refs[ref + 1], part, xbuf, base + 3 * cap)
    by_place(mid, out, lambda shard: take_own(layout, table, 12 * cap, shard, xbuf, 12 * cap))
    copy_part(cap, core3, 0, xbuf, 13 * cap)
    field[...] = jnp.zeros_like(field)

    @pl.loop(0, len(EARLY) * cap // GROUP)
    def _(g):
        multiply(layout, table, tiles, [xbuf[g * GROUP + i] for i in range(GROUP)], g * GROUP, field)


def early(layout, parts, table, tiles, arrays):
    tile = tiles.shape[1]
    blocks, _, repl = arrays[0].shape
    return pl.pallas_call(
        functools.partial(early_kernel, layout, parts),
        out_shape=jax.ShapeDtypeStruct((blocks + 1, tile, repl), jnp.float32),
        in_specs=[SMEM] + [VMEM] * (1 + len(arrays)),
        out_specs=VMEM,
        scratch_shapes=[pltpu.VMEM((len(EARLY) * layout.cap, tile, repl), jnp.bfloat16)],
        compiler_params=params(),
        cost_estimate=pl.CostEstimate(flops=0, bytes_accessed=0, transcendentals=0),
    )(table, tiles, *arrays)


def late_kernel(layout, last, table, scalars, tiles, got2, got3, field, xpos, ymom, *refs):
    cap = layout.cap
    blocks, _, repl = xpos.shape
    outs, acc = (refs[:3], refs[3]) if last else (refs[:5], refs[5])
    xout, yout = outs[:2]
    acc[...] = field[...]
    multiply(layout, table, tiles, [ref[r] for ref in (got2, got3) for r in range(cap)], len(EARLY) * cap, acc)
    if last:
        xnew, ynew, sems = refs[4:]
    else:
        xnew, ynew = xout, yout
    total = jnp.zeros((1, repl), jnp.float32)
    copies = []
    for b in range(blocks):
        x, h = xpos[b], acc[b]
        if last:
            total += jnp.sum(x * h, axis=0, keepdims=True)
        x, y = update(scalars[0], scalars[1], h, x, ymom[b])
        xnew[b] = x
        ynew[b] = y
        if last:
            copies.append(pltpu.make_async_copy(xnew.at[b], xout.at[b], sems.at[0, b]))
            copies.append(pltpu.make_async_copy(ynew.at[b], yout.at[b], sems.at[1, b]))
            copies[-2].start()
            copies[-1].start()
        else:
            outs[2][b] = x.astype(jnp.bfloat16)
    if last:
        outs[2][...] = -0.5 * total
        for copy in copies:
            copy.wait()
    else:
        other_y_kernel(layout, (0,), table, *outs[2:])


def late(layout, last, table, scalars, tiles, sources, field, xpos, ymom):
    tile = tiles.shape[1]
    blocks, _, repl = xpos.shape
    entries = len(LATE) * layout.cap
    state = jax.ShapeDtypeStruct(xpos.shape, jnp.float32)
    scratch = [pltpu.VMEM((blocks + 1, tile, repl), jnp.float32)]
    if last:
        extra = (jax.ShapeDtypeStruct((1, repl), jnp.float32),)
        scratch += [pltpu.VMEM(xpos.shape, jnp.float32)] * 2 + [pltpu.SemaphoreType.DMA((2, blocks))]
    else:
        out = jax.ShapeDtypeStruct((layout.cap, tile, repl), jnp.bfloat16)
        extra = (jax.ShapeDtypeStruct(xpos.shape, jnp.bfloat16), out, out)
    return pl.pallas_call(
        functools.partial(late_kernel, layout, last),
        out_shape=(state, state) + extra,
        in_specs=[SMEM, SMEM] + [VMEM] * (1 + len(sources) + 3),
        out_specs=((ANY, ANY) if last else (VMEM, VMEM)) + (VMEM,) * len(extra),
        scratch_shapes=scratch,
        compiler_params=params(),
        cost_estimate=pl.CostEstimate(
            flops=2 * entries * tile * tile * repl,
            bytes_accessed=entries * tile * (tile + repl) * 2 + 20 * xpos.size,
            transcendentals=0,
        ),
    )(table, scalars, tiles, *sources, field, xpos, ymom)


def along_z(pairs, value):
    return lax.ppermute(value, "row", [(a * 4 + i, b * 4 + i) for a, b in pairs for i in range(4)])


def across(flip, value):
    return lax.ppermute(value, "row", [(i, i ^ flip) for i in range(16)])


def row_sum(part):
    devices = lax.axis_size("row")
    spread = jnp.broadcast_to(part, (devices,) + part.shape[1:])
    return jnp.sum(lax.all_to_all(spread, "row", split_axis=0, concat_axis=0, tiled=True), axis=0, keepdims=True)


def body_16(tiles, tile_rows, tile_cols, counts, positions, momenta):
    slots, tile, _ = tiles.shape
    repl = positions.shape[1]
    blocks = positions.shape[0] // tile
    cap = (slots + 15) // 16
    order = blocks * tile * 16
    layout = Layout(cap)

    def other_y(js, shards):
        kernel = functools.partial(other_y_kernel, layout, js)
        return pack(kernel, [len(js) * cap] * 2, table, shards)

    def to_other_y(packs):
        return [across(2, packs[0]), across(3, packs[1])]

    xpos = positions.reshape(blocks, tile, repl)
    ymom = momenta.reshape(blocks, tile, repl)
    own0 = xpos.astype(jnp.bfloat16)
    mine, note = plan(layout, blocks, tile_rows, tile_cols, counts, tiles)
    notes = [across(flip, note) for flip in (1, 2, 3)]
    packs0 = None
    for step in range(STEPS):
        last = step == STEPS - 1
        own1 = along_z(FIRST, own0)
        mid = along_z(MIDDLE, own0)
        if step == 0:
            again, notes = lax.optimization_barrier((own0, notes))
            own2 = along_z(SECOND, again)
            own1, notes = lax.optimization_barrier((own1, notes))
            out = along_z(OUTWARD, own1)
            table, *packs01 = start(layout, mine, notes, own0, own1)
            got1 = to_other_y(packs01)
            own2, got1, mid, out = lax.optimization_barrier((own2, got1, mid, out))
            parts = ((0, 0), (0, 1), (2, 0))
            got = got1
        else:
            got0 = to_other_y(packs0)
            again, got0 = lax.optimization_barrier((own0, got0))
            own2 = along_z(SECOND, again)
            own1, got0 = lax.optimization_barrier((own1, got0))
            out = along_z(OUTWARD, own1)
            got1 = to_other_y(other_y((1,), [own1]))
            own2, got1 = lax.optimization_barrier((own2, got1))
            parts = ((0, 0), (2, 0), (4, 0))
            got = got0 + got1
        packs2 = pack(functools.partial(second_kernel, layout), [cap, cap, 3 * cap], table, [own0, own1, own2])
        got2 = to_other_y(packs2)
        core = across(1, packs2[2])
        if step == 0:
            note, core = lax.optimization_barrier((note, core))
            plane = note + notes[0] + notes[1] + notes[2]
            half = plane + across(4, plane)
        packs3 = pack(functools.partial(third_kernel, layout), [cap] * 3, table, [mid, out])
        core3 = across(1, packs3[2])
        got3 = to_other_y(packs3)
        field = early(layout, parts, table, tiles, [own0, own1, own2, mid, out, core, core3] + got + got2)
        if step == 0:
            total = (half + across(8, half))[0, SUM_AT]
            coeff = 0.7 * jnp.sqrt((order - 1) / total)
        scalars = jnp.stack([jnp.float32(0.4 - 0.1 * step), coeff])
        outs = late(layout, last, table, scalars, tiles, got3, field, xpos, ymom)
        xpos, ymom = outs[0], outs[1]
        if not last:
            own0, packs0 = outs[2], outs[3:]
    energy = row_sum(outs[2])
    return (xpos.reshape(positions.shape), ymom.reshape(momenta.shape), energy.reshape(repl))


def gathered_kernel(last, rows, cols, count, scalars, tiles, gathered, xpos, ymom, xout, yout, extra, xbuf, field, xsem):
    tile = xbuf.shape[1]
    used = count[0]

    def block_copy(s):
        return pltpu.make_async_copy(gathered.at[cols[s]], xbuf.at[s], xsem.at[s])

    @pl.loop(0, used)
    def _(s):
        block_copy(s).start()

    field[...] = jnp.zeros_like(field)

    @pl.loop(0, used)
    def _(s):
        block_copy(s).wait()
        here = pl.ds(pl.multiple_of(rows[s] * tile, tile), tile)
        field[here, :] += jnp.dot(tiles[s], xbuf[s], preferred_element_type=jnp.float32)

    x, h = xpos[...], field[...]
    if last:
        extra[...] = -0.5 * jnp.sum(x * h, axis=0, keepdims=True)
    x, y = update(scalars[0], scalars[1], h, x, ymom[...])
    xout[...] = x
    yout[...] = y
    if not last:
        extra[...] = x.astype(jnp.bfloat16)


def body_any(tiles, tile_rows, tile_cols, counts, positions, momenta):
    slots, tile, _ = tiles.shape
    order, repl = positions.shape
    devices = lax.axis_size("row")
    state = jax.ShapeDtypeStruct(positions.shape, jnp.float32)
    total = jnp.sum(lax.psum(squares(counts, tiles), "row"))
    coeff = 0.7 * jnp.sqrt((order * devices - 1) / total)
    xpos, ymom, extra = positions, momenta, positions.astype(jnp.bfloat16)
    for step in range(STEPS):
        last = step == STEPS - 1
        gathered = lax.all_gather(extra, "row", tiled=True).reshape(-1, tile, repl)
        scalars = jnp.stack([jnp.float32(0.4 - 0.1 * step), coeff])
        xpos, ymom, extra = pl.pallas_call(
            functools.partial(gathered_kernel, last),
            out_shape=(
                state,
                state,
                jax.ShapeDtypeStruct((1, repl), jnp.float32) if last else jax.ShapeDtypeStruct(state.shape, jnp.bfloat16),
            ),
            in_specs=[SMEM] * 4 + [VMEM, ANY, VMEM, VMEM],
            out_specs=(VMEM,) * 3,
            scratch_shapes=[
                pltpu.VMEM((slots, tile, repl), jnp.bfloat16),
                pltpu.VMEM(positions.shape, jnp.float32),
                pltpu.SemaphoreType.DMA((slots,)),
            ],
            compiler_params=params(),
        )(tile_rows, tile_cols, counts, scalars, tiles, gathered, xpos, ymom)
    return (xpos, ymom, lax.psum(extra, "row").reshape(repl))


def solution(mesh):
    in_specs = (
        P(("groups", "row"), None, None),
        P(("groups", "row")),
        P(("groups", "row")),
        P(("groups", "row")),
        P(("groups", "row"), None),
        P(("groups", "row"), None),
    )
    out_specs = (P(("groups", "row"), None), P(("groups", "row"), None), P("groups"))

    def body(tiles, *args):
        slots = tiles.shape[0]
        by_hand = mesh.shape["row"] == 16 and slots % GROUP == 0 and slots <= 96
        return (body_16 if by_hand else body_any)(tiles, *args)

    return jax.shard_map(body, mesh=mesh, in_specs=in_specs, out_specs=out_specs, check_vma=False)
```

```python
import functools

import jax
import jax.numpy as jnp
from jax import lax
from jax.experimental import pallas as pl
from jax.experimental.pallas import tpu as pltpu
from jax.sharding import PartitionSpec as P

STEPS = 4
GROUP = 6
LANES = 128
SUM_AT = LANES - 1
LIMIT = 16 * 2**20

SMEM = pl.BlockSpec(memory_space=pltpu.SMEM)
VMEM = pl.BlockSpec(memory_space=pltpu.VMEM)
ANY = pl.BlockSpec(memory_space=pl.ANY)


def params(limit=LIMIT):
    return pltpu.CompilerParams(vmem_limit_bytes=limit)


def squares_kernel(count, tiles, out):
    tile = tiles.shape[1]

    def add(s, acc):
        t = tiles[s].astype(jnp.float32)
        return acc + jnp.sum((t * t).reshape(tile // 8, 8, tile), axis=0)

    acc = lax.fori_loop(0, count[0], add, jnp.zeros((8, tile), jnp.float32))
    acc = jnp.sum(acc, axis=0, keepdims=True)
    out[...] = sum(acc[:, i : i + 128] for i in range(0, tile, 128))


def squares(count, tiles):
    return pl.pallas_call(
        squares_kernel,
        out_shape=jax.ShapeDtypeStruct((1, 128), jnp.float32),
        in_specs=[SMEM, VMEM],
        out_specs=VMEM,
        compiler_params=params(),
        cost_estimate=pl.CostEstimate(flops=2 * tiles.size, bytes_accessed=2 * tiles.size, transcendentals=0),
    )(count, tiles)


def update(pump, coeff, h, x, y):
    y = y + 0.5 * (-(x * x + pump) * x + coeff * h)
    return x + 0.5 * y, y


FIRST = ((0, 2), (3, 1), (1, 0), (2, 3))
SECOND = ((0, 1), (3, 2), (1, 3), (2, 0))
OUTWARD = ((1, 0), (2, 3))
MIDDLE = ((1, 2), (2, 1))


class Layout:
    def __init__(self, cap):
        self.cap = cap
        self.packs = 0
        self.entries = 12 * cap
        self.size = 12 * cap + 3 * 16 * cap

    def pack(self, j, flip):
        return self.packs + (j * 3 + flip - 1) * self.cap

    def entry(self, i):
        return self.entries + 3 * i


def whereabouts():
    me = lax.axis_index("row")
    z, yc = lax.div(me, 4), lax.rem(me, 4)
    inner = (z == 1) | (z == 2)
    near, skip = z ^ 1, z ^ 2
    return z, yc, inner, (z, jnp.where(inner, skip, near), jnp.where(inner, near, skip), z ^ 3)


EARLY = tuple((j, flip) for j in range(3) for flip in range(4)) + ((3, 0), (3, 1))
LATE = ((3, 2), (3, 3))


def plan_kernel(layout, blocks, rows, cols, count, tiles, mine, note, seen, buffer, sems):
    cap = layout.cap
    keys = 16 * cap
    slots, tile, _ = buffer.shape
    chunks = [pl.ds(first, GROUP) for first in range(0, slots, GROUP)]
    copies = [pltpu.make_async_copy(tiles.at[c], buffer.at[c], sems.at[i]) for i, c in enumerate(chunks)]
    for copy in copies:
        copy.start()

    @pl.loop(0, 16)
    def _(d):
        seen[d] = 0

    @pl.loop(0, keys)
    def _(k):
        mine[k] = 0
        mine[keys + k] = blocks
        mine[2 * keys + k] = 0

    @pl.loop(0, count[0])
    def _(s):
        source = lax.div(cols[s], blocks)
        rank = seen[source]
        seen[source] = rank + 1
        key = source * cap + jnp.minimum(rank, cap - 1)
        mine[key] = s
        mine[keys + key] = rows[s]
        mine[2 * keys + key] = lax.rem(cols[s], blocks)

    lane = lax.broadcasted_iota(jnp.int32, note.shape, 1)
    wants = jnp.zeros(note.shape, jnp.int32)
    for k in range(keys):
        wants = jnp.where(lane == k, mine[2 * keys + k], wants)

    def add(s, acc):
        t = buffer[s].astype(jnp.float32)
        return acc + jnp.sum((t * t).reshape(tile // 8, 8, tile), axis=0)

    acc = jnp.zeros((8, tile), jnp.float32)
    for i, copy in enumerate(copies):
        copy.wait()
        acc = lax.fori_loop(i * GROUP, jnp.clip(count[0], i * GROUP, (i + 1) * GROUP), add, acc)
    note[...] = jnp.where(lane == SUM_AT, jnp.sum(acc), wants.astype(jnp.float32))


def plan(layout, blocks, rows, cols, count, tiles):
    return pl.pallas_call(
        functools.partial(plan_kernel, layout, blocks),
        out_shape=(
            jax.ShapeDtypeStruct((3 * 16 * layout.cap,), jnp.int32),
            jax.ShapeDtypeStruct((1, LANES), jnp.float32),
        ),
        in_specs=[SMEM] * 3 + [ANY],
        out_specs=(SMEM, VMEM),
        scratch_shapes=[
            pltpu.SMEM((16,), jnp.int32),
            pltpu.VMEM(tiles.shape, tiles.dtype),
            pltpu.SemaphoreType.DMA((tiles.shape[0] // GROUP,)),
        ],
        compiler_params=params(59 * 2**20),
        cost_estimate=pl.CostEstimate(flops=0, bytes_accessed=0, transcendentals=0),
    )(rows, cols, count, tiles)


def fill_table(layout, mine, notes, table):
    cap = layout.cap
    keys = 16 * cap
    _, yc, _, zs = whereabouts()
    for j in range(4):
        for flip, asked in enumerate(notes, 1):
            for r in range(cap):
                table[layout.pack(j, flip) + r] = asked[0, (zs[j] * 4 + yc) * cap + r].astype(jnp.int32)
    for i, (j, flip) in enumerate(EARLY + LATE):
        for r in range(cap):
            key = (zs[j] * 4 + (yc ^ flip)) * cap + r
            at = layout.entry(i * cap + r)
            table[at] = mine[key]
            table[at + 1] = mine[keys + key]
            table[at + 2] = mine[2 * keys + key]


def start_kernel(layout, mine, note1, note2, note3, own, first, table, out2, out3):
    fill_table(layout, mine, (note1, note2, note3), table)
    other_y_kernel(layout, (0, 1), table, own, first, out2, out3)


def start(layout, mine, notes, own, first):
    _, tile, repl = own.shape
    packs = jax.ShapeDtypeStruct((2 * layout.cap, tile, repl), jnp.bfloat16)
    return pl.pallas_call(
        functools.partial(start_kernel, layout),
        out_shape=(jax.ShapeDtypeStruct((layout.size,), jnp.int32), packs, packs),
        in_specs=[SMEM] * 4 + [VMEM] * 2,
        out_specs=(SMEM, VMEM, VMEM),
        compiler_params=params(),
        cost_estimate=pl.CostEstimate(flops=0, bytes_accessed=0, transcendentals=0),
    )(mine, *notes, own, first)


def copy_asked(layout, table, j, flip, shard, out, first=0):
    at = layout.pack(j, flip)
    for r in range(layout.cap):
        out[first + r] = shard[table[at + r]]


def copy_part(cap, source, part, out, first):
    for r in range(cap):
        out[first + r] = source[part * cap + r]


def by_place(mid, out, use):
    inner = whereabouts()[2]
    pl.when(inner)(lambda: use(mid))
    pl.when(jnp.logical_not(inner))(lambda: use(out))


def other_y_kernel(layout, js, table, *refs):
    shards, outs = refs[:-2], refs[-2:]
    for i, (j, shard) in enumerate(zip(js, shards)):
        for flip in (2, 3):
            copy_asked(layout, table, j, flip, shard, outs[flip - 2], i * layout.cap)


def second_kernel(layout, table, own, first, second, out2, out3, core):
    other_y_kernel(layout, (2,), table, second, out2, out3)
    for j, shard in enumerate((own, first, second)):
        copy_asked(layout, table, j, 1, shard, core, j * layout.cap)


def third_kernel(layout, table, mid, out, out2, out3, core):
    def use(shard):
        other_y_kernel(layout, (3,), table, shard, out2, out3)
        copy_asked(layout, table, 3, 1, shard, core)

    by_place(mid, out, use)


def pack(kernel, sizes, table, arrays):
    _, tile, repl = arrays[0].shape
    return pl.pallas_call(
        kernel,
        out_shape=[jax.ShapeDtypeStruct((size, tile, repl), jnp.bfloat16) for size in sizes],
        in_specs=[SMEM] + [VMEM] * len(arrays),
        out_specs=[VMEM] * len(sizes),
        compiler_params=params(),
        cost_estimate=pl.CostEstimate(flops=0, bytes_accessed=0, transcendentals=0),
    )(table, *arrays)


def multiply(layout, table, tiles, blocks, first, field):
    prods = [
        jnp.dot(tiles[table[layout.entry(first + i)]], block, preferred_element_type=jnp.float32)
        for i, block in enumerate(blocks)
    ]
    for i, prod in enumerate(prods):
        field[table[layout.entry(first + i) + 1]] += prod


def take_own(layout, table, entry, shard, xbuf, place):
    for r in range(layout.cap):
        xbuf[place + r] = shard[table[layout.entry(entry + r) + 2]]


def early_kernel(layout, parts, table, tiles, own, first, second, mid, out, core, core3, *refs):
    cap = layout.cap
    field, xbuf = refs[-2:]
    for j, shard in enumerate((own, first, second)):
        base = 4 * cap * j
        take_own(layout, table, base, shard, xbuf, base)
        copy_part(cap, core, j, xbuf, base + cap)
        ref, part = parts[j]
        copy_part(cap, refs[ref], part, xbuf, base + 2 * cap)
        copy_part(cap, refs[ref + 1], part, xbuf, base + 3 * cap)
    by_place(mid, out, lambda shard: take_own(layout, table, 12 * cap, shard, xbuf, 12 * cap))
    copy_part(cap, core3, 0, xbuf, 13 * cap)
    field[...] = jnp.zeros_like(field)

    @pl.loop(0, len(EARLY) * cap // GROUP)
    def _(g):
        multiply(layout, table, tiles, [xbuf[g * GROUP + i] for i in range(GROUP)], g * GROUP, field)


def early(layout, parts, table, tiles, arrays):
    tile = tiles.shape[1]
    blocks, _, repl = arrays[0].shape
    return pl.pallas_call(
        functools.partial(early_kernel, layout, parts),
        out_shape=jax.ShapeDtypeStruct((blocks + 1, tile, repl), jnp.float32),
        in_specs=[SMEM] + [VMEM] * (1 + len(arrays)),
        out_specs=VMEM,
        scratch_shapes=[pltpu.VMEM((len(EARLY) * layout.cap, tile, repl), jnp.bfloat16)],
        compiler_params=params(),
        cost_estimate=pl.CostEstimate(flops=0, bytes_accessed=0, transcendentals=0),
    )(table, tiles, *arrays)


def late_kernel(layout, last, table, scalars, tiles, got2, got3, field, xpos, ymom, *refs):
    cap = layout.cap
    blocks, _, repl = xpos.shape
    outs, acc = (refs[:3], refs[3]) if last else (refs[:5], refs[5])
    xout, yout = outs[:2]
    acc[...] = field[...]
    multiply(layout, table, tiles, [ref[r] for ref in (got2, got3) for r in range(cap)], len(EARLY) * cap, acc)
    if last:
        xnew, ynew, sems = refs[4:]
    else:
        xnew, ynew = xout, yout
    total = jnp.zeros((1, repl), jnp.float32)
    copies = []
    for b in range(blocks):
        x, h = xpos[b], acc[b]
        if last:
            total += jnp.sum(x * h, axis=0, keepdims=True)
        x, y = update(scalars[0], scalars[1], h, x, ymom[b])
        xnew[b] = x
        ynew[b] = y
        if last:
            copies.append(pltpu.make_async_copy(xnew.at[b], xout.at[b], sems.at[0, b]))
            copies.append(pltpu.make_async_copy(ynew.at[b], yout.at[b], sems.at[1, b]))
            copies[-2].start()
            copies[-1].start()
        else:
            outs[2][b] = x.astype(jnp.bfloat16)
    if last:
        outs[2][...] = -0.5 * total
        for copy in copies:
            copy.wait()
    else:
        other_y_kernel(layout, (0,), table, *outs[2:])


def late(layout, last, table, scalars, tiles, sources, field, xpos, ymom):
    tile = tiles.shape[1]
    blocks, _, repl = xpos.shape
    entries = len(LATE) * layout.cap
    state = jax.ShapeDtypeStruct(xpos.shape, jnp.float32)
    scratch = [pltpu.VMEM((blocks + 1, tile, repl), jnp.float32)]
    if last:
        extra = (jax.ShapeDtypeStruct((1, repl), jnp.float32),)
        scratch += [pltpu.VMEM(xpos.shape, jnp.float32)] * 2 + [pltpu.SemaphoreType.DMA((2, blocks))]
    else:
        out = jax.ShapeDtypeStruct((layout.cap, tile, repl), jnp.bfloat16)
        extra = (jax.ShapeDtypeStruct(xpos.shape, jnp.bfloat16), out, out)
    return pl.pallas_call(
        functools.partial(late_kernel, layout, last),
        out_shape=(state, state) + extra,
        in_specs=[SMEM, SMEM] + [VMEM] * (1 + len(sources) + 3),
        out_specs=((ANY, ANY) if last else (VMEM, VMEM)) + (VMEM,) * len(extra),
        scratch_shapes=scratch,
        compiler_params=params(),
        cost_estimate=pl.CostEstimate(
            flops=2 * entries * tile * tile * repl,
            bytes_accessed=entries * tile * (tile + repl) * 2 + 20 * xpos.size,
            transcendentals=0,
        ),
    )(table, scalars, tiles, *sources, field, xpos, ymom)


def along_z(pairs, value):
    return lax.ppermute(value, "row", [(a * 4 + i, b * 4 + i) for a, b in pairs for i in range(4)])


def across(flip, value):
    return lax.ppermute(value, "row", [(i, i ^ flip) for i in range(16)])


def row_sum(part):
    devices = lax.axis_size("row")
    spread = jnp.broadcast_to(part, (devices,) + part.shape[1:])
    return jnp.sum(lax.all_to_all(spread, "row", split_axis=0, concat_axis=0, tiled=True), axis=0, keepdims=True)


def body_16(tiles, tile_rows, tile_cols, counts, positions, momenta):
    slots, tile, _ = tiles.shape
    repl = positions.shape[1]
    blocks = positions.shape[0] // tile
    cap = (slots + 15) // 16
    order = blocks * tile * 16
    layout = Layout(cap)

    def other_y(js, shards):
        kernel = functools.partial(other_y_kernel, layout, js)
        return pack(kernel, [len(js) * cap] * 2, table, shards)

    def to_other_y(packs):
        return [across(2, packs[0]), across(3, packs[1])]

    xpos = positions.reshape(blocks, tile, repl)
    ymom = momenta.reshape(blocks, tile, repl)
    own0 = xpos.astype(jnp.bfloat16)
    mine, note = plan(layout, blocks, tile_rows, tile_cols, counts, tiles)
    notes = [across(flip, note) for flip in (1, 2, 3)]
    packs0 = None
    for step in range(STEPS):
        last = step == STEPS - 1
        own1 = along_z(FIRST, own0)
        if step == 0:
            again, notes = lax.optimization_barrier((own0, notes))
            own2 = along_z(SECOND, again)
            again, own1 = lax.optimization_barrier((again, own1))
            mid = along_z(MIDDLE, again)
            out = along_z(OUTWARD, own1)
            table, *packs01 = start(layout, mine, notes, own0, own1)
            got1 = to_other_y(packs01)
            own2, got1, mid, out = lax.optimization_barrier((own2, got1, mid, out))
            parts = ((0, 0), (0, 1), (2, 0))
            got = got1
        else:
            mid = along_z(MIDDLE, own0)
            got0 = to_other_y(packs0)
            again, got0 = lax.optimization_barrier((own0, got0))
            own2 = along_z(SECOND, again)
            own1, got0 = lax.optimization_barrier((own1, got0))
            out = along_z(OUTWARD, own1)
            got1 = to_other_y(other_y((1,), [own1]))
            own2, got1 = lax.optimization_barrier((own2, got1))
            parts = ((0, 0), (2, 0), (4, 0))
            got = got0 + got1
        packs2 = pack(functools.partial(second_kernel, layout), [cap, cap, 3 * cap], table, [own0, own1, own2])
        got2 = to_other_y(packs2)
        core = across(1, packs2[2])
        if step == 0:
            note, core = lax.optimization_barrier((note, core))
            plane = note + notes[0] + notes[1] + notes[2]
            half = plane + across(4, plane)
        packs3 = pack(functools.partial(third_kernel, layout), [cap] * 3, table, [mid, out])
        core3 = across(1, packs3[2])
        got3 = to_other_y(packs3)
        field = early(layout, parts, table, tiles, [own0, own1, own2, mid, out, core, core3] + got + got2)
        if step == 0:
            total = (half + across(8, half))[0, SUM_AT]
            coeff = 0.7 * jnp.sqrt((order - 1) / total)
        scalars = jnp.stack([jnp.float32(0.4 - 0.1 * step), coeff])
        outs = late(layout, last, table, scalars, tiles, got3, field, xpos, ymom)
        xpos, ymom = outs[0], outs[1]
        if not last:
            own0, packs0 = outs[2], outs[3:]
    energy = row_sum(outs[2])
    return (xpos.reshape(positions.shape), ymom.reshape(momenta.shape), energy.reshape(repl))


def gathered_kernel(last, rows, cols, count, scalars, tiles, gathered, xpos, ymom, xout, yout, extra, xbuf, field, xsem):
    tile = xbuf.shape[1]
    used = count[0]

    def block_copy(s):
        return pltpu.make_async_copy(gathered.at[cols[s]], xbuf.at[s], xsem.at[s])

    @pl.loop(0, used)
    def _(s):
        block_copy(s).start()

    field[...] = jnp.zeros_like(field)

    @pl.loop(0, used)
    def _(s):
        block_copy(s).wait()
        here = pl.ds(pl.multiple_of(rows[s] * tile, tile), tile)
        field[here, :] += jnp.dot(tiles[s], xbuf[s], preferred_element_type=jnp.float32)

    x, h = xpos[...], field[...]
    if last:
        extra[...] = -0.5 * jnp.sum(x * h, axis=0, keepdims=True)
    x, y = update(scalars[0], scalars[1], h, x, ymom[...])
    xout[...] = x
    yout[...] = y
    if not last:
        extra[...] = x.astype(jnp.bfloat16)


def body_any(tiles, tile_rows, tile_cols, counts, positions, momenta):
    slots, tile, _ = tiles.shape
    order, repl = positions.shape
    devices = lax.axis_size("row")
    state = jax.ShapeDtypeStruct(positions.shape, jnp.float32)
    total = jnp.sum(lax.psum(squares(counts, tiles), "row"))
    coeff = 0.7 * jnp.sqrt((order * devices - 1) / total)
    xpos, ymom, extra = positions, momenta, positions.astype(jnp.bfloat16)
    for step in range(STEPS):
        last = step == STEPS - 1
        gathered = lax.all_gather(extra, "row", tiled=True).reshape(-1, tile, repl)
        scalars = jnp.stack([jnp.float32(0.4 - 0.1 * step), coeff])
        xpos, ymom, extra = pl.pallas_call(
            functools.partial(gathered_kernel, last),
            out_shape=(
                state,
                state,
                jax.ShapeDtypeStruct((1, repl), jnp.float32) if last else jax.ShapeDtypeStruct(state.shape, jnp.bfloat16),
            ),
            in_specs=[SMEM] * 4 + [VMEM, ANY, VMEM, VMEM],
            out_specs=(VMEM,) * 3,
            scratch_shapes=[
                pltpu.VMEM((slots, tile, repl), jnp.bfloat16),
                pltpu.VMEM(positions.shape, jnp.float32),
                pltpu.SemaphoreType.DMA((slots,)),
            ],
            compiler_params=params(),
        )(tile_rows, tile_cols, counts, scalars, tiles, gathered, xpos, ymom)
    return (xpos, ymom, lax.psum(extra, "row").reshape(repl))


def solution(mesh):
    in_specs = (
        P(("groups", "row"), None, None),
        P(("groups", "row")),
        P(("groups", "row")),
        P(("groups", "row")),
        P(("groups", "row"), None),
        P(("groups", "row"), None),
    )
    out_specs = (P(("groups", "row"), None), P(("groups", "row"), None), P("groups"))

    def body(tiles, *args):
        slots = tiles.shape[0]
        by_hand = mesh.shape["row"] == 16 and slots % GROUP == 0 and slots <= 96
        return (body_16 if by_hand else body_any)(tiles, *args)

    return jax.shard_map(body, mesh=mesh, in_specs=in_specs, out_specs=out_specs, check_vma=False)
```

```python
import functools

import jax
import jax.numpy as jnp
from jax import lax
from jax.experimental import pallas as pl
from jax.experimental.pallas import tpu as pltpu
from jax.sharding import PartitionSpec as P

STEPS = 4
GROUP = 6
LANES = 128
SUM_AT = LANES - 1
LIMIT = 16 * 2**20

SMEM = pl.BlockSpec(memory_space=pltpu.SMEM)
VMEM = pl.BlockSpec(memory_space=pltpu.VMEM)
ANY = pl.BlockSpec(memory_space=pl.ANY)


def params(limit=LIMIT):
    return pltpu.CompilerParams(vmem_limit_bytes=limit)


def squares_kernel(count, tiles, out):
    tile = tiles.shape[1]

    def add(s, acc):
        t = tiles[s].astype(jnp.float32)
        return acc + jnp.sum((t * t).reshape(tile // 8, 8, tile), axis=0)

    acc = lax.fori_loop(0, count[0], add, jnp.zeros((8, tile), jnp.float32))
    acc = jnp.sum(acc, axis=0, keepdims=True)
    out[...] = sum(acc[:, i : i + 128] for i in range(0, tile, 128))


def squares(count, tiles):
    return pl.pallas_call(
        squares_kernel,
        out_shape=jax.ShapeDtypeStruct((1, 128), jnp.float32),
        in_specs=[SMEM, VMEM],
        out_specs=VMEM,
        compiler_params=params(),
        cost_estimate=pl.CostEstimate(flops=2 * tiles.size, bytes_accessed=2 * tiles.size, transcendentals=0),
    )(count, tiles)


def update(pump, coeff, h, x, y):
    y = y + 0.5 * (-(x * x + pump) * x + coeff * h)
    return x + 0.5 * y, y


FIRST = ((0, 2), (3, 1), (1, 0), (2, 3))
SECOND = ((0, 1), (3, 2), (1, 3), (2, 0))
OUTWARD = ((1, 0), (2, 3))
MIDDLE = ((1, 2), (2, 1))


class Layout:
    def __init__(self, cap):
        self.cap = cap
        self.packs = 0
        self.entries = 12 * cap
        self.size = 12 * cap + 3 * 16 * cap

    def pack(self, j, flip):
        return self.packs + (j * 3 + flip - 1) * self.cap

    def entry(self, i):
        return self.entries + 3 * i


def whereabouts():
    me = lax.axis_index("row")
    z, yc = lax.div(me, 4), lax.rem(me, 4)
    inner = (z == 1) | (z == 2)
    near, skip = z ^ 1, z ^ 2
    return z, yc, inner, (z, jnp.where(inner, skip, near), jnp.where(inner, near, skip), z ^ 3)


EARLY = tuple((j, flip) for j in range(3) for flip in range(4)) + ((3, 0), (3, 1))
LATE = ((3, 2), (3, 3))


def plan_kernel(layout, blocks, rows, cols, count, tiles, mine, note, seen, buffer, sems):
    cap = layout.cap
    keys = 16 * cap
    slots, tile, _ = buffer.shape
    chunks = [pl.ds(first, GROUP) for first in range(0, slots, GROUP)]
    copies = [pltpu.make_async_copy(tiles.at[c], buffer.at[c], sems.at[i]) for i, c in enumerate(chunks)]
    for copy in copies:
        copy.start()

    @pl.loop(0, 16)
    def _(d):
        seen[d] = 0

    @pl.loop(0, keys)
    def _(k):
        mine[k] = 0
        mine[keys + k] = blocks
        mine[2 * keys + k] = 0

    @pl.loop(0, count[0])
    def _(s):
        source = lax.div(cols[s], blocks)
        rank = seen[source]
        seen[source] = rank + 1
        key = source * cap + jnp.minimum(rank, cap - 1)
        mine[key] = s
        mine[keys + key] = rows[s]
        mine[2 * keys + key] = lax.rem(cols[s], blocks)

    lane = lax.broadcasted_iota(jnp.int32, note.shape, 1)
    wants = jnp.zeros(note.shape, jnp.int32)
    for k in range(keys):
        wants = jnp.where(lane == k, mine[2 * keys + k], wants)

    def add(s, acc):
        t = buffer[s].astype(jnp.float32)
        return acc + jnp.sum((t * t).reshape(tile // 8, 8, tile), axis=0)

    acc = jnp.zeros((8, tile), jnp.float32)
    for i, copy in enumerate(copies):
        copy.wait()
        acc = lax.fori_loop(i * GROUP, jnp.clip(count[0], i * GROUP, (i + 1) * GROUP), add, acc)
    note[...] = jnp.where(lane == SUM_AT, jnp.sum(acc), wants.astype(jnp.float32))


def plan(layout, blocks, rows, cols, count, tiles):
    return pl.pallas_call(
        functools.partial(plan_kernel, layout, blocks),
        out_shape=(
            jax.ShapeDtypeStruct((3 * 16 * layout.cap,), jnp.int32),
            jax.ShapeDtypeStruct((1, LANES), jnp.float32),
        ),
        in_specs=[SMEM] * 3 + [ANY],
        out_specs=(SMEM, VMEM),
        scratch_shapes=[
            pltpu.SMEM((16,), jnp.int32),
            pltpu.VMEM(tiles.shape, tiles.dtype),
            pltpu.SemaphoreType.DMA((tiles.shape[0] // GROUP,)),
        ],
        compiler_params=params(59 * 2**20),
        cost_estimate=pl.CostEstimate(flops=0, bytes_accessed=0, transcendentals=0),
    )(rows, cols, count, tiles)


def fill_table(layout, mine, notes, table):
    cap = layout.cap
    keys = 16 * cap
    _, yc, _, zs = whereabouts()
    for j in range(4):
        for flip, asked in enumerate(notes, 1):
            for r in range(cap):
                table[layout.pack(j, flip) + r] = asked[0, (zs[j] * 4 + yc) * cap + r].astype(jnp.int32)
    for i, (j, flip) in enumerate(EARLY + LATE):
        for r in range(cap):
            key = (zs[j] * 4 + (yc ^ flip)) * cap + r
            at = layout.entry(i * cap + r)
            table[at] = mine[key]
            table[at + 1] = mine[keys + key]
            table[at + 2] = mine[2 * keys + key]


def start_kernel(layout, mine, note1, note2, note3, own, first, table, out2, out3):
    fill_table(layout, mine, (note1, note2, note3), table)
    other_y_kernel(layout, (0, 1), table, own, first, out2, out3)


def start(layout, mine, notes, own, first):
    _, tile, repl = own.shape
    packs = jax.ShapeDtypeStruct((2 * layout.cap, tile, repl), jnp.bfloat16)
    return pl.pallas_call(
        functools.partial(start_kernel, layout),
        out_shape=(jax.ShapeDtypeStruct((layout.size,), jnp.int32), packs, packs),
        in_specs=[SMEM] * 4 + [VMEM] * 2,
        out_specs=(SMEM, VMEM, VMEM),
        compiler_params=params(),
        cost_estimate=pl.CostEstimate(flops=0, bytes_accessed=0, transcendentals=0),
    )(mine, *notes, own, first)


def copy_asked(layout, table, j, flip, shard, out, first=0):
    at = layout.pack(j, flip)
    for r in range(layout.cap):
        out[first + r] = shard[table[at + r]]


def copy_part(cap, source, part, out, first):
    for r in range(cap):
        out[first + r] = source[part * cap + r]


def by_place(mid, out, use):
    inner = whereabouts()[2]
    pl.when(inner)(lambda: use(mid))
    pl.when(jnp.logical_not(inner))(lambda: use(out))


def other_y_kernel(layout, js, table, *refs):
    shards, outs = refs[:-2], refs[-2:]
    for i, (j, shard) in enumerate(zip(js, shards)):
        for flip in (2, 3):
            copy_asked(layout, table, j, flip, shard, outs[flip - 2], i * layout.cap)


def second_kernel(layout, js, table, *refs):
    shards, (out2, out3, core) = refs[:-3], refs[-3:]
    other_y_kernel(layout, (2,), table, shards[-1], out2, out3)
    for i, (j, shard) in enumerate(zip(js, shards)):
        copy_asked(layout, table, j, 1, shard, core, i * layout.cap)


def third_kernel(layout, table, mid, out, out2, out3, core):
    def use(shard):
        other_y_kernel(layout, (3,), table, shard, out2, out3)
        copy_asked(layout, table, 3, 1, shard, core)

    by_place(mid, out, use)


def pack(kernel, sizes, table, arrays):
    _, tile, repl = arrays[0].shape
    return pl.pallas_call(
        kernel,
        out_shape=[jax.ShapeDtypeStruct((size, tile, repl), jnp.bfloat16) for size in sizes],
        in_specs=[SMEM] + [VMEM] * len(arrays),
        out_specs=[VMEM] * len(sizes),
        compiler_params=params(),
        cost_estimate=pl.CostEstimate(flops=0, bytes_accessed=0, transcendentals=0),
    )(table, *arrays)


def multiply(layout, table, tiles, blocks, first, field):
    prods = [
        jnp.dot(tiles[table[layout.entry(first + i)]], block, preferred_element_type=jnp.float32)
        for i, block in enumerate(blocks)
    ]
    for i, prod in enumerate(prods):
        field[table[layout.entry(first + i) + 1]] += prod


def take_own(layout, table, entry, shard, xbuf, place):
    for r in range(layout.cap):
        xbuf[place + r] = shard[table[layout.entry(entry + r) + 2]]


def early_kernel(layout, parts, table, tiles, own, first, second, mid, out, core, core3, *refs):
    cap = layout.cap
    field, xbuf = refs[-2:]
    for j, shard in enumerate((own, first, second)):
        base = 4 * cap * j
        take_own(layout, table, base, shard, xbuf, base)
        if core.shape[0] == 3 * cap:
            copy_part(cap, core, j, xbuf, base + cap)
        elif j == 0:
            copy_part(cap, refs[-3], 0, xbuf, base + cap)
        else:
            copy_part(cap, core, j - 1, xbuf, base + cap)
        ref, part = parts[j]
        copy_part(cap, refs[ref], part, xbuf, base + 2 * cap)
        copy_part(cap, refs[ref + 1], part, xbuf, base + 3 * cap)
    by_place(mid, out, lambda shard: take_own(layout, table, 12 * cap, shard, xbuf, 12 * cap))
    copy_part(cap, core3, 0, xbuf, 13 * cap)
    field[...] = jnp.zeros_like(field)

    @pl.loop(0, len(EARLY) * cap // GROUP)
    def _(g):
        multiply(layout, table, tiles, [xbuf[g * GROUP + i] for i in range(GROUP)], g * GROUP, field)


def early(layout, parts, table, tiles, arrays):
    tile = tiles.shape[1]
    blocks, _, repl = arrays[0].shape
    return pl.pallas_call(
        functools.partial(early_kernel, layout, parts),
        out_shape=jax.ShapeDtypeStruct((blocks + 1, tile, repl), jnp.float32),
        in_specs=[SMEM] + [VMEM] * (1 + len(arrays)),
        out_specs=VMEM,
        scratch_shapes=[pltpu.VMEM((len(EARLY) * layout.cap, tile, repl), jnp.bfloat16)],
        compiler_params=params(),
        cost_estimate=pl.CostEstimate(flops=0, bytes_accessed=0, transcendentals=0),
    )(table, tiles, *arrays)


def late_kernel(layout, last, table, scalars, tiles, got2, got3, field, xpos, ymom, *refs):
    cap = layout.cap
    blocks, _, repl = xpos.shape
    outs, acc = (refs[:3], refs[3]) if last else (refs[:6], refs[6])
    xout, yout = outs[:2]
    acc[...] = field[...]
    multiply(layout, table, tiles, [ref[r] for ref in (got2, got3) for r in range(cap)], len(EARLY) * cap, acc)
    if last:
        xnew, ynew, sems = refs[4:]
    else:
        xnew, ynew = xout, yout
    total = jnp.zeros((1, repl), jnp.float32)
    copies = []
    for b in range(blocks):
        x, h = xpos[b], acc[b]
        if last:
            total += jnp.sum(x * h, axis=0, keepdims=True)
        x, y = update(scalars[0], scalars[1], h, x, ymom[b])
        xnew[b] = x
        ynew[b] = y
        if last:
            copies.append(pltpu.make_async_copy(xnew.at[b], xout.at[b], sems.at[0, b]))
            copies.append(pltpu.make_async_copy(ynew.at[b], yout.at[b], sems.at[1, b]))
            copies[-2].start()
            copies[-1].start()
        else:
            outs[2][b] = x.astype(jnp.bfloat16)
    if last:
        outs[2][...] = -0.5 * total
        for copy in copies:
            copy.wait()
    else:
        other_y_kernel(layout, (0,), table, *outs[2:5])
        copy_asked(layout, table, 0, 1, outs[2], outs[5])


def late(layout, last, table, scalars, tiles, sources, field, xpos, ymom):
    tile = tiles.shape[1]
    blocks, _, repl = xpos.shape
    entries = len(LATE) * layout.cap
    state = jax.ShapeDtypeStruct(xpos.shape, jnp.float32)
    scratch = [pltpu.VMEM((blocks + 1, tile, repl), jnp.float32)]
    if last:
        extra = (jax.ShapeDtypeStruct((1, repl), jnp.float32),)
        scratch += [pltpu.VMEM(xpos.shape, jnp.float32)] * 2 + [pltpu.SemaphoreType.DMA((2, blocks))]
    else:
        out = jax.ShapeDtypeStruct((layout.cap, tile, repl), jnp.bfloat16)
        extra = (jax.ShapeDtypeStruct(xpos.shape, jnp.bfloat16), out, out, out)
    return pl.pallas_call(
        functools.partial(late_kernel, layout, last),
        out_shape=(state, state) + extra,
        in_specs=[SMEM, SMEM] + [VMEM] * (1 + len(sources) + 3),
        out_specs=((ANY, ANY) if last else (VMEM, VMEM)) + (VMEM,) * len(extra),
        scratch_shapes=scratch,
        compiler_params=params(),
        cost_estimate=pl.CostEstimate(
            flops=2 * entries * tile * tile * repl,
            bytes_accessed=entries * tile * (tile + repl) * 2 + 20 * xpos.size,
            transcendentals=0,
        ),
    )(table, scalars, tiles, *sources, field, xpos, ymom)


def along_z(pairs, value):
    return lax.ppermute(value, "row", [(a * 4 + i, b * 4 + i) for a, b in pairs for i in range(4)])


def across(flip, value):
    return lax.ppermute(value, "row", [(i, i ^ flip) for i in range(16)])


def row_sum(part):
    devices = lax.axis_size("row")
    spread = jnp.broadcast_to(part, (devices,) + part.shape[1:])
    return jnp.sum(lax.all_to_all(spread, "row", split_axis=0, concat_axis=0, tiled=True), axis=0, keepdims=True)


def body_16(tiles, tile_rows, tile_cols, counts, positions, momenta):
    slots, tile, _ = tiles.shape
    repl = positions.shape[1]
    blocks = positions.shape[0] // tile
    cap = (slots + 15) // 16
    order = blocks * tile * 16
    layout = Layout(cap)

    def other_y(js, shards):
        kernel = functools.partial(other_y_kernel, layout, js)
        return pack(kernel, [len(js) * cap] * 2, table, shards)

    def to_other_y(packs):
        return [across(2, packs[0]), across(3, packs[1])]

    xpos = positions.reshape(blocks, tile, repl)
    ymom = momenta.reshape(blocks, tile, repl)
    own0 = xpos.astype(jnp.bfloat16)
    mine, note = plan(layout, blocks, tile_rows, tile_cols, counts, tiles)
    notes = [across(flip, note) for flip in (1, 2, 3)]
    packs0 = None
    for step in range(STEPS):
        last = step == STEPS - 1
        own1 = along_z(FIRST, own0)
        if step == 0:
            again, notes[0] = lax.optimization_barrier((own0, notes[0]))
            own2 = along_z(SECOND, again)
            again, notes = lax.optimization_barrier((again, notes))
            mid = along_z(MIDDLE, again)
            own1, notes = lax.optimization_barrier((own1, notes))
            out = along_z(OUTWARD, own1)
            table, *packs01 = start(layout, mine, notes, own0, own1)
            got1 = to_other_y(packs01)
            own2, got1, mid, out = lax.optimization_barrier((own2, got1, mid, out))
            parts, cores = ((0, 0), (0, 1), (2, 0)), []
            got = got1
        else:
            core0 = across(1, packs0[2])
            again, core0 = lax.optimization_barrier((own0, core0))
            own2 = along_z(SECOND, again)
            got0 = to_other_y(packs0)
            again, got0 = lax.optimization_barrier((again, got0))
            own1, got0 = lax.optimization_barrier((own1, got0))
            packs1 = other_y((1,), [own1])
            out = along_z(OUTWARD, own1)
            got1 = to_other_y(packs1)
            mid = along_z(MIDDLE, again)
            own2, got1 = lax.optimization_barrier((own2, got1))
            parts, cores = ((0, 0), (2, 0), (4, 0)), [core0]
            got = got0 + got1
        js, shards = ((0, 1, 2), [own0, own1, own2]) if step == 0 else ((1, 2), [own1, own2])
        packs2 = pack(functools.partial(second_kernel, layout, js), [cap, cap, len(js) * cap], table, shards)
        got2 = to_other_y(packs2)
        core = across(1, packs2[2])
        if step == 0:
            note, core = lax.optimization_barrier((note, core))
            plane = note + notes[0] + notes[1] + notes[2]
            half = plane + across(4, plane)
        packs3 = pack(functools.partial(third_kernel, layout), [cap] * 3, table, [mid, out])
        core3 = across(1, packs3[2])
        got3 = to_other_y(packs3)
        field = early(layout, parts, table, tiles, [own0, own1, own2, mid, out, core, core3] + got + got2 + cores)
        if step == 0:
            total = (half + across(8, half))[0, SUM_AT]
            coeff = 0.7 * jnp.sqrt((order - 1) / total)
        scalars = jnp.stack([jnp.float32(0.4 - 0.1 * step), coeff])
        outs = late(layout, last, table, scalars, tiles, got3, field, xpos, ymom)
        xpos, ymom = outs[0], outs[1]
        if not last:
            own0, packs0 = outs[2], outs[3:]
    energy = row_sum(outs[2])
    return (xpos.reshape(positions.shape), ymom.reshape(momenta.shape), energy.reshape(repl))


def gathered_kernel(last, rows, cols, count, scalars, tiles, gathered, xpos, ymom, xout, yout, extra, xbuf, field, xsem):
    tile = xbuf.shape[1]
    used = count[0]

    def block_copy(s):
        return pltpu.make_async_copy(gathered.at[cols[s]], xbuf.at[s], xsem.at[s])

    @pl.loop(0, used)
    def _(s):
        block_copy(s).start()

    field[...] = jnp.zeros_like(field)

    @pl.loop(0, used)
    def _(s):
        block_copy(s).wait()
        here = pl.ds(pl.multiple_of(rows[s] * tile, tile), tile)
        field[here, :] += jnp.dot(tiles[s], xbuf[s], preferred_element_type=jnp.float32)

    x, h = xpos[...], field[...]
    if last:
        extra[...] = -0.5 * jnp.sum(x * h, axis=0, keepdims=True)
    x, y = update(scalars[0], scalars[1], h, x, ymom[...])
    xout[...] = x
    yout[...] = y
    if not last:
        extra[...] = x.astype(jnp.bfloat16)


def body_any(tiles, tile_rows, tile_cols, counts, positions, momenta):
    slots, tile, _ = tiles.shape
    order, repl = positions.shape
    devices = lax.axis_size("row")
    state = jax.ShapeDtypeStruct(positions.shape, jnp.float32)
    total = jnp.sum(lax.psum(squares(counts, tiles), "row"))
    coeff = 0.7 * jnp.sqrt((order * devices - 1) / total)
    xpos, ymom, extra = positions, momenta, positions.astype(jnp.bfloat16)
    for step in range(STEPS):
        last = step == STEPS - 1
        gathered = lax.all_gather(extra, "row", tiled=True).reshape(-1, tile, repl)
        scalars = jnp.stack([jnp.float32(0.4 - 0.1 * step), coeff])
        xpos, ymom, extra = pl.pallas_call(
            functools.partial(gathered_kernel, last),
            out_shape=(
                state,
                state,
                jax.ShapeDtypeStruct((1, repl), jnp.float32) if last else jax.ShapeDtypeStruct(state.shape, jnp.bfloat16),
            ),
            in_specs=[SMEM] * 4 + [VMEM, ANY, VMEM, VMEM],
            out_specs=(VMEM,) * 3,
            scratch_shapes=[
                pltpu.VMEM((slots, tile, repl), jnp.bfloat16),
                pltpu.VMEM(positions.shape, jnp.float32),
                pltpu.SemaphoreType.DMA((slots,)),
            ],
            compiler_params=params(),
        )(tile_rows, tile_cols, counts, scalars, tiles, gathered, xpos, ymom)
    return (xpos, ymom, lax.psum(extra, "row").reshape(repl))


def solution(mesh):
    in_specs = (
        P(("groups", "row"), None, None),
        P(("groups", "row")),
        P(("groups", "row")),
        P(("groups", "row")),
        P(("groups", "row"), None),
        P(("groups", "row"), None),
    )
    out_specs = (P(("groups", "row"), None), P(("groups", "row"), None), P("groups"))

    def body(tiles, *args):
        slots = tiles.shape[0]
        by_hand = mesh.shape["row"] == 16 and slots % GROUP == 0 and slots <= 96
        return (body_16 if by_hand else body_any)(tiles, *args)

    return jax.shard_map(body, mesh=mesh, in_specs=in_specs, out_specs=out_specs, check_vma=False)
```

```python
import functools

import jax
import jax.numpy as jnp
from jax import lax
from jax.experimental import pallas as pl
from jax.experimental.pallas import tpu as pltpu
from jax.sharding import PartitionSpec as P

STEPS = 4
GROUP = 6
LANES = 128
SUM_AT = LANES - 1
LIMIT = 16 * 2**20

SMEM = pl.BlockSpec(memory_space=pltpu.SMEM)
VMEM = pl.BlockSpec(memory_space=pltpu.VMEM)
ANY = pl.BlockSpec(memory_space=pl.ANY)


def params(limit=LIMIT):
    return pltpu.CompilerParams(vmem_limit_bytes=limit)


def squares_kernel(count, tiles, out):
    tile = tiles.shape[1]

    def add(s, acc):
        t = tiles[s].astype(jnp.float32)
        return acc + jnp.sum((t * t).reshape(tile // 8, 8, tile), axis=0)

    acc = lax.fori_loop(0, count[0], add, jnp.zeros((8, tile), jnp.float32))
    acc = jnp.sum(acc, axis=0, keepdims=True)
    out[...] = sum(acc[:, i : i + 128] for i in range(0, tile, 128))


def squares(count, tiles):
    return pl.pallas_call(
        squares_kernel,
        out_shape=jax.ShapeDtypeStruct((1, 128), jnp.float32),
        in_specs=[SMEM, VMEM],
        out_specs=VMEM,
        compiler_params=params(),
        cost_estimate=pl.CostEstimate(flops=2 * tiles.size, bytes_accessed=2 * tiles.size, transcendentals=0),
    )(count, tiles)


def update(pump, coeff, h, x, y):
    y = y + 0.5 * (-(x * x + pump) * x + coeff * h)
    return x + 0.5 * y, y


FIRST = ((0, 2), (3, 1), (1, 0), (2, 3))
SECOND = ((0, 1), (3, 2), (1, 3), (2, 0))
OUTWARD = ((1, 0), (2, 3))
MIDDLE = ((1, 2), (2, 1))


class Layout:
    def __init__(self, cap):
        self.cap = cap
        self.packs = 0
        self.entries = 12 * cap
        self.size = 12 * cap + 3 * 16 * cap

    def pack(self, j, flip):
        return self.packs + (j * 3 + flip - 1) * self.cap

    def entry(self, i):
        return self.entries + 3 * i


def whereabouts():
    me = lax.axis_index("row")
    z, yc = lax.div(me, 4), lax.rem(me, 4)
    inner = (z == 1) | (z == 2)
    near, skip = z ^ 1, z ^ 2
    return z, yc, inner, (z, jnp.where(inner, skip, near), jnp.where(inner, near, skip), z ^ 3)


EARLY = tuple((j, flip) for j in range(3) for flip in range(4)) + ((3, 0), (3, 1))
LATE = ((3, 2), (3, 3))


def plan_kernel(layout, blocks, rows, cols, count, tiles, mine, note, seen, buffer, sems):
    cap = layout.cap
    keys = 16 * cap
    slots, tile, _ = buffer.shape
    chunks = [pl.ds(first, GROUP) for first in range(0, slots, GROUP)]
    copies = [pltpu.make_async_copy(tiles.at[c], buffer.at[c], sems.at[i]) for i, c in enumerate(chunks)]
    for copy in copies:
        copy.start()

    @pl.loop(0, 16)
    def _(d):
        seen[d] = 0

    @pl.loop(0, keys)
    def _(k):
        mine[k] = 0
        mine[keys + k] = blocks
        mine[2 * keys + k] = 0

    @pl.loop(0, count[0])
    def _(s):
        source = lax.div(cols[s], blocks)
        rank = seen[source]
        seen[source] = rank + 1
        key = source * cap + jnp.minimum(rank, cap - 1)
        mine[key] = s
        mine[keys + key] = rows[s]
        mine[2 * keys + key] = lax.rem(cols[s], blocks)

    lane = lax.broadcasted_iota(jnp.int32, note.shape, 1)
    wants = jnp.zeros(note.shape, jnp.int32)
    for k in range(keys):
        wants = jnp.where(lane == k, mine[2 * keys + k], wants)

    def add(s, acc):
        t = buffer[s].astype(jnp.float32)
        return acc + jnp.sum((t * t).reshape(tile // 8, 8, tile), axis=0)

    acc = jnp.zeros((8, tile), jnp.float32)
    for i, copy in enumerate(copies):
        copy.wait()
        acc = lax.fori_loop(i * GROUP, jnp.clip(count[0], i * GROUP, (i + 1) * GROUP), add, acc)
    note[...] = jnp.where(lane == SUM_AT, jnp.sum(acc), wants.astype(jnp.float32))


def plan(layout, blocks, rows, cols, count, tiles):
    return pl.pallas_call(
        functools.partial(plan_kernel, layout, blocks),
        out_shape=(
            jax.ShapeDtypeStruct((3 * 16 * layout.cap,), jnp.int32),
            jax.ShapeDtypeStruct((1, LANES), jnp.float32),
        ),
        in_specs=[SMEM] * 3 + [ANY],
        out_specs=(SMEM, VMEM),
        scratch_shapes=[
            pltpu.SMEM((16,), jnp.int32),
            pltpu.VMEM(tiles.shape, tiles.dtype),
            pltpu.SemaphoreType.DMA((tiles.shape[0] // GROUP,)),
        ],
        compiler_params=params(59 * 2**20),
        cost_estimate=pl.CostEstimate(flops=0, bytes_accessed=0, transcendentals=0),
    )(rows, cols, count, tiles)


def fill_table(layout, mine, notes, table):
    cap = layout.cap
    keys = 16 * cap
    _, yc, _, zs = whereabouts()
    for j in range(4):
        for flip, asked in enumerate(notes, 1):
            for r in range(cap):
                table[layout.pack(j, flip) + r] = asked[0, (zs[j] * 4 + yc) * cap + r].astype(jnp.int32)
    for i, (j, flip) in enumerate(EARLY + LATE):
        for r in range(cap):
            key = (zs[j] * 4 + (yc ^ flip)) * cap + r
            at = layout.entry(i * cap + r)
            table[at] = mine[key]
            table[at + 1] = mine[keys + key]
            table[at + 2] = mine[2 * keys + key]


def start_kernel(layout, mine, note1, note2, note3, own, first, table, out2, out3):
    fill_table(layout, mine, (note1, note2, note3), table)
    other_y_kernel(layout, (0, 1), table, own, first, out2, out3)


def start(layout, mine, notes, own, first):
    _, tile, repl = own.shape
    packs = jax.ShapeDtypeStruct((2 * layout.cap, tile, repl), jnp.bfloat16)
    return pl.pallas_call(
        functools.partial(start_kernel, layout),
        out_shape=(jax.ShapeDtypeStruct((layout.size,), jnp.int32), packs, packs),
        in_specs=[SMEM] * 4 + [VMEM] * 2,
        out_specs=(SMEM, VMEM, VMEM),
        compiler_params=params(),
        cost_estimate=pl.CostEstimate(flops=0, bytes_accessed=0, transcendentals=0),
    )(mine, *notes, own, first)


def copy_asked(layout, table, j, flip, shard, out, first=0):
    at = layout.pack(j, flip)
    for r in range(layout.cap):
        out[first + r] = shard[table[at + r]]


def copy_part(cap, source, part, out, first):
    for r in range(cap):
        out[first + r] = source[part * cap + r]


def by_place(mid, out, use):
    inner = whereabouts()[2]
    pl.when(inner)(lambda: use(mid))
    pl.when(jnp.logical_not(inner))(lambda: use(out))


def other_y_kernel(layout, js, table, *refs):
    shards, outs = refs[:-2], refs[-2:]
    for i, (j, shard) in enumerate(zip(js, shards)):
        for flip in (2, 3):
            copy_asked(layout, table, j, flip, shard, outs[flip - 2], i * layout.cap)


def second_kernel(layout, js, table, *refs):
    shards, (out2, out3, core) = refs[:-3], refs[-3:]
    other_y_kernel(layout, (2,), table, shards[-1], out2, out3)
    for i, (j, shard) in enumerate(zip(js, shards)):
        copy_asked(layout, table, j, 1, shard, core, i * layout.cap)


def third_kernel(layout, table, mid, out, out2, out3, core):
    def use(shard):
        other_y_kernel(layout, (3,), table, shard, out2, out3)
        copy_asked(layout, table, 3, 1, shard, core)

    by_place(mid, out, use)


def pack(kernel, sizes, table, arrays, after=()):
    _, tile, repl = arrays[0].shape
    first_out = 1 + len(arrays) + len(after)

    def picked(*refs):
        kernel(*refs[: 1 + len(arrays)], *refs[first_out:])

    return pl.pallas_call(
        picked,
        out_shape=[jax.ShapeDtypeStruct((size, tile, repl), jnp.bfloat16) for size in sizes],
        in_specs=[SMEM] + [VMEM] * len(arrays) + [ANY] * len(after),
        out_specs=[VMEM] * len(sizes),
        compiler_params=params(),
        cost_estimate=pl.CostEstimate(flops=0, bytes_accessed=0, transcendentals=0),
    )(table, *arrays, *after)


def multiply(layout, table, tiles, blocks, first, field):
    prods = [
        jnp.dot(tiles[table[layout.entry(first + i)]], block, preferred_element_type=jnp.float32)
        for i, block in enumerate(blocks)
    ]
    for i, prod in enumerate(prods):
        field[table[layout.entry(first + i) + 1]] += prod


def take_own(layout, table, entry, shard, xbuf, place):
    for r in range(layout.cap):
        xbuf[place + r] = shard[table[layout.entry(entry + r) + 2]]


def early_kernel(layout, parts, table, tiles, own, first, second, mid, out, core, core3, *refs):
    cap = layout.cap
    field, xbuf = refs[-2:]
    for j, shard in enumerate((own, first, second)):
        base = 4 * cap * j
        take_own(layout, table, base, shard, xbuf, base)
        if core.shape[0] == 3 * cap:
            copy_part(cap, core, j, xbuf, base + cap)
        elif j == 0:
            copy_part(cap, refs[-3], 0, xbuf, base + cap)
        else:
            copy_part(cap, core, j - 1, xbuf, base + cap)
        ref, part = parts[j]
        copy_part(cap, refs[ref], part, xbuf, base + 2 * cap)
        copy_part(cap, refs[ref + 1], part, xbuf, base + 3 * cap)
    by_place(mid, out, lambda shard: take_own(layout, table, 12 * cap, shard, xbuf, 12 * cap))
    copy_part(cap, core3, 0, xbuf, 13 * cap)
    field[...] = jnp.zeros_like(field)

    @pl.loop(0, len(EARLY) * cap // GROUP)
    def _(g):
        multiply(layout, table, tiles, [xbuf[g * GROUP + i] for i in range(GROUP)], g * GROUP, field)


def early(layout, parts, table, tiles, arrays):
    tile = tiles.shape[1]
    blocks, _, repl = arrays[0].shape
    return pl.pallas_call(
        functools.partial(early_kernel, layout, parts),
        out_shape=jax.ShapeDtypeStruct((blocks + 1, tile, repl), jnp.float32),
        in_specs=[SMEM] + [VMEM] * (1 + len(arrays)),
        out_specs=VMEM,
        scratch_shapes=[pltpu.VMEM((len(EARLY) * layout.cap, tile, repl), jnp.bfloat16)],
        compiler_params=params(),
        cost_estimate=pl.CostEstimate(flops=0, bytes_accessed=0, transcendentals=0),
    )(table, tiles, *arrays)


def late_kernel(layout, last, table, scalars, tiles, got2, got3, field, xpos, ymom, *refs):
    cap = layout.cap
    blocks, _, repl = xpos.shape
    outs, acc = (refs[:3], refs[3]) if last else (refs[:6], refs[6])
    xout, yout = outs[:2]
    acc[...] = field[...]
    multiply(layout, table, tiles, [ref[r] for ref in (got2, got3) for r in range(cap)], len(EARLY) * cap, acc)
    if last:
        xnew, ynew, sems = refs[4:]
    else:
        xnew, ynew = xout, yout
    total = jnp.zeros((1, repl), jnp.float32)
    copies = []
    for b in range(blocks):
        x, h = xpos[b], acc[b]
        if last:
            total += jnp.sum(x * h, axis=0, keepdims=True)
        x, y = update(scalars[0], scalars[1], h, x, ymom[b])
        xnew[b] = x
        ynew[b] = y
        if last:
            copies.append(pltpu.make_async_copy(xnew.at[b], xout.at[b], sems.at[0, b]))
            copies.append(pltpu.make_async_copy(ynew.at[b], yout.at[b], sems.at[1, b]))
            copies[-2].start()
            copies[-1].start()
        else:
            outs[2][b] = x.astype(jnp.bfloat16)
    if last:
        outs[2][...] = -0.5 * total
        for copy in copies:
            copy.wait()
    else:
        other_y_kernel(layout, (0,), table, *outs[2:5])
        copy_asked(layout, table, 0, 1, outs[2], outs[5])


def late(layout, last, table, scalars, tiles, sources, field, xpos, ymom):
    tile = tiles.shape[1]
    blocks, _, repl = xpos.shape
    entries = len(LATE) * layout.cap
    state = jax.ShapeDtypeStruct(xpos.shape, jnp.float32)
    scratch = [pltpu.VMEM((blocks + 1, tile, repl), jnp.float32)]
    if last:
        extra = (jax.ShapeDtypeStruct((1, repl), jnp.float32),)
        scratch += [pltpu.VMEM(xpos.shape, jnp.float32)] * 2 + [pltpu.SemaphoreType.DMA((2, blocks))]
    else:
        out = jax.ShapeDtypeStruct((layout.cap, tile, repl), jnp.bfloat16)
        extra = (jax.ShapeDtypeStruct(xpos.shape, jnp.bfloat16), out, out, out)
    return pl.pallas_call(
        functools.partial(late_kernel, layout, last),
        out_shape=(state, state) + extra,
        in_specs=[SMEM, SMEM] + [VMEM] * (1 + len(sources) + 3),
        out_specs=((ANY, ANY) if last else (VMEM, VMEM)) + (VMEM,) * len(extra),
        scratch_shapes=scratch,
        compiler_params=params(),
        cost_estimate=pl.CostEstimate(
            flops=2 * entries * tile * tile * repl,
            bytes_accessed=entries * tile * (tile + repl) * 2 + 20 * xpos.size,
            transcendentals=0,
        ),
    )(table, scalars, tiles, *sources, field, xpos, ymom)


def along_z(pairs, value):
    return lax.ppermute(value, "row", [(a * 4 + i, b * 4 + i) for a, b in pairs for i in range(4)])


def across(flip, value):
    return lax.ppermute(value, "row", [(i, i ^ flip) for i in range(16)])


def row_sum(part):
    devices = lax.axis_size("row")
    spread = jnp.broadcast_to(part, (devices,) + part.shape[1:])
    return jnp.sum(lax.all_to_all(spread, "row", split_axis=0, concat_axis=0, tiled=True), axis=0, keepdims=True)


def body_16(tiles, tile_rows, tile_cols, counts, positions, momenta):
    slots, tile, _ = tiles.shape
    repl = positions.shape[1]
    blocks = positions.shape[0] // tile
    cap = (slots + 15) // 16
    order = blocks * tile * 16
    layout = Layout(cap)

    def other_y(js, shards):
        kernel = functools.partial(other_y_kernel, layout, js)
        return pack(kernel, [len(js) * cap] * 2, table, shards)

    def to_other_y(packs):
        return [across(2, packs[0]), across(3, packs[1])]

    xpos = positions.reshape(blocks, tile, repl)
    ymom = momenta.reshape(blocks, tile, repl)
    own0 = xpos.astype(jnp.bfloat16)
    mine, note = plan(layout, blocks, tile_rows, tile_cols, counts, tiles)
    notes = [across(flip, note) for flip in (1, 2, 3)]
    packs0 = None
    for step in range(STEPS):
        last = step == STEPS - 1
        own1 = along_z(FIRST, own0)
        if step == 0:
            again, notes[0] = lax.optimization_barrier((own0, notes[0]))
            own2 = along_z(SECOND, again)
            again, notes = lax.optimization_barrier((again, notes))
            mid = along_z(MIDDLE, again)
            own1, notes = lax.optimization_barrier((own1, notes))
            out = along_z(OUTWARD, own1)
            table, *packs01 = start(layout, mine, notes, own0, own1)
            got1 = to_other_y(packs01)
            corner = touch(tiles, own2)
            own2, got1 = lax.optimization_barrier((own2, got1))
            parts, cores, after = ((0, 0), (0, 1), (2, 0)), [], [corner]
            got = got1
        else:
            core0 = across(1, packs0[2])
            again, core0 = lax.optimization_barrier((own0, core0))
            own2 = along_z(SECOND, again)
            got0 = to_other_y(packs0)
            again, got0 = lax.optimization_barrier((again, got0))
            own1, got0 = lax.optimization_barrier((own1, got0))
            packs1 = other_y((1,), [own1])
            out = along_z(OUTWARD, own1)
            got1 = to_other_y(packs1)
            mid = along_z(MIDDLE, again)
            own2, got1 = lax.optimization_barrier((own2, got1))
            parts, cores, after = ((0, 0), (2, 0), (4, 0)), [core0], []
            got = got0 + got1
        js, shards = ((0, 1, 2), [own0, own1, own2]) if step == 0 else ((1, 2), [own1, own2])
        packs2 = pack(functools.partial(second_kernel, layout, js), [cap, cap, len(js) * cap], table, shards, after)
        got2 = to_other_y(packs2)
        core = across(1, packs2[2])
        packs3 = pack(functools.partial(third_kernel, layout), [cap] * 3, table, [mid, out])
        if step == 0:
            note, packs3 = lax.optimization_barrier((note, packs3))
            plane = note + notes[0] + notes[1] + notes[2]
            half = plane + across(4, plane)
        core3 = across(1, packs3[2])
        got3 = to_other_y(packs3)
        if step == 0:
            got2, half = lax.optimization_barrier((got2, half))
        field = early(layout, parts, table, tiles, [own0, own1, own2, mid, out, core, core3] + got + got2 + cores)
        if step == 0:
            total = (half + across(8, half))[0, SUM_AT]
            coeff = 0.7 * jnp.sqrt((order - 1) / total)
        scalars = jnp.stack([jnp.float32(0.4 - 0.1 * step), coeff])
        outs = late(layout, last, table, scalars, tiles, got3, field, xpos, ymom)
        xpos, ymom = outs[0], outs[1]
        if not last:
            own0, packs0 = outs[2], outs[3:]
    energy = row_sum(outs[2])
    return (xpos.reshape(positions.shape), ymom.reshape(momenta.shape), energy.reshape(repl))


def touch_kernel(tiles, own, out):
    out[...] = tiles[0, :8, :128]


def touch(tiles, own):
    return pl.pallas_call(
        touch_kernel,
        out_shape=jax.ShapeDtypeStruct((8, 128), tiles.dtype),
        in_specs=[VMEM, ANY],
        out_specs=VMEM,
        compiler_params=params(),
        cost_estimate=pl.CostEstimate(flops=0, bytes_accessed=0, transcendentals=0),
    )(tiles, own)


def gathered_kernel(last, rows, cols, count, scalars, tiles, gathered, xpos, ymom, xout, yout, extra, xbuf, field, xsem):
    tile = xbuf.shape[1]
    used = count[0]

    def block_copy(s):
        return pltpu.make_async_copy(gathered.at[cols[s]], xbuf.at[s], xsem.at[s])

    @pl.loop(0, used)
    def _(s):
        block_copy(s).start()

    field[...] = jnp.zeros_like(field)

    @pl.loop(0, used)
    def _(s):
        block_copy(s).wait()
        here = pl.ds(pl.multiple_of(rows[s] * tile, tile), tile)
        field[here, :] += jnp.dot(tiles[s], xbuf[s], preferred_element_type=jnp.float32)

    x, h = xpos[...], field[...]
    if last:
        extra[...] = -0.5 * jnp.sum(x * h, axis=0, keepdims=True)
    x, y = update(scalars[0], scalars[1], h, x, ymom[...])
    xout[...] = x
    yout[...] = y
    if not last:
        extra[...] = x.astype(jnp.bfloat16)


def body_any(tiles, tile_rows, tile_cols, counts, positions, momenta):
    slots, tile, _ = tiles.shape
    order, repl = positions.shape
    devices = lax.axis_size("row")
    state = jax.ShapeDtypeStruct(positions.shape, jnp.float32)
    total = jnp.sum(lax.psum(squares(counts, tiles), "row"))
    coeff = 0.7 * jnp.sqrt((order * devices - 1) / total)
    xpos, ymom, extra = positions, momenta, positions.astype(jnp.bfloat16)
    for step in range(STEPS):
        last = step == STEPS - 1
        gathered = lax.all_gather(extra, "row", tiled=True).reshape(-1, tile, repl)
        scalars = jnp.stack([jnp.float32(0.4 - 0.1 * step), coeff])
        xpos, ymom, extra = pl.pallas_call(
            functools.partial(gathered_kernel, last),
            out_shape=(
                state,
                state,
                jax.ShapeDtypeStruct((1, repl), jnp.float32) if last else jax.ShapeDtypeStruct(state.shape, jnp.bfloat16),
            ),
            in_specs=[SMEM] * 4 + [VMEM, ANY, VMEM, VMEM],
            out_specs=(VMEM,) * 3,
            scratch_shapes=[
                pltpu.VMEM((slots, tile, repl), jnp.bfloat16),
                pltpu.VMEM(positions.shape, jnp.float32),
                pltpu.SemaphoreType.DMA((slots,)),
            ],
            compiler_params=params(),
        )(tile_rows, tile_cols, counts, scalars, tiles, gathered, xpos, ymom)
    return (xpos, ymom, lax.psum(extra, "row").reshape(repl))


def solution(mesh):
    in_specs = (
        P(("groups", "row"), None, None),
        P(("groups", "row")),
        P(("groups", "row")),
        P(("groups", "row")),
        P(("groups", "row"), None),
        P(("groups", "row"), None),
    )
    out_specs = (P(("groups", "row"), None), P(("groups", "row"), None), P("groups"))

    def body(tiles, *args):
        slots = tiles.shape[0]
        by_hand = mesh.shape["row"] == 16 and slots % GROUP == 0 and slots <= 96
        return (body_16 if by_hand else body_any)(tiles, *args)

    return jax.shard_map(body, mesh=mesh, in_specs=in_specs, out_specs=out_specs, check_vma=False)
```

```python
import functools

import jax
import jax.numpy as jnp
from jax import lax
from jax.experimental import pallas as pl
from jax.experimental.pallas import tpu as pltpu
from jax.sharding import PartitionSpec as P

STEPS = 4
GROUP = 6
LANES = 128
SUM_AT = LANES - 1
LIMIT = 16 * 2**20

SMEM = pl.BlockSpec(memory_space=pltpu.SMEM)
VMEM = pl.BlockSpec(memory_space=pltpu.VMEM)
ANY = pl.BlockSpec(memory_space=pl.ANY)


def params(limit=LIMIT):
    return pltpu.CompilerParams(vmem_limit_bytes=limit)


def squares_kernel(count, tiles, out):
    tile = tiles.shape[1]

    def add(s, acc):
        t = tiles[s].astype(jnp.float32)
        return acc + jnp.sum((t * t).reshape(tile // 8, 8, tile), axis=0)

    acc = lax.fori_loop(0, count[0], add, jnp.zeros((8, tile), jnp.float32))
    acc = jnp.sum(acc, axis=0, keepdims=True)
    out[...] = sum(acc[:, i : i + 128] for i in range(0, tile, 128))


def squares(count, tiles):
    return pl.pallas_call(
        squares_kernel,
        out_shape=jax.ShapeDtypeStruct((1, 128), jnp.float32),
        in_specs=[SMEM, VMEM],
        out_specs=VMEM,
        compiler_params=params(),
        cost_estimate=pl.CostEstimate(flops=2 * tiles.size, bytes_accessed=2 * tiles.size, transcendentals=0),
    )(count, tiles)


def update(pump, coeff, h, x, y):
    y = y + 0.5 * (-(x * x + pump) * x + coeff * h)
    return x + 0.5 * y, y


FIRST = ((0, 2), (3, 1), (1, 0), (2, 3))
SECOND = ((0, 1), (3, 2), (1, 3), (2, 0))
OUTWARD = ((1, 0), (2, 3))
MIDDLE = ((1, 2), (2, 1))


class Layout:
    def __init__(self, cap):
        self.cap = cap
        self.packs = 0
        self.entries = 12 * cap
        self.size = 12 * cap + 3 * 16 * cap

    def pack(self, j, flip):
        return self.packs + (j * 3 + flip - 1) * self.cap

    def entry(self, i):
        return self.entries + 3 * i


def whereabouts():
    me = lax.axis_index("row")
    z, yc = lax.div(me, 4), lax.rem(me, 4)
    inner = (z == 1) | (z == 2)
    near, skip = z ^ 1, z ^ 2
    return z, yc, inner, (z, jnp.where(inner, skip, near), jnp.where(inner, near, skip), z ^ 3)


EARLY = tuple((j, flip) for j in range(3) for flip in range(4)) + ((3, 0), (3, 1))
LATE = ((3, 2), (3, 3))


def plan_kernel(layout, blocks, rows, cols, count, tiles, mine, note, seen, buffer, sems):
    cap = layout.cap
    keys = 16 * cap
    slots, tile, _ = buffer.shape
    chunks = [pl.ds(first, GROUP) for first in range(0, slots, GROUP)]
    copies = [pltpu.make_async_copy(tiles.at[c], buffer.at[c], sems.at[i]) for i, c in enumerate(chunks)]
    for copy in copies:
        copy.start()

    @pl.loop(0, 16)
    def _(d):
        seen[d] = 0

    @pl.loop(0, keys)
    def _(k):
        mine[k] = 0
        mine[keys + k] = blocks
        mine[2 * keys + k] = 0

    @pl.loop(0, count[0])
    def _(s):
        source = lax.div(cols[s], blocks)
        rank = seen[source]
        seen[source] = rank + 1
        key = source * cap + jnp.minimum(rank, cap - 1)
        mine[key] = s
        mine[keys + key] = rows[s]
        mine[2 * keys + key] = lax.rem(cols[s], blocks)

    lane = lax.broadcasted_iota(jnp.int32, note.shape, 1)
    wants = jnp.zeros(note.shape, jnp.int32)
    for k in range(keys):
        wants = jnp.where(lane == k, mine[2 * keys + k], wants)

    def add(s, acc):
        t = buffer[s].astype(jnp.float32)
        return acc + jnp.sum((t * t).reshape(tile // 8, 8, tile), axis=0)

    acc = jnp.zeros((8, tile), jnp.float32)
    for i, copy in enumerate(copies):
        copy.wait()
        acc = lax.fori_loop(i * GROUP, jnp.clip(count[0], i * GROUP, (i + 1) * GROUP), add, acc)
    note[...] = jnp.where(lane == SUM_AT, jnp.sum(acc), wants.astype(jnp.float32))


def plan(layout, blocks, rows, cols, count, tiles):
    return pl.pallas_call(
        functools.partial(plan_kernel, layout, blocks),
        out_shape=(
            jax.ShapeDtypeStruct((3 * 16 * layout.cap,), jnp.int32),
            jax.ShapeDtypeStruct((1, LANES), jnp.float32),
        ),
        in_specs=[SMEM] * 3 + [ANY],
        out_specs=(SMEM, VMEM),
        scratch_shapes=[
            pltpu.SMEM((16,), jnp.int32),
            pltpu.VMEM(tiles.shape, tiles.dtype),
            pltpu.SemaphoreType.DMA((tiles.shape[0] // GROUP,)),
        ],
        compiler_params=params(59 * 2**20),
        cost_estimate=pl.CostEstimate(flops=0, bytes_accessed=0, transcendentals=0),
    )(rows, cols, count, tiles)


def fill_table(layout, mine, notes, table):
    cap = layout.cap
    keys = 16 * cap
    _, yc, _, zs = whereabouts()
    for j in range(4):
        for flip, asked in enumerate(notes, 1):
            for r in range(cap):
                table[layout.pack(j, flip) + r] = asked[0, (zs[j] * 4 + yc) * cap + r].astype(jnp.int32)
    for i, (j, flip) in enumerate(EARLY + LATE):
        for r in range(cap):
            key = (zs[j] * 4 + (yc ^ flip)) * cap + r
            at = layout.entry(i * cap + r)
            table[at] = mine[key]
            table[at + 1] = mine[keys + key]
            table[at + 2] = mine[2 * keys + key]


def start_kernel(layout, mine, note1, note2, note3, own, first, table, out2, out3):
    fill_table(layout, mine, (note1, note2, note3), table)
    other_y_kernel(layout, (0, 1), table, own, first, out2, out3)


def start(layout, mine, notes, own, first):
    _, tile, repl = own.shape
    packs = jax.ShapeDtypeStruct((2 * layout.cap, tile, repl), jnp.bfloat16)
    return pl.pallas_call(
        functools.partial(start_kernel, layout),
        out_shape=(jax.ShapeDtypeStruct((layout.size,), jnp.int32), packs, packs),
        in_specs=[SMEM] * 4 + [VMEM] * 2,
        out_specs=(SMEM, VMEM, VMEM),
        compiler_params=params(),
        cost_estimate=pl.CostEstimate(flops=0, bytes_accessed=0, transcendentals=0),
    )(mine, *notes, own, first)


def copy_asked(layout, table, j, flip, shard, out, first=0):
    at = layout.pack(j, flip)
    for r in range(layout.cap):
        out[first + r] = shard[table[at + r]]


def copy_part(cap, source, part, out, first):
    for r in range(cap):
        out[first + r] = source[part * cap + r]


def by_place(mid, out, use):
    inner = whereabouts()[2]
    pl.when(inner)(lambda: use(mid))
    pl.when(jnp.logical_not(inner))(lambda: use(out))


def other_y_kernel(layout, js, table, *refs):
    shards, outs = refs[:-2], refs[-2:]
    for i, (j, shard) in enumerate(zip(js, shards)):
        for flip in (2, 3):
            copy_asked(layout, table, j, flip, shard, outs[flip - 2], i * layout.cap)


def second_kernel(layout, js, table, *refs):
    shards, (out2, out3, core) = refs[:-3], refs[-3:]
    other_y_kernel(layout, (2,), table, shards[-1], out2, out3)
    for i, (j, shard) in enumerate(zip(js, shards)):
        copy_asked(layout, table, j, 1, shard, core, i * layout.cap)


def third_kernel(layout, table, mid, out, out2, out3, core):
    def use(shard):
        other_y_kernel(layout, (3,), table, shard, out2, out3)
        copy_asked(layout, table, 3, 1, shard, core)

    by_place(mid, out, use)


def pack(kernel, sizes, table, arrays, after=()):
    _, tile, repl = arrays[0].shape
    first_out = 1 + len(arrays) + len(after)

    def picked(*refs):
        kernel(*refs[: 1 + len(arrays)], *refs[first_out:])

    return pl.pallas_call(
        picked,
        out_shape=[jax.ShapeDtypeStruct((size, tile, repl), jnp.bfloat16) for size in sizes],
        in_specs=[SMEM] + [VMEM] * len(arrays) + [ANY] * len(after),
        out_specs=[VMEM] * len(sizes),
        compiler_params=params(),
        cost_estimate=pl.CostEstimate(flops=0, bytes_accessed=0, transcendentals=0),
    )(table, *arrays, *after)


def multiply(layout, table, tiles, blocks, first, field):
    prods = [
        jnp.dot(tiles[table[layout.entry(first + i)]], block, preferred_element_type=jnp.float32)
        for i, block in enumerate(blocks)
    ]
    for i, prod in enumerate(prods):
        field[table[layout.entry(first + i) + 1]] += prod


def take_own(layout, table, entry, shard, xbuf, place):
    for r in range(layout.cap):
        xbuf[place + r] = shard[table[layout.entry(entry + r) + 2]]


def early_kernel(layout, parts, table, tiles, own, first, second, mid, out, core, core3, *refs):
    cap = layout.cap
    field, xbuf = refs[-2:]
    for j, shard in enumerate((own, first, second)):
        base = 4 * cap * j
        take_own(layout, table, base, shard, xbuf, base)
        if core.shape[0] == 3 * cap:
            copy_part(cap, core, j, xbuf, base + cap)
        elif j == 0:
            copy_part(cap, refs[-3], 0, xbuf, base + cap)
        else:
            copy_part(cap, core, j - 1, xbuf, base + cap)
        ref, part = parts[j]
        copy_part(cap, refs[ref], part, xbuf, base + 2 * cap)
        copy_part(cap, refs[ref + 1], part, xbuf, base + 3 * cap)
    by_place(mid, out, lambda shard: take_own(layout, table, 12 * cap, shard, xbuf, 12 * cap))
    copy_part(cap, core3, 0, xbuf, 13 * cap)
    field[...] = jnp.zeros_like(field)

    @pl.loop(0, len(EARLY) * cap // GROUP)
    def _(g):
        multiply(layout, table, tiles, [xbuf[g * GROUP + i] for i in range(GROUP)], g * GROUP, field)


def early(layout, parts, table, tiles, arrays):
    tile = tiles.shape[1]
    blocks, _, repl = arrays[0].shape
    return pl.pallas_call(
        functools.partial(early_kernel, layout, parts),
        out_shape=jax.ShapeDtypeStruct((blocks + 1, tile, repl), jnp.float32),
        in_specs=[SMEM] + [VMEM] * (1 + len(arrays)),
        out_specs=VMEM,
        scratch_shapes=[pltpu.VMEM((len(EARLY) * layout.cap, tile, repl), jnp.bfloat16)],
        compiler_params=params(),
        cost_estimate=pl.CostEstimate(flops=0, bytes_accessed=0, transcendentals=0),
    )(table, tiles, *arrays)


def late_field(layout, table, tiles, got2, got3, field, acc):
    cap = layout.cap
    acc[...] = field[...]
    multiply(layout, table, tiles, [ref[r] for ref in (got2, got3) for r in range(cap)], len(EARLY) * cap, acc)


def late_kernel(layout, table, scalars, tiles, got2, got3, field, xpos, ymom, xout, yout, xb, out2, out3, core, acc):
    late_field(layout, table, tiles, got2, got3, field, acc)
    for b in range(xpos.shape[0]):
        x, y = update(scalars[0], scalars[1], acc[b], xpos[b], ymom[b])
        xout[b] = x
        yout[b] = y
        xb[b] = x.astype(jnp.bfloat16)
    other_y_kernel(layout, (0,), table, xb, out2, out3)
    copy_asked(layout, table, 0, 1, xb, core)


def late(layout, table, scalars, tiles, sources, field, xpos, ymom):
    tile = tiles.shape[1]
    blocks, _, repl = xpos.shape
    entries = len(LATE) * layout.cap
    state = jax.ShapeDtypeStruct(xpos.shape, jnp.float32)
    out = jax.ShapeDtypeStruct((layout.cap, tile, repl), jnp.bfloat16)
    return pl.pallas_call(
        functools.partial(late_kernel, layout),
        out_shape=(state, state, jax.ShapeDtypeStruct(xpos.shape, jnp.bfloat16), out, out, out),
        in_specs=[SMEM, SMEM] + [VMEM] * (1 + len(sources) + 3),
        out_specs=(VMEM,) * 6,
        scratch_shapes=[pltpu.VMEM((blocks + 1, tile, repl), jnp.float32)],
        compiler_params=params(),
        cost_estimate=pl.CostEstimate(
            flops=2 * entries * tile * tile * repl,
            bytes_accessed=entries * tile * (tile + repl) * 2 + 20 * xpos.size,
            transcendentals=0,
        ),
    )(table, scalars, tiles, *sources, field, xpos, ymom)


def energy_kernel(layout, table, tiles, got2, got3, field, xpos, energy, acc):
    late_field(layout, table, tiles, got2, got3, field, acc)
    total = jnp.zeros(xpos.shape[1:], jnp.float32)
    for b in range(xpos.shape[0]):
        total += xpos[b] * acc[b]
    energy[...] = -0.5 * jnp.sum(total, axis=0, keepdims=True)


def last_field(layout, table, tiles, sources, field, xpos):
    return pl.pallas_call(
        functools.partial(energy_kernel, layout),
        out_shape=(
            jax.ShapeDtypeStruct((1, xpos.shape[2]), jnp.float32),
            jax.ShapeDtypeStruct(field.shape, jnp.float32),
        ),
        in_specs=[SMEM] + [VMEM] * (1 + len(sources) + 2),
        out_specs=(VMEM, VMEM),
        compiler_params=params(),
        cost_estimate=pl.CostEstimate(flops=0, bytes_accessed=0, transcendentals=0),
    )(table, tiles, *sources, field, xpos)


def update_kernel(scalars, field, xpos, ymom, xout, yout, xnew, ynew, sems):
    copies = []
    for b in range(xpos.shape[0]):
        x, y = update(scalars[0], scalars[1], field[b], xpos[b], ymom[b])
        xnew[b] = x
        ynew[b] = y
        for i, (new, out) in enumerate(((xnew, xout), (ynew, yout))):
            copies.append(pltpu.make_async_copy(new.at[b], out.at[b], sems.at[i, b]))
            copies[-1].start()
    for copy in copies:
        copy.wait()


def last_update(scalars, field, xpos, ymom):
    state = jax.ShapeDtypeStruct(xpos.shape, jnp.float32)
    return pl.pallas_call(
        update_kernel,
        out_shape=(state, state),
        in_specs=[SMEM] + [VMEM] * 3,
        out_specs=(ANY, ANY),
        scratch_shapes=[pltpu.VMEM(xpos.shape, jnp.float32)] * 2 + [pltpu.SemaphoreType.DMA((2, xpos.shape[0]))],
        compiler_params=params(),
        cost_estimate=pl.CostEstimate(flops=10 * xpos.size, bytes_accessed=20 * xpos.size, transcendentals=0),
    )(scalars, field, xpos, ymom)


def along_z(pairs, value):
    return lax.ppermute(value, "row", [(a * 4 + i, b * 4 + i) for a, b in pairs for i in range(4)])


def across(flip, value):
    return lax.ppermute(value, "row", [(i, i ^ flip) for i in range(16)])


def row_sum(part):
    devices = lax.axis_size("row")
    spread = jnp.broadcast_to(part, (devices,) + part.shape[1:])
    return jnp.sum(lax.all_to_all(spread, "row", split_axis=0, concat_axis=0, tiled=True), axis=0, keepdims=True)


def body_16(tiles, tile_rows, tile_cols, counts, positions, momenta):
    slots, tile, _ = tiles.shape
    repl = positions.shape[1]
    blocks = positions.shape[0] // tile
    cap = (slots + 15) // 16
    order = blocks * tile * 16
    layout = Layout(cap)

    def other_y(js, shards):
        kernel = functools.partial(other_y_kernel, layout, js)
        return pack(kernel, [len(js) * cap] * 2, table, shards)

    def to_other_y(packs):
        return [across(2, packs[0]), across(3, packs[1])]

    xpos = positions.reshape(blocks, tile, repl)
    ymom = momenta.reshape(blocks, tile, repl)
    own0 = xpos.astype(jnp.bfloat16)
    mine, note = plan(layout, blocks, tile_rows, tile_cols, counts, tiles)
    notes = [across(flip, note) for flip in (1, 2, 3)]
    packs0 = None
    for step in range(STEPS):
        last = step == STEPS - 1
        own1 = along_z(FIRST, own0)
        if step == 0:
            again, notes[0] = lax.optimization_barrier((own0, notes[0]))
            own2 = along_z(SECOND, again)
            again, notes = lax.optimization_barrier((again, notes))
            mid = along_z(MIDDLE, again)
            own1, notes = lax.optimization_barrier((own1, notes))
            out = along_z(OUTWARD, own1)
            table, *packs01 = start(layout, mine, notes, own0, own1)
            got1 = to_other_y(packs01)
            corner = touch(tiles, own2)
            own2, got1 = lax.optimization_barrier((own2, got1))
            parts, cores, after = ((0, 0), (0, 1), (2, 0)), [], [corner]
            got = got1
        else:
            core0 = across(1, packs0[2])
            again, core0 = lax.optimization_barrier((own0, core0))
            own2 = along_z(SECOND, again)
            got0 = to_other_y(packs0)
            again, got0 = lax.optimization_barrier((again, got0))
            own1, got0 = lax.optimization_barrier((own1, got0))
            packs1 = other_y((1,), [own1])
            out = along_z(OUTWARD, own1)
            got1 = to_other_y(packs1)
            mid = along_z(MIDDLE, again)
            own2, got1 = lax.optimization_barrier((own2, got1))
            parts, cores, after = ((0, 0), (2, 0), (4, 0)), [core0], []
            got = got0 + got1
        js, shards = ((0, 1, 2), [own0, own1, own2]) if step == 0 else ((1, 2), [own1, own2])
        packs2 = pack(functools.partial(second_kernel, layout, js), [cap, cap, len(js) * cap], table, shards, after)
        got2 = to_other_y(packs2)
        core = across(1, packs2[2])
        packs3 = pack(functools.partial(third_kernel, layout), [cap] * 3, table, [mid, out])
        if step == 0:
            note, packs3 = lax.optimization_barrier((note, packs3))
            plane = note + notes[0] + notes[1] + notes[2]
            half = plane + across(4, plane)
        core3 = across(1, packs3[2])
        got3 = to_other_y(packs3)
        if step == 0:
            got2, half = lax.optimization_barrier((got2, half))
        field = early(layout, parts, table, tiles, [own0, own1, own2, mid, out, core, core3] + got + got2 + cores)
        if step == 0:
            total = (half + across(8, half))[0, SUM_AT]
            coeff = 0.7 * jnp.sqrt((order - 1) / total)
        scalars = jnp.stack([jnp.float32(0.4 - 0.1 * step), coeff])
        if last:
            part, field = last_field(layout, table, tiles, got3, field, xpos)
            energy = row_sum(part)
            xpos, ymom = last_update(scalars, field, xpos, ymom)
        else:
            xpos, ymom, own0, *packs0 = late(layout, table, scalars, tiles, got3, field, xpos, ymom)
    return (xpos.reshape(positions.shape), ymom.reshape(momenta.shape), energy.reshape(repl))


def touch_kernel(tiles, own, out):
    out[...] = tiles[0, :8, :128]


def touch(tiles, own):
    return pl.pallas_call(
        touch_kernel,
        out_shape=jax.ShapeDtypeStruct((8, 128), tiles.dtype),
        in_specs=[VMEM, ANY],
        out_specs=VMEM,
        compiler_params=params(),
        cost_estimate=pl.CostEstimate(flops=0, bytes_accessed=0, transcendentals=0),
    )(tiles, own)


def gathered_kernel(last, rows, cols, count, scalars, tiles, gathered, xpos, ymom, xout, yout, extra, xbuf, field, xsem):
    tile = xbuf.shape[1]
    used = count[0]

    def block_copy(s):
        return pltpu.make_async_copy(gathered.at[cols[s]], xbuf.at[s], xsem.at[s])

    @pl.loop(0, used)
    def _(s):
        block_copy(s).start()

    field[...] = jnp.zeros_like(field)

    @pl.loop(0, used)
    def _(s):
        block_copy(s).wait()
        here = pl.ds(pl.multiple_of(rows[s] * tile, tile), tile)
        field[here, :] += jnp.dot(tiles[s], xbuf[s], preferred_element_type=jnp.float32)

    x, h = xpos[...], field[...]
    if last:
        extra[...] = -0.5 * jnp.sum(x * h, axis=0, keepdims=True)
    x, y = update(scalars[0], scalars[1], h, x, ymom[...])
    xout[...] = x
    yout[...] = y
    if not last:
        extra[...] = x.astype(jnp.bfloat16)


def body_any(tiles, tile_rows, tile_cols, counts, positions, momenta):
    slots, tile, _ = tiles.shape
    order, repl = positions.shape
    devices = lax.axis_size("row")
    state = jax.ShapeDtypeStruct(positions.shape, jnp.float32)
    total = jnp.sum(lax.psum(squares(counts, tiles), "row"))
    coeff = 0.7 * jnp.sqrt((order * devices - 1) / total)
    xpos, ymom, extra = positions, momenta, positions.astype(jnp.bfloat16)
    for step in range(STEPS):
        last = step == STEPS - 1
        gathered = lax.all_gather(extra, "row", tiled=True).reshape(-1, tile, repl)
        scalars = jnp.stack([jnp.float32(0.4 - 0.1 * step), coeff])
        xpos, ymom, extra = pl.pallas_call(
            functools.partial(gathered_kernel, last),
            out_shape=(
                state,
                state,
                jax.ShapeDtypeStruct((1, repl), jnp.float32) if last else jax.ShapeDtypeStruct(state.shape, jnp.bfloat16),
            ),
            in_specs=[SMEM] * 4 + [VMEM, ANY, VMEM, VMEM],
            out_specs=(VMEM,) * 3,
            scratch_shapes=[
                pltpu.VMEM((slots, tile, repl), jnp.bfloat16),
                pltpu.VMEM(positions.shape, jnp.float32),
                pltpu.SemaphoreType.DMA((slots,)),
            ],
            compiler_params=params(),
        )(tile_rows, tile_cols, counts, scalars, tiles, gathered, xpos, ymom)
    return (xpos, ymom, lax.psum(extra, "row").reshape(repl))


def solution(mesh):
    in_specs = (
        P(("groups", "row"), None, None),
        P(("groups", "row")),
        P(("groups", "row")),
        P(("groups", "row")),
        P(("groups", "row"), None),
        P(("groups", "row"), None),
    )
    out_specs = (P(("groups", "row"), None), P(("groups", "row"), None), P("groups"))

    def body(tiles, *args):
        slots = tiles.shape[0]
        by_hand = mesh.shape["row"] == 16 and slots % GROUP == 0 and slots <= 96
        return (body_16 if by_hand else body_any)(tiles, *args)

    return jax.shard_map(body, mesh=mesh, in_specs=in_specs, out_specs=out_specs, check_vma=False)
```

```python
import functools

import jax
import jax.numpy as jnp
from jax import lax
from jax.experimental import pallas as pl
from jax.experimental.pallas import tpu as pltpu
from jax.sharding import PartitionSpec as P

STEPS = 4
GROUP = 6
LANES = 128
SUM_AT = LANES - 1
LIMIT = 16 * 2**20

SMEM = pl.BlockSpec(memory_space=pltpu.SMEM)
VMEM = pl.BlockSpec(memory_space=pltpu.VMEM)
ANY = pl.BlockSpec(memory_space=pl.ANY)


def params(limit=LIMIT):
    return pltpu.CompilerParams(vmem_limit_bytes=limit)


def squares_kernel(count, tiles, out):
    tile = tiles.shape[1]

    def add(s, acc):
        t = tiles[s].astype(jnp.float32)
        return acc + jnp.sum((t * t).reshape(tile // 8, 8, tile), axis=0)

    acc = lax.fori_loop(0, count[0], add, jnp.zeros((8, tile), jnp.float32))
    acc = jnp.sum(acc, axis=0, keepdims=True)
    out[...] = sum(acc[:, i : i + 128] for i in range(0, tile, 128))


def squares(count, tiles):
    return pl.pallas_call(
        squares_kernel,
        out_shape=jax.ShapeDtypeStruct((1, 128), jnp.float32),
        in_specs=[SMEM, VMEM],
        out_specs=VMEM,
        compiler_params=params(),
        cost_estimate=pl.CostEstimate(flops=2 * tiles.size, bytes_accessed=2 * tiles.size, transcendentals=0),
    )(count, tiles)


def update(pump, coeff, h, x, y):
    y = y + 0.5 * (-(x * x + pump) * x + coeff * h)
    return x + 0.5 * y, y


FIRST = ((0, 2), (3, 1), (1, 0), (2, 3))
SECOND = ((0, 1), (3, 2), (1, 3), (2, 0))
OUTWARD = ((1, 0), (2, 3))
MIDDLE = ((1, 2), (2, 1))


class Layout:
    def __init__(self, cap):
        self.cap = cap
        self.packs = 0
        self.entries = 12 * cap
        self.size = 12 * cap + 3 * 16 * cap

    def pack(self, j, flip):
        return self.packs + (j * 3 + flip - 1) * self.cap

    def entry(self, i):
        return self.entries + 3 * i


def whereabouts():
    me = lax.axis_index("row")
    z, yc = lax.div(me, 4), lax.rem(me, 4)
    inner = (z == 1) | (z == 2)
    near, skip = z ^ 1, z ^ 2
    return z, yc, inner, (z, jnp.where(inner, skip, near), jnp.where(inner, near, skip), z ^ 3)


EARLY = tuple((j, flip) for j in range(3) for flip in range(4)) + ((3, 0), (3, 1))
LATE = ((3, 2), (3, 3))


def plan_kernel(layout, blocks, rows, cols, count, tiles, mine, note, seen, buffer, sems):
    cap = layout.cap
    keys = 16 * cap
    slots, tile, _ = buffer.shape
    chunks = [pl.ds(first, GROUP) for first in range(0, slots, GROUP)]
    copies = [pltpu.make_async_copy(tiles.at[c], buffer.at[c], sems.at[i]) for i, c in enumerate(chunks)]
    for copy in copies:
        copy.start()

    @pl.loop(0, 16)
    def _(d):
        seen[d] = 0

    @pl.loop(0, keys)
    def _(k):
        mine[k] = 0
        mine[keys + k] = blocks
        mine[2 * keys + k] = 0

    @pl.loop(0, count[0])
    def _(s):
        source = lax.div(cols[s], blocks)
        rank = seen[source]
        seen[source] = rank + 1
        key = source * cap + jnp.minimum(rank, cap - 1)
        mine[key] = s
        mine[keys + key] = rows[s]
        mine[2 * keys + key] = lax.rem(cols[s], blocks)

    lane = lax.broadcasted_iota(jnp.int32, note.shape, 1)
    wants = jnp.zeros(note.shape, jnp.int32)
    for k in range(keys):
        wants = jnp.where(lane == k, mine[2 * keys + k], wants)

    def add(s, acc):
        t = buffer[s].astype(jnp.float32)
        return acc + jnp.sum((t * t).reshape(tile // 8, 8, tile), axis=0)

    acc = jnp.zeros((8, tile), jnp.float32)
    for i, copy in enumerate(copies):
        copy.wait()
        acc = lax.fori_loop(i * GROUP, jnp.clip(count[0], i * GROUP, (i + 1) * GROUP), add, acc)
    note[...] = jnp.where(lane == SUM_AT, jnp.sum(acc), wants.astype(jnp.float32))


def plan(layout, blocks, rows, cols, count, tiles):
    return pl.pallas_call(
        functools.partial(plan_kernel, layout, blocks),
        out_shape=(
            jax.ShapeDtypeStruct((3 * 16 * layout.cap,), jnp.int32),
            jax.ShapeDtypeStruct((1, LANES), jnp.float32),
        ),
        in_specs=[SMEM] * 3 + [ANY],
        out_specs=(SMEM, VMEM),
        scratch_shapes=[
            pltpu.SMEM((16,), jnp.int32),
            pltpu.VMEM(tiles.shape, tiles.dtype),
            pltpu.SemaphoreType.DMA((tiles.shape[0] // GROUP,)),
        ],
        compiler_params=params(59 * 2**20),
        cost_estimate=pl.CostEstimate(flops=0, bytes_accessed=0, transcendentals=0),
    )(rows, cols, count, tiles)


def fill_table(layout, mine, notes, table):
    cap = layout.cap
    keys = 16 * cap
    _, yc, _, zs = whereabouts()
    for j in range(4):
        for flip, asked in enumerate(notes, 1):
            for r in range(cap):
                table[layout.pack(j, flip) + r] = asked[0, (zs[j] * 4 + yc) * cap + r].astype(jnp.int32)
    for i, (j, flip) in enumerate(EARLY + LATE):
        for r in range(cap):
            key = (zs[j] * 4 + (yc ^ flip)) * cap + r
            at = layout.entry(i * cap + r)
            table[at] = mine[key]
            table[at + 1] = mine[keys + key]
            table[at + 2] = mine[2 * keys + key]


def start_kernel(layout, mine, note1, note2, note3, own, first, table, out2, out3):
    fill_table(layout, mine, (note1, note2, note3), table)
    other_y_kernel(layout, (0, 1), table, own, first, out2, out3)


def start(layout, mine, notes, own, first):
    _, tile, repl = own.shape
    packs = jax.ShapeDtypeStruct((2 * layout.cap, tile, repl), jnp.bfloat16)
    return pl.pallas_call(
        functools.partial(start_kernel, layout),
        out_shape=(jax.ShapeDtypeStruct((layout.size,), jnp.int32), packs, packs),
        in_specs=[SMEM] * 4 + [VMEM] * 2,
        out_specs=(SMEM, VMEM, VMEM),
        compiler_params=params(),
        cost_estimate=pl.CostEstimate(flops=0, bytes_accessed=0, transcendentals=0),
    )(mine, *notes, own, first)


def copy_asked(layout, table, j, flip, shard, out, first=0):
    at = layout.pack(j, flip)
    for r in range(layout.cap):
        out[first + r] = shard[table[at + r]]


def copy_part(cap, source, part, out, first):
    for r in range(cap):
        out[first + r] = source[part * cap + r]


def by_place(mid, out, use):
    inner = whereabouts()[2]
    pl.when(inner)(lambda: use(mid))
    pl.when(jnp.logical_not(inner))(lambda: use(out))


def other_y_kernel(layout, js, table, *refs):
    shards, outs = refs[:-2], refs[-2:]
    for i, (j, shard) in enumerate(zip(js, shards)):
        for flip in (2, 3):
            copy_asked(layout, table, j, flip, shard, outs[flip - 2], i * layout.cap)


def second_kernel(layout, js, table, *refs):
    shards, (out2, out3, core) = refs[:-3], refs[-3:]
    other_y_kernel(layout, (2,), table, shards[-1], out2, out3)
    for i, (j, shard) in enumerate(zip(js, shards)):
        copy_asked(layout, table, j, 1, shard, core, i * layout.cap)


def third_kernel(layout, table, mid, out, out2, out3, core):
    def use(shard):
        other_y_kernel(layout, (3,), table, shard, out2, out3)
        copy_asked(layout, table, 3, 1, shard, core)

    by_place(mid, out, use)


def pack(kernel, sizes, table, arrays, after=()):
    _, tile, repl = arrays[0].shape
    first_out = 1 + len(arrays) + len(after)

    def picked(*refs):
        kernel(*refs[: 1 + len(arrays)], *refs[first_out:])

    return pl.pallas_call(
        picked,
        out_shape=[jax.ShapeDtypeStruct((size, tile, repl), jnp.bfloat16) for size in sizes],
        in_specs=[SMEM] + [VMEM] * len(arrays) + [ANY] * len(after),
        out_specs=[VMEM] * len(sizes),
        compiler_params=params(),
        cost_estimate=pl.CostEstimate(flops=0, bytes_accessed=0, transcendentals=0),
    )(table, *arrays, *after)


def multiply(layout, table, tiles, blocks, first, field):
    prods = [
        jnp.dot(tiles[table[layout.entry(first + i)]], block, preferred_element_type=jnp.float32)
        for i, block in enumerate(blocks)
    ]
    for i, prod in enumerate(prods):
        field[table[layout.entry(first + i) + 1]] += prod


def take_own(layout, table, entry, shard, xbuf, place):
    for r in range(layout.cap):
        xbuf[place + r] = shard[table[layout.entry(entry + r) + 2]]


def early_kernel(layout, parts, table, tiles, own, first, second, mid, out, core, core3, *refs):
    cap = layout.cap
    field, xbuf = refs[-2:]
    for j, shard in enumerate((own, first, second)):
        base = 4 * cap * j
        take_own(layout, table, base, shard, xbuf, base)
        if core.shape[0] == 3 * cap:
            copy_part(cap, core, j, xbuf, base + cap)
        elif j == 0:
            copy_part(cap, refs[-3], 0, xbuf, base + cap)
        else:
            copy_part(cap, core, j - 1, xbuf, base + cap)
        ref, part = parts[j]
        copy_part(cap, refs[ref], part, xbuf, base + 2 * cap)
        copy_part(cap, refs[ref + 1], part, xbuf, base + 3 * cap)
    by_place(mid, out, lambda shard: take_own(layout, table, 12 * cap, shard, xbuf, 12 * cap))
    copy_part(cap, core3, 0, xbuf, 13 * cap)
    field[...] = jnp.zeros_like(field)

    @pl.loop(0, len(EARLY) * cap // GROUP)
    def _(g):
        multiply(layout, table, tiles, [xbuf[g * GROUP + i] for i in range(GROUP)], g * GROUP, field)


def early(layout, parts, table, tiles, arrays):
    tile = tiles.shape[1]
    blocks, _, repl = arrays[0].shape
    return pl.pallas_call(
        functools.partial(early_kernel, layout, parts),
        out_shape=jax.ShapeDtypeStruct((blocks + 1, tile, repl), jnp.float32),
        in_specs=[SMEM] + [VMEM] * (1 + len(arrays)),
        out_specs=VMEM,
        scratch_shapes=[pltpu.VMEM((len(EARLY) * layout.cap, tile, repl), jnp.bfloat16)],
        compiler_params=params(),
        cost_estimate=pl.CostEstimate(flops=0, bytes_accessed=0, transcendentals=0),
    )(table, tiles, *arrays)


def late_field(layout, table, tiles, got2, got3, field, acc):
    cap = layout.cap
    acc[...] = field[...]
    multiply(layout, table, tiles, [ref[r] for ref in (got2, got3) for r in range(cap)], len(EARLY) * cap, acc)


def late_kernel(layout, table, scalars, tiles, got2, got3, field, xpos, ymom, xout, yout, xb, out2, out3, core, acc):
    late_field(layout, table, tiles, got2, got3, field, acc)
    for b in range(xpos.shape[0]):
        x, y = update(scalars[0], scalars[1], acc[b], xpos[b], ymom[b])
        xout[b] = x
        yout[b] = y
        xb[b] = x.astype(jnp.bfloat16)
    other_y_kernel(layout, (0,), table, xb, out2, out3)
    copy_asked(layout, table, 0, 1, xb, core)


def late(layout, table, scalars, tiles, sources, field, xpos, ymom):
    tile = tiles.shape[1]
    blocks, _, repl = xpos.shape
    entries = len(LATE) * layout.cap
    state = jax.ShapeDtypeStruct(xpos.shape, jnp.float32)
    out = jax.ShapeDtypeStruct((layout.cap, tile, repl), jnp.bfloat16)
    return pl.pallas_call(
        functools.partial(late_kernel, layout),
        out_shape=(state, state, jax.ShapeDtypeStruct(xpos.shape, jnp.bfloat16), out, out, out),
        in_specs=[SMEM, SMEM] + [VMEM] * (1 + len(sources) + 3),
        out_specs=(VMEM,) * 6,
        scratch_shapes=[pltpu.VMEM((blocks + 1, tile, repl), jnp.float32)],
        compiler_params=params(),
        cost_estimate=pl.CostEstimate(
            flops=2 * entries * tile * tile * repl,
            bytes_accessed=entries * tile * (tile + repl) * 2 + 20 * xpos.size,
            transcendentals=0,
        ),
    )(table, scalars, tiles, *sources, field, xpos, ymom)


def energy_kernel(layout, table, tiles, got2, got3, field, xpos, energy, acc):
    late_field(layout, table, tiles, got2, got3, field, acc)
    total = jnp.zeros(xpos.shape[1:], jnp.float32)
    for b in range(xpos.shape[0]):
        total += xpos[b] * acc[b]
    part = -0.5 * jnp.sum(total, axis=0, keepdims=True)
    for i in range(energy.shape[0]):
        energy[i] = part


def last_field(layout, table, tiles, sources, field, xpos):
    return pl.pallas_call(
        functools.partial(energy_kernel, layout),
        out_shape=(
            jax.ShapeDtypeStruct((16, 1, xpos.shape[2]), jnp.float32),
            jax.ShapeDtypeStruct(field.shape, jnp.float32),
        ),
        in_specs=[SMEM] + [VMEM] * (1 + len(sources) + 2),
        out_specs=(VMEM, VMEM),
        compiler_params=params(),
        cost_estimate=pl.CostEstimate(flops=0, bytes_accessed=0, transcendentals=0),
    )(table, tiles, *sources, field, xpos)


def update_kernel(scalars, field, xpos, ymom, xout, yout, xnew, ynew, sems):
    copies = []
    for b in range(xpos.shape[0]):
        x, y = update(scalars[0], scalars[1], field[b], xpos[b], ymom[b])
        xnew[b] = x
        ynew[b] = y
        for i, (new, out) in enumerate(((xnew, xout), (ynew, yout))):
            copies.append(pltpu.make_async_copy(new.at[b], out.at[b], sems.at[i, b]))
            copies[-1].start()
    for copy in copies:
        copy.wait()


def last_update(scalars, field, xpos, ymom):
    state = jax.ShapeDtypeStruct(xpos.shape, jnp.float32)
    return pl.pallas_call(
        update_kernel,
        out_shape=(state, state),
        in_specs=[SMEM] + [VMEM] * 3,
        out_specs=(ANY, ANY),
        scratch_shapes=[pltpu.VMEM(xpos.shape, jnp.float32)] * 2 + [pltpu.SemaphoreType.DMA((2, xpos.shape[0]))],
        compiler_params=params(),
        cost_estimate=pl.CostEstimate(flops=10 * xpos.size, bytes_accessed=20 * xpos.size, transcendentals=0),
    )(scalars, field, xpos, ymom)


def along_z(pairs, value):
    return lax.ppermute(value, "row", [(a * 4 + i, b * 4 + i) for a, b in pairs for i in range(4)])


def across(flip, value):
    return lax.ppermute(value, "row", [(i, i ^ flip) for i in range(16)])


def row_sum(parts):
    return jnp.sum(lax.all_to_all(parts, "row", split_axis=0, concat_axis=0, tiled=True), axis=0)


def body_16(tiles, tile_rows, tile_cols, counts, positions, momenta):
    slots, tile, _ = tiles.shape
    repl = positions.shape[1]
    blocks = positions.shape[0] // tile
    cap = (slots + 15) // 16
    order = blocks * tile * 16
    layout = Layout(cap)

    def other_y(js, shards):
        kernel = functools.partial(other_y_kernel, layout, js)
        return pack(kernel, [len(js) * cap] * 2, table, shards)

    def to_other_y(packs):
        return [across(2, packs[0]), across(3, packs[1])]

    xpos = positions.reshape(blocks, tile, repl)
    ymom = momenta.reshape(blocks, tile, repl)
    own0 = xpos.astype(jnp.bfloat16)
    mine, note = plan(layout, blocks, tile_rows, tile_cols, counts, tiles)
    notes = [across(flip, note) for flip in (1, 2, 3)]
    packs0 = None
    for step in range(STEPS):
        last = step == STEPS - 1
        own1 = along_z(FIRST, own0)
        if step == 0:
            again, notes[0] = lax.optimization_barrier((own0, notes[0]))
            own2 = along_z(SECOND, again)
            again, notes = lax.optimization_barrier((again, notes))
            mid = along_z(MIDDLE, again)
            own1, notes = lax.optimization_barrier((own1, notes))
            out = along_z(OUTWARD, own1)
            table, *packs01 = start(layout, mine, notes, own0, own1)
            got1 = to_other_y(packs01)
            corner = touch(tiles, own2)
            own2, got1 = lax.optimization_barrier((own2, got1))
            parts, cores, after = ((0, 0), (0, 1), (2, 0)), [], [corner]
            got = got1
        else:
            core0 = across(1, packs0[2])
            again, core0 = lax.optimization_barrier((own0, core0))
            own2 = along_z(SECOND, again)
            got0 = to_other_y(packs0)
            again, got0 = lax.optimization_barrier((again, got0))
            own1, got0 = lax.optimization_barrier((own1, got0))
            packs1 = other_y((1,), [own1])
            out = along_z(OUTWARD, own1)
            got1 = to_other_y(packs1)
            mid = along_z(MIDDLE, again)
            own2, got1 = lax.optimization_barrier((own2, got1))
            parts, cores, after = ((0, 0), (2, 0), (4, 0)), [core0], []
            got = got0 + got1
        js, shards = ((0, 1, 2), [own0, own1, own2]) if step == 0 else ((1, 2), [own1, own2])
        packs2 = pack(functools.partial(second_kernel, layout, js), [cap, cap, len(js) * cap], table, shards, after)
        got2 = to_other_y(packs2)
        core = across(1, packs2[2])
        packs3 = pack(functools.partial(third_kernel, layout), [cap] * 3, table, [mid, out])
        if step == 0:
            note, packs3 = lax.optimization_barrier((note, packs3))
            plane = note + notes[0] + notes[1] + notes[2]
            half = plane + across(4, plane)
        core3 = across(1, packs3[2])
        got3 = to_other_y(packs3)
        if step == 0:
            got2, half = lax.optimization_barrier((got2, half))
            sums = across(8, half)
        field = early(layout, parts, table, tiles, [own0, own1, own2, mid, out, core, core3] + got + got2 + cores)
        if step == 0:
            field, sums = lax.optimization_barrier((field, sums))
            total = (half + sums)[0, SUM_AT]
            coeff = 0.7 * jnp.sqrt((order - 1) / total)
        scalars = jnp.stack([jnp.float32(0.4 - 0.1 * step), coeff])
        if last:
            part, field = last_field(layout, table, tiles, got3, field, xpos)
            energy = row_sum(part)
            xpos, ymom = last_update(scalars, field, xpos, ymom)
        else:
            xpos, ymom, own0, *packs0 = late(layout, table, scalars, tiles, got3, field, xpos, ymom)
    return (xpos.reshape(positions.shape), ymom.reshape(momenta.shape), energy.reshape(repl))


def touch_kernel(tiles, own, out):
    out[...] = tiles[0, :8, :128]


def touch(tiles, own):
    return pl.pallas_call(
        touch_kernel,
        out_shape=jax.ShapeDtypeStruct((8, 128), tiles.dtype),
        in_specs=[VMEM, ANY],
        out_specs=VMEM,
        compiler_params=params(),
        cost_estimate=pl.CostEstimate(flops=0, bytes_accessed=0, transcendentals=0),
    )(tiles, own)


def gathered_kernel(last, rows, cols, count, scalars, tiles, gathered, xpos, ymom, xout, yout, extra, xbuf, field, xsem):
    tile = xbuf.shape[1]
    used = count[0]

    def block_copy(s):
        return pltpu.make_async_copy(gathered.at[cols[s]], xbuf.at[s], xsem.at[s])

    @pl.loop(0, used)
    def _(s):
        block_copy(s).start()

    field[...] = jnp.zeros_like(field)

    @pl.loop(0, used)
    def _(s):
        block_copy(s).wait()
        here = pl.ds(pl.multiple_of(rows[s] * tile, tile), tile)
        field[here, :] += jnp.dot(tiles[s], xbuf[s], preferred_element_type=jnp.float32)

    x, h = xpos[...], field[...]
    if last:
        extra[...] = -0.5 * jnp.sum(x * h, axis=0, keepdims=True)
    x, y = update(scalars[0], scalars[1], h, x, ymom[...])
    xout[...] = x
    yout[...] = y
    if not last:
        extra[...] = x.astype(jnp.bfloat16)


def body_any(tiles, tile_rows, tile_cols, counts, positions, momenta):
    slots, tile, _ = tiles.shape
    order, repl = positions.shape
    devices = lax.axis_size("row")
    state = jax.ShapeDtypeStruct(positions.shape, jnp.float32)
    total = jnp.sum(lax.psum(squares(counts, tiles), "row"))
    coeff = 0.7 * jnp.sqrt((order * devices - 1) / total)
    xpos, ymom, extra = positions, momenta, positions.astype(jnp.bfloat16)
    for step in range(STEPS):
        last = step == STEPS - 1
        gathered = lax.all_gather(extra, "row", tiled=True).reshape(-1, tile, repl)
        scalars = jnp.stack([jnp.float32(0.4 - 0.1 * step), coeff])
        xpos, ymom, extra = pl.pallas_call(
            functools.partial(gathered_kernel, last),
            out_shape=(
                state,
                state,
                jax.ShapeDtypeStruct((1, repl), jnp.float32) if last else jax.ShapeDtypeStruct(state.shape, jnp.bfloat16),
            ),
            in_specs=[SMEM] * 4 + [VMEM, ANY, VMEM, VMEM],
            out_specs=(VMEM,) * 3,
            scratch_shapes=[
                pltpu.VMEM((slots, tile, repl), jnp.bfloat16),
                pltpu.VMEM(positions.shape, jnp.float32),
                pltpu.SemaphoreType.DMA((slots,)),
            ],
            compiler_params=params(),
        )(tile_rows, tile_cols, counts, scalars, tiles, gathered, xpos, ymom)
    return (xpos, ymom, lax.psum(extra, "row").reshape(repl))


def solution(mesh):
    in_specs = (
        P(("groups", "row"), None, None),
        P(("groups", "row")),
        P(("groups", "row")),
        P(("groups", "row")),
        P(("groups", "row"), None),
        P(("groups", "row"), None),
    )
    out_specs = (P(("groups", "row"), None), P(("groups", "row"), None), P("groups"))

    def body(tiles, *args):
        slots = tiles.shape[0]
        by_hand = mesh.shape["row"] == 16 and slots % GROUP == 0 and slots <= 96
        return (body_16 if by_hand else body_any)(tiles, *args)

    return jax.shard_map(body, mesh=mesh, in_specs=in_specs, out_specs=out_specs, check_vma=False)
```

```python
import functools

import jax
import jax.numpy as jnp
from jax import lax
from jax.experimental import pallas as pl
from jax.experimental.pallas import tpu as pltpu
from jax.sharding import PartitionSpec as P

STEPS = 4
GROUP = 6
LANES = 128
SUM_AT = LANES - 1
LIMIT = 16 * 2**20

SMEM = pl.BlockSpec(memory_space=pltpu.SMEM)
VMEM = pl.BlockSpec(memory_space=pltpu.VMEM)
ANY = pl.BlockSpec(memory_space=pl.ANY)


def params(limit=LIMIT):
    return pltpu.CompilerParams(vmem_limit_bytes=limit)


def squares_kernel(count, tiles, out):
    tile = tiles.shape[1]

    def add(s, acc):
        t = tiles[s].astype(jnp.float32)
        return acc + jnp.sum((t * t).reshape(tile // 8, 8, tile), axis=0)

    acc = lax.fori_loop(0, count[0], add, jnp.zeros((8, tile), jnp.float32))
    acc = jnp.sum(acc, axis=0, keepdims=True)
    out[...] = sum(acc[:, i : i + 128] for i in range(0, tile, 128))


def squares(count, tiles):
    return pl.pallas_call(
        squares_kernel,
        out_shape=jax.ShapeDtypeStruct((1, 128), jnp.float32),
        in_specs=[SMEM, VMEM],
        out_specs=VMEM,
        compiler_params=params(),
        cost_estimate=pl.CostEstimate(flops=2 * tiles.size, bytes_accessed=2 * tiles.size, transcendentals=0),
    )(count, tiles)


def update(pump, coeff, h, x, y):
    y = y + 0.5 * (-(x * x + pump) * x + coeff * h)
    return x + 0.5 * y, y


FIRST = ((0, 2), (3, 1), (1, 0), (2, 3))
SECOND = ((0, 1), (3, 2), (1, 3), (2, 0))
OUTWARD = ((1, 0), (2, 3))
MIDDLE = ((1, 2), (2, 1))


class Layout:
    def __init__(self, cap):
        self.cap = cap
        self.packs = 0
        self.entries = 12 * cap
        self.size = 12 * cap + 3 * 16 * cap

    def pack(self, j, flip):
        return self.packs + (j * 3 + flip - 1) * self.cap

    def entry(self, i):
        return self.entries + 3 * i


def whereabouts():
    me = lax.axis_index("row")
    z, yc = lax.div(me, 4), lax.rem(me, 4)
    inner = (z == 1) | (z == 2)
    near, skip = z ^ 1, z ^ 2
    return z, yc, inner, (z, jnp.where(inner, skip, near), jnp.where(inner, near, skip), z ^ 3)


EARLY = tuple((j, flip) for j in range(3) for flip in range(4)) + ((3, 0), (3, 1))
LATE = ((3, 2), (3, 3))


def plan_kernel(layout, blocks, rows, cols, count, tiles, mine, note, seen, buffer, sems):
    cap = layout.cap
    keys = 16 * cap
    slots, tile, _ = buffer.shape
    chunks = [pl.ds(first, GROUP) for first in range(0, slots, GROUP)]
    copies = [pltpu.make_async_copy(tiles.at[c], buffer.at[c], sems.at[i]) for i, c in enumerate(chunks)]
    for copy in copies:
        copy.start()

    @pl.loop(0, 16)
    def _(d):
        seen[d] = 0

    @pl.loop(0, keys)
    def _(k):
        mine[k] = 0
        mine[keys + k] = blocks
        mine[2 * keys + k] = 0

    @pl.loop(0, count[0])
    def _(s):
        source = lax.div(cols[s], blocks)
        rank = seen[source]
        seen[source] = rank + 1
        key = source * cap + jnp.minimum(rank, cap - 1)
        mine[key] = s
        mine[keys + key] = rows[s]
        mine[2 * keys + key] = lax.rem(cols[s], blocks)

    lane = lax.broadcasted_iota(jnp.int32, note.shape, 1)
    wants = jnp.zeros(note.shape, jnp.int32)
    for k in range(keys):
        wants = jnp.where(lane == k, mine[2 * keys + k], wants)

    def add(s, acc):
        t = buffer[s].astype(jnp.float32)
        return acc + jnp.sum((t * t).reshape(tile // 64, 64, tile), axis=0)

    acc = jnp.zeros((64, tile), jnp.float32)
    for i, copy in enumerate(copies):
        copy.wait()
        acc = lax.fori_loop(i * GROUP, jnp.clip(count[0], i * GROUP, (i + 1) * GROUP), add, acc)
    note[...] = jnp.where(lane == SUM_AT, jnp.sum(acc), wants.astype(jnp.float32))


def plan(layout, blocks, rows, cols, count, tiles):
    return pl.pallas_call(
        functools.partial(plan_kernel, layout, blocks),
        out_shape=(
            jax.ShapeDtypeStruct((3 * 16 * layout.cap,), jnp.int32),
            jax.ShapeDtypeStruct((1, LANES), jnp.float32),
        ),
        in_specs=[SMEM] * 3 + [ANY],
        out_specs=(SMEM, VMEM),
        scratch_shapes=[
            pltpu.SMEM((16,), jnp.int32),
            pltpu.VMEM(tiles.shape, tiles.dtype),
            pltpu.SemaphoreType.DMA((tiles.shape[0] // GROUP,)),
        ],
        compiler_params=params(59 * 2**20),
        cost_estimate=pl.CostEstimate(flops=0, bytes_accessed=0, transcendentals=0),
    )(rows, cols, count, tiles)


def fill_table(layout, mine, notes, table):
    cap = layout.cap
    keys = 16 * cap
    _, yc, _, zs = whereabouts()
    for j in range(4):
        for flip, asked in enumerate(notes, 1):
            for r in range(cap):
                table[layout.pack(j, flip) + r] = asked[0, (zs[j] * 4 + yc) * cap + r].astype(jnp.int32)
    for i, (j, flip) in enumerate(EARLY + LATE):
        for r in range(cap):
            key = (zs[j] * 4 + (yc ^ flip)) * cap + r
            at = layout.entry(i * cap + r)
            table[at] = mine[key]
            table[at + 1] = mine[keys + key]
            table[at + 2] = mine[2 * keys + key]


def start_kernel(layout, mine, note1, note2, note3, own, first, table, out2, out3):
    fill_table(layout, mine, (note1, note2, note3), table)
    other_y_kernel(layout, (0, 1), table, own, first, out2, out3)


def start(layout, mine, notes, own, first):
    _, tile, repl = own.shape
    packs = jax.ShapeDtypeStruct((2 * layout.cap, tile, repl), jnp.bfloat16)
    return pl.pallas_call(
        functools.partial(start_kernel, layout),
        out_shape=(jax.ShapeDtypeStruct((layout.size,), jnp.int32), packs, packs),
        in_specs=[SMEM] * 4 + [VMEM] * 2,
        out_specs=(SMEM, VMEM, VMEM),
        compiler_params=params(),
        cost_estimate=pl.CostEstimate(flops=0, bytes_accessed=0, transcendentals=0),
    )(mine, *notes, own, first)


def copy_asked(layout, table, j, flip, shard, out, first=0):
    at = layout.pack(j, flip)
    for r in range(layout.cap):
        out[first + r] = shard[table[at + r]]


def copy_part(cap, source, part, out, first):
    for r in range(cap):
        out[first + r] = source[part * cap + r]


def by_place(mid, out, use):
    inner = whereabouts()[2]
    pl.when(inner)(lambda: use(mid))
    pl.when(jnp.logical_not(inner))(lambda: use(out))


def other_y_kernel(layout, js, table, *refs):
    shards, outs = refs[:-2], refs[-2:]
    for i, (j, shard) in enumerate(zip(js, shards)):
        for flip in (2, 3):
            copy_asked(layout, table, j, flip, shard, outs[flip - 2], i * layout.cap)


def second_kernel(layout, js, table, *refs):
    shards, (out2, out3, core) = refs[:-3], refs[-3:]
    other_y_kernel(layout, (2,), table, shards[-1], out2, out3)
    for i, (j, shard) in enumerate(zip(js, shards)):
        copy_asked(layout, table, j, 1, shard, core, i * layout.cap)


def third_kernel(layout, table, mid, out, out2, out3, core):
    def use(shard):
        other_y_kernel(layout, (3,), table, shard, out2, out3)
        copy_asked(layout, table, 3, 1, shard, core)

    by_place(mid, out, use)


def pack(kernel, sizes, table, arrays, after=()):
    _, tile, repl = arrays[0].shape
    first_out = 1 + len(arrays) + len(after)

    def picked(*refs):
        kernel(*refs[: 1 + len(arrays)], *refs[first_out:])

    return pl.pallas_call(
        picked,
        out_shape=[jax.ShapeDtypeStruct((size, tile, repl), jnp.bfloat16) for size in sizes],
        in_specs=[SMEM] + [VMEM] * len(arrays) + [ANY] * len(after),
        out_specs=[VMEM] * len(sizes),
        compiler_params=params(),
        cost_estimate=pl.CostEstimate(flops=0, bytes_accessed=0, transcendentals=0),
    )(table, *arrays, *after)


def multiply(layout, table, tiles, blocks, first, field):
    prods = [
        jnp.dot(tiles[table[layout.entry(first + i)]], block, preferred_element_type=jnp.float32)
        for i, block in enumerate(blocks)
    ]
    for i, prod in enumerate(prods):
        field[table[layout.entry(first + i) + 1]] += prod


def take_own(layout, table, entry, shard, xbuf, place):
    for r in range(layout.cap):
        xbuf[place + r] = shard[table[layout.entry(entry + r) + 2]]


def early_kernel(layout, parts, table, tiles, own, first, second, mid, out, core, core3, *refs):
    cap = layout.cap
    field, xbuf = refs[-2:]
    for j, shard in enumerate((own, first, second)):
        base = 4 * cap * j
        take_own(layout, table, base, shard, xbuf, base)
        if core.shape[0] == 3 * cap:
            copy_part(cap, core, j, xbuf, base + cap)
        elif j == 0:
            copy_part(cap, refs[-3], 0, xbuf, base + cap)
        else:
            copy_part(cap, core, j - 1, xbuf, base + cap)
        ref, part = parts[j]
        copy_part(cap, refs[ref], part, xbuf, base + 2 * cap)
        copy_part(cap, refs[ref + 1], part, xbuf, base + 3 * cap)
    by_place(mid, out, lambda shard: take_own(layout, table, 12 * cap, shard, xbuf, 12 * cap))
    copy_part(cap, core3, 0, xbuf, 13 * cap)
    field[...] = jnp.zeros_like(field)

    @pl.loop(0, len(EARLY) * cap // GROUP)
    def _(g):
        multiply(layout, table, tiles, [xbuf[g * GROUP + i] for i in range(GROUP)], g * GROUP, field)


def early(layout, parts, table, tiles, arrays):
    tile = tiles.shape[1]
    blocks, _, repl = arrays[0].shape
    return pl.pallas_call(
        functools.partial(early_kernel, layout, parts),
        out_shape=jax.ShapeDtypeStruct((blocks + 1, tile, repl), jnp.float32),
        in_specs=[SMEM] + [VMEM] * (1 + len(arrays)),
        out_specs=VMEM,
        scratch_shapes=[pltpu.VMEM((len(EARLY) * layout.cap, tile, repl), jnp.bfloat16)],
        compiler_params=params(),
        cost_estimate=pl.CostEstimate(flops=0, bytes_accessed=0, transcendentals=0),
    )(table, tiles, *arrays)


def late_field(layout, table, tiles, got2, got3, field, acc):
    cap = layout.cap
    acc[...] = field[...]
    multiply(layout, table, tiles, [ref[r] for ref in (got2, got3) for r in range(cap)], len(EARLY) * cap, acc)


def late_kernel(layout, table, scalars, tiles, got2, got3, field, xpos, ymom, xout, yout, xb, out2, out3, core, acc):
    late_field(layout, table, tiles, got2, got3, field, acc)
    for b in range(xpos.shape[0]):
        x, y = update(scalars[0], scalars[1], acc[b], xpos[b], ymom[b])
        xout[b] = x
        yout[b] = y
        xb[b] = x.astype(jnp.bfloat16)
    other_y_kernel(layout, (0,), table, xb, out2, out3)
    copy_asked(layout, table, 0, 1, xb, core)


def late(layout, table, scalars, tiles, sources, field, xpos, ymom):
    tile = tiles.shape[1]
    blocks, _, repl = xpos.shape
    entries = len(LATE) * layout.cap
    state = jax.ShapeDtypeStruct(xpos.shape, jnp.float32)
    out = jax.ShapeDtypeStruct((layout.cap, tile, repl), jnp.bfloat16)
    return pl.pallas_call(
        functools.partial(late_kernel, layout),
        out_shape=(state, state, jax.ShapeDtypeStruct(xpos.shape, jnp.bfloat16), out, out, out),
        in_specs=[SMEM, SMEM] + [VMEM] * (1 + len(sources) + 3),
        out_specs=(VMEM,) * 6,
        scratch_shapes=[pltpu.VMEM((blocks + 1, tile, repl), jnp.float32)],
        compiler_params=params(),
        cost_estimate=pl.CostEstimate(
            flops=2 * entries * tile * tile * repl,
            bytes_accessed=entries * tile * (tile + repl) * 2 + 20 * xpos.size,
            transcendentals=0,
        ),
    )(table, scalars, tiles, *sources, field, xpos, ymom)


def energy_kernel(layout, table, tiles, got2, got3, field, xpos, energy, acc):
    late_field(layout, table, tiles, got2, got3, field, acc)
    total = jnp.zeros(xpos.shape[1:], jnp.float32)
    for b in range(xpos.shape[0]):
        total += xpos[b] * acc[b]
    part = -0.5 * jnp.sum(total, axis=0, keepdims=True)
    energy[...] = jnp.broadcast_to(part[None], energy.shape)


def last_field(layout, table, tiles, sources, field, xpos):
    return pl.pallas_call(
        functools.partial(energy_kernel, layout),
        out_shape=(
            jax.ShapeDtypeStruct((16, 1, xpos.shape[2]), jnp.float32),
            jax.ShapeDtypeStruct(field.shape, jnp.float32),
        ),
        in_specs=[SMEM] + [VMEM] * (1 + len(sources) + 2),
        out_specs=(VMEM, VMEM),
        compiler_params=params(),
        cost_estimate=pl.CostEstimate(flops=0, bytes_accessed=0, transcendentals=0),
    )(table, tiles, *sources, field, xpos)


def update_kernel(scalars, field, xpos, ymom, xout, yout, xnew, ynew, sems):
    copies = []
    for b in range(xpos.shape[0]):
        x, y = update(scalars[0], scalars[1], field[b], xpos[b], ymom[b])
        xnew[b] = x
        ynew[b] = y
        for i, (new, out) in enumerate(((xnew, xout), (ynew, yout))):
            copies.append(pltpu.make_async_copy(new.at[b], out.at[b], sems.at[i, b]))
            copies[-1].start()
    for copy in copies:
        copy.wait()


def last_update(scalars, field, xpos, ymom):
    state = jax.ShapeDtypeStruct(xpos.shape, jnp.float32)
    return pl.pallas_call(
        update_kernel,
        out_shape=(state, state),
        in_specs=[SMEM] + [VMEM] * 3,
        out_specs=(ANY, ANY),
        scratch_shapes=[pltpu.VMEM(xpos.shape, jnp.float32)] * 2 + [pltpu.SemaphoreType.DMA((2, xpos.shape[0]))],
        compiler_params=params(),
        cost_estimate=pl.CostEstimate(flops=10 * xpos.size, bytes_accessed=20 * xpos.size, transcendentals=0),
    )(scalars, field, xpos, ymom)


def along_z(pairs, value):
    return lax.ppermute(value, "row", [(a * 4 + i, b * 4 + i) for a, b in pairs for i in range(4)])


def across(flip, value):
    return lax.ppermute(value, "row", [(i, i ^ flip) for i in range(16)])


def row_sum(parts):
    return jnp.sum(lax.all_to_all(parts, "row", split_axis=0, concat_axis=0, tiled=True), axis=0)


def body_16(tiles, tile_rows, tile_cols, counts, positions, momenta):
    slots, tile, _ = tiles.shape
    repl = positions.shape[1]
    blocks = positions.shape[0] // tile
    cap = (slots + 15) // 16
    order = blocks * tile * 16
    layout = Layout(cap)

    def other_y(js, shards):
        kernel = functools.partial(other_y_kernel, layout, js)
        return pack(kernel, [len(js) * cap] * 2, table, shards)

    def to_other_y(packs):
        return [across(2, packs[0]), across(3, packs[1])]

    xpos = positions.reshape(blocks, tile, repl)
    ymom = momenta.reshape(blocks, tile, repl)
    own0 = xpos.astype(jnp.bfloat16)
    mine, note = plan(layout, blocks, tile_rows, tile_cols, counts, tiles)
    notes = [across(flip, note) for flip in (1, 2, 3)]
    packs0 = None
    for step in range(STEPS):
        last = step == STEPS - 1
        own1 = along_z(FIRST, own0)
        if step == 0:
            again, notes[0] = lax.optimization_barrier((own0, notes[0]))
            own2 = along_z(SECOND, again)
            again, notes = lax.optimization_barrier((again, notes))
            mid = along_z(MIDDLE, again)
            own1, notes = lax.optimization_barrier((own1, notes))
            out = along_z(OUTWARD, own1)
            table, *packs01 = start(layout, mine, notes, own0, own1)
            got1 = to_other_y(packs01)
            corner = touch(tiles, own2)
            own2, got1 = lax.optimization_barrier((own2, got1))
            parts, cores, after = ((0, 0), (0, 1), (2, 0)), [], [corner]
            got = got1
        else:
            core0 = across(1, packs0[2])
            again, core0 = lax.optimization_barrier((own0, core0))
            own2 = along_z(SECOND, again)
            got0 = to_other_y(packs0)
            again, got0 = lax.optimization_barrier((again, got0))
            own1, got0 = lax.optimization_barrier((own1, got0))
            packs1 = other_y((1,), [own1])
            out = along_z(OUTWARD, own1)
            got1 = to_other_y(packs1)
            mid = along_z(MIDDLE, again)
            own2, got1 = lax.optimization_barrier((own2, got1))
            parts, cores, after = ((0, 0), (2, 0), (4, 0)), [core0], []
            got = got0 + got1
        js, shards = ((0, 1, 2), [own0, own1, own2]) if step == 0 else ((1, 2), [own1, own2])
        packs2 = pack(functools.partial(second_kernel, layout, js), [cap, cap, len(js) * cap], table, shards, after)
        got2 = to_other_y(packs2)
        core = across(1, packs2[2])
        packs3 = pack(functools.partial(third_kernel, layout), [cap] * 3, table, [mid, out])
        if step == 0:
            note, packs3 = lax.optimization_barrier((note, packs3))
            plane = note + notes[0] + notes[1] + notes[2]
            half = plane + across(4, plane)
        core3 = across(1, packs3[2])
        got3 = to_other_y(packs3)
        if step == 0:
            got2, half = lax.optimization_barrier((got2, half))
            sums = across(8, half)
        field = early(layout, parts, table, tiles, [own0, own1, own2, mid, out, core, core3] + got + got2 + cores)
        if step == 0:
            field, sums = lax.optimization_barrier((field, sums))
            total = (half + sums)[0, SUM_AT]
            coeff = 0.7 * jnp.sqrt((order - 1) / total)
        scalars = jnp.stack([jnp.float32(0.4 - 0.1 * step), coeff])
        if last:
            part, field = last_field(layout, table, tiles, got3, field, xpos)
            energy = row_sum(part)
            xpos, ymom = last_update(scalars, field, xpos, ymom)
        else:
            xpos, ymom, own0, *packs0 = late(layout, table, scalars, tiles, got3, field, xpos, ymom)
    return (xpos.reshape(positions.shape), ymom.reshape(momenta.shape), energy.reshape(repl))


def touch_kernel(tiles, own, out):
    out[...] = tiles[0, :8, :128]


def touch(tiles, own):
    return pl.pallas_call(
        touch_kernel,
        out_shape=jax.ShapeDtypeStruct((8, 128), tiles.dtype),
        in_specs=[VMEM, ANY],
        out_specs=VMEM,
        compiler_params=params(),
        cost_estimate=pl.CostEstimate(flops=0, bytes_accessed=0, transcendentals=0),
    )(tiles, own)


def gathered_kernel(last, rows, cols, count, scalars, tiles, gathered, xpos, ymom, xout, yout, extra, xbuf, field, xsem):
    tile = xbuf.shape[1]
    used = count[0]

    def block_copy(s):
        return pltpu.make_async_copy(gathered.at[cols[s]], xbuf.at[s], xsem.at[s])

    @pl.loop(0, used)
    def _(s):
        block_copy(s).start()

    field[...] = jnp.zeros_like(field)

    @pl.loop(0, used)
    def _(s):
        block_copy(s).wait()
        here = pl.ds(pl.multiple_of(rows[s] * tile, tile), tile)
        field[here, :] += jnp.dot(tiles[s], xbuf[s], preferred_element_type=jnp.float32)

    x, h = xpos[...], field[...]
    if last:
        extra[...] = -0.5 * jnp.sum(x * h, axis=0, keepdims=True)
    x, y = update(scalars[0], scalars[1], h, x, ymom[...])
    xout[...] = x
    yout[...] = y
    if not last:
        extra[...] = x.astype(jnp.bfloat16)


def body_any(tiles, tile_rows, tile_cols, counts, positions, momenta):
    slots, tile, _ = tiles.shape
    order, repl = positions.shape
    devices = lax.axis_size("row")
    state = jax.ShapeDtypeStruct(positions.shape, jnp.float32)
    total = jnp.sum(lax.psum(squares(counts, tiles), "row"))
    coeff = 0.7 * jnp.sqrt((order * devices - 1) / total)
    xpos, ymom, extra = positions, momenta, positions.astype(jnp.bfloat16)
    for step in range(STEPS):
        last = step == STEPS - 1
        gathered = lax.all_gather(extra, "row", tiled=True).reshape(-1, tile, repl)
        scalars = jnp.stack([jnp.float32(0.4 - 0.1 * step), coeff])
        xpos, ymom, extra = pl.pallas_call(
            functools.partial(gathered_kernel, last),
            out_shape=(
                state,
                state,
                jax.ShapeDtypeStruct((1, repl), jnp.float32) if last else jax.ShapeDtypeStruct(state.shape, jnp.bfloat16),
            ),
            in_specs=[SMEM] * 4 + [VMEM, ANY, VMEM, VMEM],
            out_specs=(VMEM,) * 3,
            scratch_shapes=[
                pltpu.VMEM((slots, tile, repl), jnp.bfloat16),
                pltpu.VMEM(positions.shape, jnp.float32),
                pltpu.SemaphoreType.DMA((slots,)),
            ],
            compiler_params=params(),
        )(tile_rows, tile_cols, counts, scalars, tiles, gathered, xpos, ymom)
    return (xpos, ymom, lax.psum(extra, "row").reshape(repl))


def solution(mesh):
    in_specs = (
        P(("groups", "row"), None, None),
        P(("groups", "row")),
        P(("groups", "row")),
        P(("groups", "row")),
        P(("groups", "row"), None),
        P(("groups", "row"), None),
    )
    out_specs = (P(("groups", "row"), None), P(("groups", "row"), None), P("groups"))

    def body(tiles, *args):
        slots = tiles.shape[0]
        by_hand = mesh.shape["row"] == 16 and slots % GROUP == 0 and slots <= 96
        return (body_16 if by_hand else body_any)(tiles, *args)

    return jax.shard_map(body, mesh=mesh, in_specs=in_specs, out_specs=out_specs, check_vma=False)
```

```python
import functools

import jax
import jax.numpy as jnp
from jax import lax
from jax.experimental import pallas as pl
from jax.experimental.pallas import tpu as pltpu
from jax.sharding import PartitionSpec as P

STEPS = 4
GROUP = 6
LANES = 128
SUM_AT = LANES - 1
LIMIT = 16 * 2**20

SMEM = pl.BlockSpec(memory_space=pltpu.SMEM)
VMEM = pl.BlockSpec(memory_space=pltpu.VMEM)
ANY = pl.BlockSpec(memory_space=pl.ANY)


def params(limit=LIMIT):
    return pltpu.CompilerParams(vmem_limit_bytes=limit)


def squares_kernel(count, tiles, out):
    tile = tiles.shape[1]

    def add(s, acc):
        t = tiles[s].astype(jnp.float32)
        return acc + jnp.sum((t * t).reshape(tile // 8, 8, tile), axis=0)

    acc = lax.fori_loop(0, count[0], add, jnp.zeros((8, tile), jnp.float32))
    acc = jnp.sum(acc, axis=0, keepdims=True)
    out[...] = sum(acc[:, i : i + 128] for i in range(0, tile, 128))


def squares(count, tiles):
    return pl.pallas_call(
        squares_kernel,
        out_shape=jax.ShapeDtypeStruct((1, 128), jnp.float32),
        in_specs=[SMEM, VMEM],
        out_specs=VMEM,
        compiler_params=params(),
        cost_estimate=pl.CostEstimate(flops=2 * tiles.size, bytes_accessed=2 * tiles.size, transcendentals=0),
    )(count, tiles)


def update(pump, coeff, h, x, y):
    y = y + 0.5 * (-(x * x + pump) * x + coeff * h)
    return x + 0.5 * y, y


FIRST = ((0, 2), (3, 1), (1, 0), (2, 3))
SECOND = ((0, 1), (3, 2), (1, 3), (2, 0))
OUTWARD = ((1, 0), (2, 3))
MIDDLE = ((1, 2), (2, 1))


class Layout:
    def __init__(self, cap):
        self.cap = cap
        self.packs = 0
        self.entries = 12 * cap
        self.size = 12 * cap + 3 * 16 * cap

    def pack(self, j, flip):
        return self.packs + (j * 3 + flip - 1) * self.cap

    def entry(self, i):
        return self.entries + 3 * i


def whereabouts():
    me = lax.axis_index("row")
    z, yc = lax.div(me, 4), lax.rem(me, 4)
    inner = (z == 1) | (z == 2)
    near, skip = z ^ 1, z ^ 2
    return z, yc, inner, (z, jnp.where(inner, skip, near), jnp.where(inner, near, skip), z ^ 3)


EARLY = tuple((j, flip) for j in range(3) for flip in range(4)) + ((3, 0), (3, 1))
LATE = ((3, 2), (3, 3))


def plan_kernel(layout, blocks, rows, cols, count, tiles, mine, note, seen, buffer, sems):
    cap = layout.cap
    keys = 16 * cap
    slots, tile, _ = buffer.shape
    chunks = [pl.ds(first, GROUP) for first in range(0, slots, GROUP)]
    copies = [pltpu.make_async_copy(tiles.at[c], buffer.at[c], sems.at[i]) for i, c in enumerate(chunks)]
    for i, copy in enumerate(copies):
        pl.when(count[0] > i * GROUP)(copy.start)

    @pl.loop(0, 16)
    def _(d):
        seen[d] = 0

    @pl.loop(0, keys)
    def _(k):
        mine[k] = 0
        mine[keys + k] = blocks
        mine[2 * keys + k] = 0

    @pl.loop(0, count[0])
    def _(s):
        source = lax.div(cols[s], blocks)
        rank = seen[source]
        seen[source] = rank + 1
        key = source * cap + jnp.minimum(rank, cap - 1)
        mine[key] = s
        mine[keys + key] = rows[s]
        mine[2 * keys + key] = lax.rem(cols[s], blocks)

    lane = lax.broadcasted_iota(jnp.int32, note.shape, 1)
    wants = jnp.zeros(note.shape, jnp.int32)
    for k in range(keys):
        wants = jnp.where(lane == k, mine[2 * keys + k], wants)

    def add(s, acc):
        t = buffer[s].astype(jnp.float32)
        return acc + jnp.sum((t * t).reshape(tile // 8, 8, tile), axis=0)

    acc = jnp.zeros((8, tile), jnp.float32)
    for i, copy in enumerate(copies):
        pl.when(count[0] > i * GROUP)(copy.wait)
        acc = lax.fori_loop(i * GROUP, jnp.clip(count[0], i * GROUP, (i + 1) * GROUP), add, acc)
    note[...] = jnp.where(lane == SUM_AT, jnp.sum(acc), wants.astype(jnp.float32))


def plan(layout, blocks, rows, cols, count, tiles):
    return pl.pallas_call(
        functools.partial(plan_kernel, layout, blocks),
        out_shape=(
            jax.ShapeDtypeStruct((3 * 16 * layout.cap,), jnp.int32),
            jax.ShapeDtypeStruct((1, LANES), jnp.float32),
        ),
        in_specs=[SMEM] * 3 + [ANY],
        out_specs=(SMEM, VMEM),
        scratch_shapes=[
            pltpu.SMEM((16,), jnp.int32),
            pltpu.VMEM(tiles.shape, tiles.dtype),
            pltpu.SemaphoreType.DMA((tiles.shape[0] // GROUP,)),
        ],
        compiler_params=params(59 * 2**20),
        cost_estimate=pl.CostEstimate(flops=0, bytes_accessed=0, transcendentals=0),
    )(rows, cols, count, tiles)


def fill_table(layout, mine, notes, table):
    cap = layout.cap
    keys = 16 * cap
    _, yc, _, zs = whereabouts()
    for j in range(4):
        for flip, asked in enumerate(notes, 1):
            for r in range(cap):
                table[layout.pack(j, flip) + r] = asked[0, (zs[j] * 4 + yc) * cap + r].astype(jnp.int32)
    for i, (j, flip) in enumerate(EARLY + LATE):
        for r in range(cap):
            key = (zs[j] * 4 + (yc ^ flip)) * cap + r
            at = layout.entry(i * cap + r)
            table[at] = mine[key]
            table[at + 1] = mine[keys + key]
            table[at + 2] = mine[2 * keys + key]


def start_kernel(layout, mine, note1, note2, note3, own, first, table, out2, out3):
    fill_table(layout, mine, (note1, note2, note3), table)
    other_y_kernel(layout, (0, 1), table, own, first, out2, out3)


def start(layout, mine, notes, own, first):
    _, tile, repl = own.shape
    packs = jax.ShapeDtypeStruct((2 * layout.cap, tile, repl), jnp.bfloat16)
    return pl.pallas_call(
        functools.partial(start_kernel, layout),
        out_shape=(jax.ShapeDtypeStruct((layout.size,), jnp.int32), packs, packs),
        in_specs=[SMEM] * 4 + [VMEM] * 2,
        out_specs=(SMEM, VMEM, VMEM),
        compiler_params=params(),
        cost_estimate=pl.CostEstimate(flops=0, bytes_accessed=0, transcendentals=0),
    )(mine, *notes, own, first)


def copy_asked(layout, table, j, flip, shard, out, first=0):
    at = layout.pack(j, flip)
    for r in range(layout.cap):
        out[first + r] = shard[table[at + r]]


def copy_part(cap, source, part, out, first):
    for r in range(cap):
        out[first + r] = source[part * cap + r]


def by_place(mid, out, use):
    inner = whereabouts()[2]
    pl.when(inner)(lambda: use(mid))
    pl.when(jnp.logical_not(inner))(lambda: use(out))


def other_y_kernel(layout, js, table, *refs):
    shards, outs = refs[:-2], refs[-2:]
    for i, (j, shard) in enumerate(zip(js, shards)):
        for flip in (2, 3):
            copy_asked(layout, table, j, flip, shard, outs[flip - 2], i * layout.cap)


def second_kernel(layout, js, table, *refs):
    shards, (out2, out3, core) = refs[:-3], refs[-3:]
    other_y_kernel(layout, (2,), table, shards[-1], out2, out3)
    for i, (j, shard) in enumerate(zip(js, shards)):
        copy_asked(layout, table, j, 1, shard, core, i * layout.cap)


def third_kernel(layout, table, mid, out, out2, out3, core):
    def use(shard):
        other_y_kernel(layout, (3,), table, shard, out2, out3)
        copy_asked(layout, table, 3, 1, shard, core)

    by_place(mid, out, use)


def pack(kernel, sizes, table, arrays, after=()):
    _, tile, repl = arrays[0].shape
    first_out = 1 + len(arrays) + len(after)

    def picked(*refs):
        kernel(*refs[: 1 + len(arrays)], *refs[first_out:])

    return pl.pallas_call(
        picked,
        out_shape=[jax.ShapeDtypeStruct((size, tile, repl), jnp.bfloat16) for size in sizes],
        in_specs=[SMEM] + [VMEM] * len(arrays) + [ANY] * len(after),
        out_specs=[VMEM] * len(sizes),
        compiler_params=params(),
        cost_estimate=pl.CostEstimate(flops=0, bytes_accessed=0, transcendentals=0),
    )(table, *arrays, *after)


def multiply(layout, table, tiles, blocks, first, field):
    prods = [
        jnp.dot(tiles[table[layout.entry(first + i)]], block, preferred_element_type=jnp.float32)
        for i, block in enumerate(blocks)
    ]
    for i, prod in enumerate(prods):
        field[table[layout.entry(first + i) + 1]] += prod


def take_own(layout, table, entry, shard, xbuf, place):
    for r in range(layout.cap):
        xbuf[place + r] = shard[table[layout.entry(entry + r) + 2]]


def early_kernel(layout, parts, table, tiles, own, first, second, mid, out, core, core3, *refs):
    cap = layout.cap
    field, xbuf = refs[-2:]
    for j, shard in enumerate((own, first, second)):
        base = 4 * cap * j
        take_own(layout, table, base, shard, xbuf, base)
        if core.shape[0] == 3 * cap:
            copy_part(cap, core, j, xbuf, base + cap)
        elif j == 0:
            copy_part(cap, refs[-3], 0, xbuf, base + cap)
        else:
            copy_part(cap, core, j - 1, xbuf, base + cap)
        ref, part = parts[j]
        copy_part(cap, refs[ref], part, xbuf, base + 2 * cap)
        copy_part(cap, refs[ref + 1], part, xbuf, base + 3 * cap)
    by_place(mid, out, lambda shard: take_own(layout, table, 12 * cap, shard, xbuf, 12 * cap))
    copy_part(cap, core3, 0, xbuf, 13 * cap)
    field[...] = jnp.zeros_like(field)

    @pl.loop(0, len(EARLY) * cap // GROUP)
    def _(g):
        multiply(layout, table, tiles, [xbuf[g * GROUP + i] for i in range(GROUP)], g * GROUP, field)


def early(layout, parts, table, tiles, arrays):
    tile = tiles.shape[1]
    blocks, _, repl = arrays[0].shape
    return pl.pallas_call(
        functools.partial(early_kernel, layout, parts),
        out_shape=jax.ShapeDtypeStruct((blocks + 1, tile, repl), jnp.float32),
        in_specs=[SMEM] + [VMEM] * (1 + len(arrays)),
        out_specs=VMEM,
        scratch_shapes=[pltpu.VMEM((len(EARLY) * layout.cap, tile, repl), jnp.bfloat16)],
        compiler_params=params(),
        cost_estimate=pl.CostEstimate(flops=0, bytes_accessed=0, transcendentals=0),
    )(table, tiles, *arrays)


def late_field(layout, table, tiles, got2, got3, field, acc):
    cap = layout.cap
    acc[...] = field[...]
    multiply(layout, table, tiles, [ref[r] for ref in (got2, got3) for r in range(cap)], len(EARLY) * cap, acc)


def late_kernel(layout, table, scalars, tiles, got2, got3, field, xpos, ymom, xout, yout, xb, out2, out3, core, acc):
    late_field(layout, table, tiles, got2, got3, field, acc)
    for b in range(xpos.shape[0]):
        x, y = update(scalars[0], scalars[1], acc[b], xpos[b], ymom[b])
        xout[b] = x
        yout[b] = y
        xb[b] = x.astype(jnp.bfloat16)
    other_y_kernel(layout, (0,), table, xb, out2, out3)
    copy_asked(layout, table, 0, 1, xb, core)


def late(layout, table, scalars, tiles, sources, field, xpos, ymom):
    tile = tiles.shape[1]
    blocks, _, repl = xpos.shape
    entries = len(LATE) * layout.cap
    state = jax.ShapeDtypeStruct(xpos.shape, jnp.float32)
    out = jax.ShapeDtypeStruct((layout.cap, tile, repl), jnp.bfloat16)
    return pl.pallas_call(
        functools.partial(late_kernel, layout),
        out_shape=(state, state, jax.ShapeDtypeStruct(xpos.shape, jnp.bfloat16), out, out, out),
        in_specs=[SMEM, SMEM] + [VMEM] * (1 + len(sources) + 3),
        out_specs=(VMEM,) * 6,
        scratch_shapes=[pltpu.VMEM((blocks + 1, tile, repl), jnp.float32)],
        compiler_params=params(),
        cost_estimate=pl.CostEstimate(
            flops=2 * entries * tile * tile * repl,
            bytes_accessed=entries * tile * (tile + repl) * 2 + 20 * xpos.size,
            transcendentals=0,
        ),
    )(table, scalars, tiles, *sources, field, xpos, ymom)


def energy_kernel(layout, table, tiles, got2, got3, field, xpos, energy, acc):
    late_field(layout, table, tiles, got2, got3, field, acc)
    total = jnp.zeros(xpos.shape[1:], jnp.float32)
    for b in range(xpos.shape[0]):
        total += xpos[b] * acc[b]
    part = -0.5 * jnp.sum(total, axis=0, keepdims=True)
    for i in range(energy.shape[0]):
        energy[i] = part


def last_field(layout, table, tiles, sources, field, xpos):
    return pl.pallas_call(
        functools.partial(energy_kernel, layout),
        out_shape=(
            jax.ShapeDtypeStruct((16, 1, xpos.shape[2]), jnp.float32),
            jax.ShapeDtypeStruct(field.shape, jnp.float32),
        ),
        in_specs=[SMEM] + [VMEM] * (1 + len(sources) + 2),
        out_specs=(VMEM, VMEM),
        compiler_params=params(),
        cost_estimate=pl.CostEstimate(flops=0, bytes_accessed=0, transcendentals=0),
    )(table, tiles, *sources, field, xpos)


def update_kernel(scalars, field, xpos, ymom, xout, yout, xnew, ynew, sems):
    copies = []
    for b in range(xpos.shape[0]):
        x, y = update(scalars[0], scalars[1], field[b], xpos[b], ymom[b])
        xnew[b] = x
        ynew[b] = y
        for i, (new, out) in enumerate(((xnew, xout), (ynew, yout))):
            copies.append(pltpu.make_async_copy(new.at[b], out.at[b], sems.at[i, b]))
            copies[-1].start()
    for copy in copies:
        copy.wait()


def last_update(scalars, field, xpos, ymom):
    state = jax.ShapeDtypeStruct(xpos.shape, jnp.float32)
    return pl.pallas_call(
        update_kernel,
        out_shape=(state, state),
        in_specs=[SMEM] + [VMEM] * 3,
        out_specs=(ANY, ANY),
        scratch_shapes=[pltpu.VMEM(xpos.shape, jnp.float32)] * 2 + [pltpu.SemaphoreType.DMA((2, xpos.shape[0]))],
        compiler_params=params(),
        cost_estimate=pl.CostEstimate(flops=10 * xpos.size, bytes_accessed=20 * xpos.size, transcendentals=0),
    )(scalars, field, xpos, ymom)


def along_z(pairs, value):
    return lax.ppermute(value, "row", [(a * 4 + i, b * 4 + i) for a, b in pairs for i in range(4)])


def across(flip, value):
    return lax.ppermute(value, "row", [(i, i ^ flip) for i in range(16)])


def row_sum(parts):
    return jnp.sum(lax.all_to_all(parts, "row", split_axis=0, concat_axis=0, tiled=True), axis=0)


def body_16(tiles, tile_rows, tile_cols, counts, positions, momenta):
    slots, tile, _ = tiles.shape
    repl = positions.shape[1]
    blocks = positions.shape[0] // tile
    cap = (slots + 15) // 16
    order = blocks * tile * 16
    layout = Layout(cap)

    def other_y(js, shards):
        kernel = functools.partial(other_y_kernel, layout, js)
        return pack(kernel, [len(js) * cap] * 2, table, shards)

    def to_other_y(packs):
        return [across(2, packs[0]), across(3, packs[1])]

    xpos = positions.reshape(blocks, tile, repl)
    ymom = momenta.reshape(blocks, tile, repl)
    own0 = xpos.astype(jnp.bfloat16)
    mine, note = plan(layout, blocks, tile_rows, tile_cols, counts, tiles)
    notes = [across(flip, note) for flip in (1, 2, 3)]
    packs0 = None
    for step in range(STEPS):
        last = step == STEPS - 1
        own1 = along_z(FIRST, own0)
        if step == 0:
            again, notes[0] = lax.optimization_barrier((own0, notes[0]))
            own2 = along_z(SECOND, again)
            again, notes = lax.optimization_barrier((again, notes))
            mid = along_z(MIDDLE, again)
            own1, notes = lax.optimization_barrier((own1, notes))
            out = along_z(OUTWARD, own1)
            table, *packs01 = start(layout, mine, notes, own0, own1)
            got1 = to_other_y(packs01)
            corner = touch(tiles, own2)
            own2, got1 = lax.optimization_barrier((own2, got1))
            parts, cores, after = ((0, 0), (0, 1), (2, 0)), [], [corner]
            got = got1
        else:
            core0 = across(1, packs0[2])
            again, core0 = lax.optimization_barrier((own0, core0))
            own2 = along_z(SECOND, again)
            got0 = to_other_y(packs0)
            again, got0 = lax.optimization_barrier((again, got0))
            own1, got0 = lax.optimization_barrier((own1, got0))
            packs1 = other_y((1,), [own1])
            out = along_z(OUTWARD, own1)
            got1 = to_other_y(packs1)
            mid = along_z(MIDDLE, again)
            own2, got1 = lax.optimization_barrier((own2, got1))
            parts, cores, after = ((0, 0), (2, 0), (4, 0)), [core0], []
            got = got0 + got1
        js, shards = ((0, 1, 2), [own0, own1, own2]) if step == 0 else ((1, 2), [own1, own2])
        packs2 = pack(functools.partial(second_kernel, layout, js), [cap, cap, len(js) * cap], table, shards, after)
        got2 = to_other_y(packs2)
        core = across(1, packs2[2])
        packs3 = pack(functools.partial(third_kernel, layout), [cap] * 3, table, [mid, out])
        if step == 0:
            note, packs3 = lax.optimization_barrier((note, packs3))
            plane = note + notes[0] + notes[1] + notes[2]
            half = plane + across(4, plane)
        core3 = across(1, packs3[2])
        got3 = to_other_y(packs3)
        if step == 0:
            got2, half = lax.optimization_barrier((got2, half))
            sums = across(8, half)
        field = early(layout, parts, table, tiles, [own0, own1, own2, mid, out, core, core3] + got + got2 + cores)
        if step == 0:
            field, sums = lax.optimization_barrier((field, sums))
            total = (half + sums)[0, SUM_AT]
            coeff = 0.7 * jnp.sqrt((order - 1) / total)
        scalars = jnp.stack([jnp.float32(0.4 - 0.1 * step), coeff])
        if last:
            part, field = last_field(layout, table, tiles, got3, field, xpos)
            energy = row_sum(part)
            xpos, ymom = last_update(scalars, field, xpos, ymom)
        else:
            xpos, ymom, own0, *packs0 = late(layout, table, scalars, tiles, got3, field, xpos, ymom)
    return (xpos.reshape(positions.shape), ymom.reshape(momenta.shape), energy.reshape(repl))


def touch_kernel(tiles, own, out):
    out[...] = tiles[0, :8, :128]


def touch(tiles, own):
    return pl.pallas_call(
        touch_kernel,
        out_shape=jax.ShapeDtypeStruct((8, 128), tiles.dtype),
        in_specs=[VMEM, ANY],
        out_specs=VMEM,
        compiler_params=params(),
        cost_estimate=pl.CostEstimate(flops=0, bytes_accessed=0, transcendentals=0),
    )(tiles, own)


def gathered_kernel(last, rows, cols, count, scalars, tiles, gathered, xpos, ymom, xout, yout, extra, xbuf, field, xsem):
    tile = xbuf.shape[1]
    used = count[0]

    def block_copy(s):
        return pltpu.make_async_copy(gathered.at[cols[s]], xbuf.at[s], xsem.at[s])

    @pl.loop(0, used)
    def _(s):
        block_copy(s).start()

    field[...] = jnp.zeros_like(field)

    @pl.loop(0, used)
    def _(s):
        block_copy(s).wait()
        here = pl.ds(pl.multiple_of(rows[s] * tile, tile), tile)
        field[here, :] += jnp.dot(tiles[s], xbuf[s], preferred_element_type=jnp.float32)

    x, h = xpos[...], field[...]
    if last:
        extra[...] = -0.5 * jnp.sum(x * h, axis=0, keepdims=True)
    x, y = update(scalars[0], scalars[1], h, x, ymom[...])
    xout[...] = x
    yout[...] = y
    if not last:
        extra[...] = x.astype(jnp.bfloat16)


def body_any(tiles, tile_rows, tile_cols, counts, positions, momenta):
    slots, tile, _ = tiles.shape
    order, repl = positions.shape
    devices = lax.axis_size("row")
    state = jax.ShapeDtypeStruct(positions.shape, jnp.float32)
    total = jnp.sum(lax.psum(squares(counts, tiles), "row"))
    coeff = 0.7 * jnp.sqrt((order * devices - 1) / total)
    xpos, ymom, extra = positions, momenta, positions.astype(jnp.bfloat16)
    for step in range(STEPS):
        last = step == STEPS - 1
        gathered = lax.all_gather(extra, "row", tiled=True).reshape(-1, tile, repl)
        scalars = jnp.stack([jnp.float32(0.4 - 0.1 * step), coeff])
        xpos, ymom, extra = pl.pallas_call(
            functools.partial(gathered_kernel, last),
            out_shape=(
                state,
                state,
                jax.ShapeDtypeStruct((1, repl), jnp.float32) if last else jax.ShapeDtypeStruct(state.shape, jnp.bfloat16),
            ),
            in_specs=[SMEM] * 4 + [VMEM, ANY, VMEM, VMEM],
            out_specs=(VMEM,) * 3,
            scratch_shapes=[
                pltpu.VMEM((slots, tile, repl), jnp.bfloat16),
                pltpu.VMEM(positions.shape, jnp.float32),
                pltpu.SemaphoreType.DMA((slots,)),
            ],
            compiler_params=params(),
        )(tile_rows, tile_cols, counts, scalars, tiles, gathered, xpos, ymom)
    return (xpos, ymom, lax.psum(extra, "row").reshape(repl))


def solution(mesh):
    in_specs = (
        P(("groups", "row"), None, None),
        P(("groups", "row")),
        P(("groups", "row")),
        P(("groups", "row")),
        P(("groups", "row"), None),
        P(("groups", "row"), None),
    )
    out_specs = (P(("groups", "row"), None), P(("groups", "row"), None), P("groups"))

    def body(tiles, *args):
        slots = tiles.shape[0]
        by_hand = mesh.shape["row"] == 16 and slots % GROUP == 0 and slots <= 96
        return (body_16 if by_hand else body_any)(tiles, *args)

    return jax.shard_map(body, mesh=mesh, in_specs=in_specs, out_specs=out_specs, check_vma=False)
```

```python
import functools

import jax
import jax.numpy as jnp
from jax import lax
from jax.experimental import pallas as pl
from jax.experimental.pallas import tpu as pltpu
from jax.sharding import PartitionSpec as P

STEPS = 4
GROUP = 6
LANES = 128
SUM_AT = LANES - 1
LIMIT = 16 * 2**20

SMEM = pl.BlockSpec(memory_space=pltpu.SMEM)
VMEM = pl.BlockSpec(memory_space=pltpu.VMEM)
ANY = pl.BlockSpec(memory_space=pl.ANY)


def params(limit=LIMIT):
    return pltpu.CompilerParams(vmem_limit_bytes=limit)


def squares_kernel(count, tiles, out):
    tile = tiles.shape[1]

    def add(s, acc):
        t = tiles[s].astype(jnp.float32)
        return acc + jnp.sum((t * t).reshape(tile // 8, 8, tile), axis=0)

    acc = lax.fori_loop(0, count[0], add, jnp.zeros((8, tile), jnp.float32))
    acc = jnp.sum(acc, axis=0, keepdims=True)
    out[...] = sum(acc[:, i : i + 128] for i in range(0, tile, 128))


def squares(count, tiles):
    return pl.pallas_call(
        squares_kernel,
        out_shape=jax.ShapeDtypeStruct((1, 128), jnp.float32),
        in_specs=[SMEM, VMEM],
        out_specs=VMEM,
        compiler_params=params(),
        cost_estimate=pl.CostEstimate(flops=2 * tiles.size, bytes_accessed=2 * tiles.size, transcendentals=0),
    )(count, tiles)


def update(pump, coeff, h, x, y):
    y = y + 0.5 * (-(x * x + pump) * x + coeff * h)
    return x + 0.5 * y, y


FIRST = ((0, 2), (3, 1), (1, 0), (2, 3))
SECOND = ((0, 1), (3, 2), (1, 3), (2, 0))
OUTWARD = ((1, 0), (2, 3))
MIDDLE = ((1, 2), (2, 1))


class Layout:
    def __init__(self, cap):
        self.cap = cap
        self.packs = 0
        self.entries = 12 * cap
        self.size = 12 * cap + 3 * 16 * cap

    def pack(self, j, flip):
        return self.packs + (j * 3 + flip - 1) * self.cap

    def entry(self, i):
        return self.entries + 3 * i


def whereabouts():
    me = lax.axis_index("row")
    z, yc = lax.div(me, 4), lax.rem(me, 4)
    inner = (z == 1) | (z == 2)
    near, skip = z ^ 1, z ^ 2
    return z, yc, inner, (z, jnp.where(inner, skip, near), jnp.where(inner, near, skip), z ^ 3)


EARLY = tuple((j, flip) for j in range(3) for flip in range(4)) + ((3, 0), (3, 1))
LATE = ((3, 2), (3, 3))


def plan_kernel(layout, blocks, rows, cols, count, tiles, mine, note, seen, buffer, sems):
    cap = layout.cap
    keys = 16 * cap
    slots, tile, _ = buffer.shape
    chunks = [pl.ds(first, GROUP) for first in range(0, slots, GROUP)]
    copies = [pltpu.make_async_copy(tiles.at[c], buffer.at[c], sems.at[i]) for i, c in enumerate(chunks)]
    for copy in copies:
        copy.start()

    @pl.loop(0, 16)
    def _(d):
        seen[d] = 0

    @pl.loop(0, keys)
    def _(k):
        mine[k] = 0
        mine[keys + k] = blocks
        mine[2 * keys + k] = 0

    @pl.loop(0, count[0])
    def _(s):
        source = lax.div(cols[s], blocks)
        rank = seen[source]
        seen[source] = rank + 1
        key = source * cap + jnp.minimum(rank, cap - 1)
        mine[key] = s
        mine[keys + key] = rows[s]
        mine[2 * keys + key] = lax.rem(cols[s], blocks)

    lane = lax.broadcasted_iota(jnp.int32, note.shape, 1)
    wants = jnp.zeros(note.shape, jnp.int32)
    for k in range(keys):
        wants = jnp.where(lane == k, mine[2 * keys + k], wants)

    def add(s, acc):
        t = buffer[s].astype(jnp.float32)
        return acc + jnp.sum((t * t).reshape(tile // 8, 8, tile), axis=0)

    acc = jnp.zeros((8, tile), jnp.float32)
    for i, copy in enumerate(copies):
        copy.wait()
        acc = lax.fori_loop(i * GROUP, jnp.clip(count[0], i * GROUP, (i + 1) * GROUP), add, acc)
    note[...] = jnp.where(lane == SUM_AT, jnp.sum(acc), wants.astype(jnp.float32))


def plan(layout, blocks, rows, cols, count, tiles):
    return pl.pallas_call(
        functools.partial(plan_kernel, layout, blocks),
        out_shape=(
            jax.ShapeDtypeStruct((3 * 16 * layout.cap,), jnp.int32),
            jax.ShapeDtypeStruct((1, LANES), jnp.float32),
        ),
        in_specs=[SMEM] * 3 + [ANY],
        out_specs=(SMEM, VMEM),
        scratch_shapes=[
            pltpu.SMEM((16,), jnp.int32),
            pltpu.VMEM(tiles.shape, tiles.dtype),
            pltpu.SemaphoreType.DMA((tiles.shape[0] // GROUP,)),
        ],
        compiler_params=params(59 * 2**20),
        cost_estimate=pl.CostEstimate(flops=0, bytes_accessed=0, transcendentals=0),
    )(rows, cols, count, tiles)


def fill_table(layout, mine, notes, table):
    cap = layout.cap
    keys = 16 * cap
    _, yc, _, zs = whereabouts()
    for j in range(4):
        for flip, asked in enumerate(notes, 1):
            for r in range(cap):
                table[layout.pack(j, flip) + r] = asked[0, (zs[j] * 4 + yc) * cap + r].astype(jnp.int32)
    for i, (j, flip) in enumerate(EARLY + LATE):
        for r in range(cap):
            key = (zs[j] * 4 + (yc ^ flip)) * cap + r
            at = layout.entry(i * cap + r)
            table[at] = mine[key]
            table[at + 1] = mine[keys + key]
            table[at + 2] = mine[2 * keys + key]


def start_kernel(layout, mine, note1, note2, note3, own, first, table, out2, out3):
    fill_table(layout, mine, (note1, note2, note3), table)
    other_y_kernel(layout, (0, 1), table, own, first, out2, out3)


def start(layout, mine, notes, own, first):
    _, tile, repl = own.shape
    packs = jax.ShapeDtypeStruct((2 * layout.cap, tile, repl), jnp.bfloat16)
    return pl.pallas_call(
        functools.partial(start_kernel, layout),
        out_shape=(jax.ShapeDtypeStruct((layout.size,), jnp.int32), packs, packs),
        in_specs=[SMEM] * 4 + [VMEM] * 2,
        out_specs=(SMEM, VMEM, VMEM),
        compiler_params=params(),
        cost_estimate=pl.CostEstimate(flops=0, bytes_accessed=0, transcendentals=0),
    )(mine, *notes, own, first)


def copy_asked(layout, table, j, flip, shard, out, first=0):
    at = layout.pack(j, flip)
    for r in range(layout.cap):
        out[first + r] = shard[table[at + r]]


def copy_part(cap, source, part, out, first):
    for r in range(cap):
        out[first + r] = source[part * cap + r]


def by_place(mid, out, use):
    inner = whereabouts()[2]
    pl.when(inner)(lambda: use(mid))
    pl.when(jnp.logical_not(inner))(lambda: use(out))


def other_y_kernel(layout, js, table, *refs):
    shards, outs = refs[:-2], refs[-2:]
    for i, (j, shard) in enumerate(zip(js, shards)):
        for flip in (2, 3):
            copy_asked(layout, table, j, flip, shard, outs[flip - 2], i * layout.cap)


def second_kernel(layout, js, table, *refs):
    shards, (out2, out3, core) = refs[:-3], refs[-3:]
    other_y_kernel(layout, (2,), table, shards[-1], out2, out3)
    for i, (j, shard) in enumerate(zip(js, shards)):
        copy_asked(layout, table, j, 1, shard, core, i * layout.cap)


def third_kernel(layout, table, mid, out, out2, out3, core):
    def use(shard):
        other_y_kernel(layout, (3,), table, shard, out2, out3)
        copy_asked(layout, table, 3, 1, shard, core)

    by_place(mid, out, use)


def pack(kernel, sizes, table, arrays, after=()):
    _, tile, repl = arrays[0].shape
    first_out = 1 + len(arrays) + len(after)

    def picked(*refs):
        kernel(*refs[: 1 + len(arrays)], *refs[first_out:])

    return pl.pallas_call(
        picked,
        out_shape=[jax.ShapeDtypeStruct((size, tile, repl), jnp.bfloat16) for size in sizes],
        in_specs=[SMEM] + [VMEM] * len(arrays) + [ANY] * len(after),
        out_specs=[VMEM] * len(sizes),
        compiler_params=params(),
        cost_estimate=pl.CostEstimate(flops=0, bytes_accessed=0, transcendentals=0),
    )(table, *arrays, *after)


def multiply(layout, table, tiles, blocks, first, field):
    prods = [
        jnp.dot(tiles[table[layout.entry(first + i)]], block, preferred_element_type=jnp.float32)
        for i, block in enumerate(blocks)
    ]
    for i, prod in enumerate(prods):
        field[table[layout.entry(first + i) + 1]] += prod


def take_own(layout, table, entry, shard, xbuf, place):
    for r in range(layout.cap):
        xbuf[place + r] = shard[table[layout.entry(entry + r) + 2]]


def early_kernel(layout, parts, table, tiles, own, first, second, mid, out, core, core3, *refs):
    cap = layout.cap
    field, xbuf = refs[-2:]
    for j, shard in enumerate((own, first, second)):
        base = 4 * cap * j
        take_own(layout, table, base, shard, xbuf, base)
        if core.shape[0] == 3 * cap:
            copy_part(cap, core, j, xbuf, base + cap)
        elif j == 0:
            copy_part(cap, refs[-3], 0, xbuf, base + cap)
        else:
            copy_part(cap, core, j - 1, xbuf, base + cap)
        ref, part = parts[j]
        copy_part(cap, refs[ref], part, xbuf, base + 2 * cap)
        copy_part(cap, refs[ref + 1], part, xbuf, base + 3 * cap)
    by_place(mid, out, lambda shard: take_own(layout, table, 12 * cap, shard, xbuf, 12 * cap))
    copy_part(cap, core3, 0, xbuf, 13 * cap)
    field[...] = jnp.zeros_like(field)

    @pl.loop(0, len(EARLY) * cap // GROUP)
    def _(g):
        multiply(layout, table, tiles, [xbuf[g * GROUP + i] for i in range(GROUP)], g * GROUP, field)


def early(layout, parts, table, tiles, arrays):
    tile = tiles.shape[1]
    blocks, _, repl = arrays[0].shape
    return pl.pallas_call(
        functools.partial(early_kernel, layout, parts),
        out_shape=jax.ShapeDtypeStruct((blocks + 1, tile, repl), jnp.float32),
        in_specs=[SMEM] + [VMEM] * (1 + len(arrays)),
        out_specs=VMEM,
        scratch_shapes=[pltpu.VMEM((len(EARLY) * layout.cap, tile, repl), jnp.bfloat16)],
        compiler_params=params(),
        cost_estimate=pl.CostEstimate(flops=0, bytes_accessed=0, transcendentals=0),
    )(table, tiles, *arrays)


def late_field(layout, table, tiles, got2, got3, field, acc):
    cap = layout.cap
    acc[...] = field[...]
    multiply(layout, table, tiles, [ref[r] for ref in (got2, got3) for r in range(cap)], len(EARLY) * cap, acc)


def late_kernel(layout, table, scalars, tiles, got2, got3, field, xpos, ymom, xout, yout, xb, out2, out3, core, acc):
    late_field(layout, table, tiles, got2, got3, field, acc)
    for b in range(xpos.shape[0]):
        x, y = update(scalars[0], scalars[1], acc[b], xpos[b], ymom[b])
        xout[b] = x
        yout[b] = y
        xb[b] = x.astype(jnp.bfloat16)
    other_y_kernel(layout, (0,), table, xb, out2, out3)
    copy_asked(layout, table, 0, 1, xb, core)


def late(layout, table, scalars, tiles, sources, field, xpos, ymom):
    tile = tiles.shape[1]
    blocks, _, repl = xpos.shape
    entries = len(LATE) * layout.cap
    state = jax.ShapeDtypeStruct(xpos.shape, jnp.float32)
    out = jax.ShapeDtypeStruct((layout.cap, tile, repl), jnp.bfloat16)
    return pl.pallas_call(
        functools.partial(late_kernel, layout),
        out_shape=(state, state, jax.ShapeDtypeStruct(xpos.shape, jnp.bfloat16), out, out, out),
        in_specs=[SMEM, SMEM] + [VMEM] * (1 + len(sources) + 3),
        out_specs=(VMEM,) * 6,
        scratch_shapes=[pltpu.VMEM((blocks + 1, tile, repl), jnp.float32)],
        compiler_params=params(),
        cost_estimate=pl.CostEstimate(
            flops=2 * entries * tile * tile * repl,
            bytes_accessed=entries * tile * (tile + repl) * 2 + 20 * xpos.size,
            transcendentals=0,
        ),
    )(table, scalars, tiles, *sources, field, xpos, ymom)


def energy_kernel(layout, table, tiles, got2, got3, field, xpos, energy, acc):
    late_field(layout, table, tiles, got2, got3, field, acc)
    total = jnp.zeros(xpos.shape[1:], jnp.float32)
    for b in range(xpos.shape[0]):
        total += xpos[b] * acc[b]
    part = -0.5 * jnp.sum(total, axis=0, keepdims=True)
    for i in range(energy.shape[0]):
        energy[i] = part


def last_field(layout, table, tiles, sources, field, xpos):
    return pl.pallas_call(
        functools.partial(energy_kernel, layout),
        out_shape=(
            jax.ShapeDtypeStruct((16, 1, xpos.shape[2]), jnp.float32),
            jax.ShapeDtypeStruct(field.shape, jnp.float32),
        ),
        in_specs=[SMEM] + [VMEM] * (1 + len(sources) + 2),
        out_specs=(VMEM, VMEM),
        compiler_params=params(),
        cost_estimate=pl.CostEstimate(flops=0, bytes_accessed=0, transcendentals=0),
    )(table, tiles, *sources, field, xpos)


def update_kernel(scalars, field, xpos, ymom, xout, yout, xnew, ynew, sems):
    copies = []
    for b in range(xpos.shape[0]):
        x, y = update(scalars[0], scalars[1], field[b], xpos[b], ymom[b])
        xnew[b] = x
        ynew[b] = y
        for i, (new, out) in enumerate(((xnew, xout), (ynew, yout))):
            copies.append(pltpu.make_async_copy(new.at[b], out.at[b], sems.at[i, b]))
            copies[-1].start()
    for copy in copies:
        copy.wait()


def last_update(scalars, field, xpos, ymom):
    state = jax.ShapeDtypeStruct(xpos.shape, jnp.float32)
    return pl.pallas_call(
        update_kernel,
        out_shape=(state, state),
        in_specs=[SMEM] + [VMEM] * 3,
        out_specs=(ANY, ANY),
        scratch_shapes=[pltpu.VMEM(xpos.shape, jnp.float32)] * 2 + [pltpu.SemaphoreType.DMA((2, xpos.shape[0]))],
        compiler_params=params(),
        cost_estimate=pl.CostEstimate(flops=10 * xpos.size, bytes_accessed=20 * xpos.size, transcendentals=0),
    )(scalars, field, xpos, ymom)


def along_z(pairs, value):
    return lax.ppermute(value, "row", [(a * 4 + i, b * 4 + i) for a, b in pairs for i in range(4)])


def across(flip, value):
    return lax.ppermute(value, "row", [(i, i ^ flip) for i in range(16)])


def row_sum(parts):
    return jnp.sum(lax.all_to_all(parts, "row", split_axis=0, concat_axis=0, tiled=True), axis=0)


def body_16(tiles, tile_rows, tile_cols, counts, positions, momenta):
    slots, tile, _ = tiles.shape
    repl = positions.shape[1]
    blocks = positions.shape[0] // tile
    cap = (slots + 15) // 16
    order = blocks * tile * 16
    layout = Layout(cap)

    def other_y(js, shards):
        kernel = functools.partial(other_y_kernel, layout, js)
        return pack(kernel, [len(js) * cap] * 2, table, shards)

    def to_other_y(packs):
        return [across(2, packs[0]), across(3, packs[1])]

    xpos = positions.reshape(blocks, tile, repl)
    ymom = momenta.reshape(blocks, tile, repl)
    own0 = xpos.astype(jnp.bfloat16)
    mine, note = plan(layout, blocks, tile_rows, tile_cols, counts, tiles)
    notes = [across(flip, note) for flip in (1, 2, 3)]
    packs0 = None
    for step in range(STEPS):
        last = step == STEPS - 1
        own1 = along_z(FIRST, own0)
        if step == 0:
            again, notes[0] = lax.optimization_barrier((own0, notes[0]))
            own2 = along_z(SECOND, again)
            again, notes = lax.optimization_barrier((again, notes))
            mid = along_z(MIDDLE, again)
            own1, notes = lax.optimization_barrier((own1, notes))
            out = along_z(OUTWARD, own1)
            table, *packs01 = start(layout, mine, notes, own0, own1)
            got1 = to_other_y(packs01)
            corner = touch(tiles, own2)
            own2, got1 = lax.optimization_barrier((own2, got1))
            parts, cores, after = ((0, 0), (0, 1), (2, 0)), [], [corner]
            got = got1
        else:
            core0 = across(1, packs0[2])
            again, core0 = lax.optimization_barrier((own0, core0))
            own2 = along_z(SECOND, again)
            got0 = to_other_y(packs0)
            again, own1, got0 = lax.optimization_barrier((again, own1, got0))
            packs1 = other_y((1,), [own1])
            out = along_z(OUTWARD, own1)
            got1 = to_other_y(packs1)
            mid = along_z(MIDDLE, again)
            own2, got1 = lax.optimization_barrier((own2, got1))
            parts, cores, after = ((0, 0), (2, 0), (4, 0)), [core0], []
            got = got0 + got1
        js, shards = ((0, 1, 2), [own0, own1, own2]) if step == 0 else ((1, 2), [own1, own2])
        packs2 = pack(functools.partial(second_kernel, layout, js), [cap, cap, len(js) * cap], table, shards, after)
        got2 = to_other_y(packs2)
        core = across(1, packs2[2])
        packs3 = pack(functools.partial(third_kernel, layout), [cap] * 3, table, [mid, out])
        if step == 0:
            note, packs3 = lax.optimization_barrier((note, packs3))
            plane = note + notes[0] + notes[1] + notes[2]
            half = plane + across(4, plane)
        core3 = across(1, packs3[2])
        got3 = to_other_y(packs3)
        if step == 0:
            got2, half = lax.optimization_barrier((got2, half))
            sums = across(8, half)
        field = early(layout, parts, table, tiles, [own0, own1, own2, mid, out, core, core3] + got + got2 + cores)
        if step == 0:
            field, sums = lax.optimization_barrier((field, sums))
            total = (half + sums)[0, SUM_AT]
            coeff = 0.7 * jnp.sqrt((order - 1) / total)
        scalars = jnp.stack([jnp.float32(0.4 - 0.1 * step), coeff])
        if last:
            part, field = last_field(layout, table, tiles, got3, field, xpos)
            energy = row_sum(part)
            xpos, ymom = last_update(scalars, field, xpos, ymom)
        else:
            xpos, ymom, own0, *packs0 = late(layout, table, scalars, tiles, got3, field, xpos, ymom)
    return (xpos.reshape(positions.shape), ymom.reshape(momenta.shape), energy.reshape(repl))


def touch_kernel(tiles, own, out):
    out[...] = tiles[0, :8, :128]


def touch(tiles, own):
    return pl.pallas_call(
        touch_kernel,
        out_shape=jax.ShapeDtypeStruct((8, 128), tiles.dtype),
        in_specs=[VMEM, ANY],
        out_specs=VMEM,
        compiler_params=params(),
        cost_estimate=pl.CostEstimate(flops=0, bytes_accessed=0, transcendentals=0),
    )(tiles, own)


def gathered_kernel(last, rows, cols, count, scalars, tiles, gathered, xpos, ymom, xout, yout, extra, xbuf, field, xsem):
    tile = xbuf.shape[1]
    used = count[0]

    def block_copy(s):
        return pltpu.make_async_copy(gathered.at[cols[s]], xbuf.at[s], xsem.at[s])

    @pl.loop(0, used)
    def _(s):
        block_copy(s).start()

    field[...] = jnp.zeros_like(field)

    @pl.loop(0, used)
    def _(s):
        block_copy(s).wait()
        here = pl.ds(pl.multiple_of(rows[s] * tile, tile), tile)
        field[here, :] += jnp.dot(tiles[s], xbuf[s], preferred_element_type=jnp.float32)

    x, h = xpos[...], field[...]
    if last:
        extra[...] = -0.5 * jnp.sum(x * h, axis=0, keepdims=True)
    x, y = update(scalars[0], scalars[1], h, x, ymom[...])
    xout[...] = x
    yout[...] = y
    if not last:
        extra[...] = x.astype(jnp.bfloat16)


def body_any(tiles, tile_rows, tile_cols, counts, positions, momenta):
    slots, tile, _ = tiles.shape
    order, repl = positions.shape
    devices = lax.axis_size("row")
    state = jax.ShapeDtypeStruct(positions.shape, jnp.float32)
    total = jnp.sum(lax.psum(squares(counts, tiles), "row"))
    coeff = 0.7 * jnp.sqrt((order * devices - 1) / total)
    xpos, ymom, extra = positions, momenta, positions.astype(jnp.bfloat16)
    for step in range(STEPS):
        last = step == STEPS - 1
        gathered = lax.all_gather(extra, "row", tiled=True).reshape(-1, tile, repl)
        scalars = jnp.stack([jnp.float32(0.4 - 0.1 * step), coeff])
        xpos, ymom, extra = pl.pallas_call(
            functools.partial(gathered_kernel, last),
            out_shape=(
                state,
                state,
                jax.ShapeDtypeStruct((1, repl), jnp.float32) if last else jax.ShapeDtypeStruct(state.shape, jnp.bfloat16),
            ),
            in_specs=[SMEM] * 4 + [VMEM, ANY, VMEM, VMEM],
            out_specs=(VMEM,) * 3,
            scratch_shapes=[
                pltpu.VMEM((slots, tile, repl), jnp.bfloat16),
                pltpu.VMEM(positions.shape, jnp.float32),
                pltpu.SemaphoreType.DMA((slots,)),
            ],
            compiler_params=params(),
        )(tile_rows, tile_cols, counts, scalars, tiles, gathered, xpos, ymom)
    return (xpos, ymom, lax.psum(extra, "row").reshape(repl))


def solution(mesh):
    in_specs = (
        P(("groups", "row"), None, None),
        P(("groups", "row")),
        P(("groups", "row")),
        P(("groups", "row")),
        P(("groups", "row"), None),
        P(("groups", "row"), None),
    )
    out_specs = (P(("groups", "row"), None), P(("groups", "row"), None), P("groups"))

    def body(tiles, *args):
        slots = tiles.shape[0]
        by_hand = mesh.shape["row"] == 16 and slots % GROUP == 0 and slots <= 96
        return (body_16 if by_hand else body_any)(tiles, *args)

    return jax.shard_map(body, mesh=mesh, in_specs=in_specs, out_specs=out_specs, check_vma=False)
```
